256 devices in a mesh: wa: 8 (over x, core), pb: 4 (over y), ka: 8 (over z).
Axes of the slice: x: 4, y: 4, z: 8, core: 2. Of those that a mesh axis runs over, the one named last changes fastest.
Arguments:
- slater: bfloat16 [6144, 9216], P(('wa', 'pb', 'ka')), may hold values from -6 to 6
- inverse: bfloat16 [6144, 2304], P(('wa', 'pb', 'ka')), may hold values from -1.75 to 1.75
- send_rows: int32 [2048, 3], P(('wa', 'pb', 'ka')), may hold values from 0 to 23
- take_rows: int32 [6144], P(('wa', 'pb', 'ka')), may hold values from 0 to 47, as said below
- pair_table: int32 [4, 16], replicated, may hold values from 0 to 15, each once within a row
- rotated_chol: bfloat16 [4, 9216, 512], P('pb', 'ka'), may hold values from -0.0625 to 0.0625
- chol_vectors: bfloat16 [4, 512, 36864], P('pb', None, 'ka'), may hold values from -0.125 to 0.125
- aux_noise: bfloat16 [6144, 2048], P('wa', 'pb'), may hold values from -6 to 6
Outputs:
- moved_walkers: bfloat16 [6144, 9216], P(('wa', 'pb', 'ka'))
- fields: bfloat16 [6144, 2048], P('wa', 'pb')
The draws below stay inside these ranges and needn't reach their ends.
Inputs may be any that keep to these rules, and one draw needn't show every extreme that they name: `pair_table`: each row of a momentum transfer is a permutation of the 16 k-points. `send_rows`: row b * 8 + d lists the local rows (0 to 23) of the walkers that the device of block b sends to the device with wa index d and the same pb and ka indices; only the first entries that the receiver takes are read. `take_rows`: A slot's value t below 24 names the device's own walker t; t = 24 + s * 3 + j names entry j of the list that the device with wa index s (same pb and ka indices) sends to this device. s is never the device's own wa index; from each source the entries used are its first ones, each used by one slot only, at most 3 of them; on every device some source fills all 3, and on some device every other source does.
All inputs are finite; a program needn't handle non-finite values.
Results may differ from the reference program's by a relative error of at most 0.015.
Values may be sent and summed in bfloat16 or wider, within the bound.
A program may use at most 128 MiB of HBM per device.

```python
import math
import jax
import jax.numpy as jnp
from jax import lax

NK = 16
NORB = 48
NOCC = 12
NCHOL = 512
WB = 24
PAIR = 3
NQ = 4
WGROUPS = 8
BLOCKS = 256
WALKERS = 6144


def draw_take_rows(key, part):
    blocks = WALKERS // WB
    groups = WGROUPS
    per_group = blocks // groups
    key_count, key_force, key_full, key_local, key_perm = jax.random.split(jax.random.fold_in(key, 7), 5)
    counts = jax.random.randint(key_count, (blocks, groups), 0, PAIR + 1)
    dest_group = jnp.arange(blocks) // per_group
    offset_group = jax.random.randint(key_force, (blocks,), 1, groups)
    forced = (dest_group + offset_group) % groups
    sources = jnp.arange(groups)
    counts = jnp.where(sources[None, :] == forced[:, None], PAIR, counts)
    full_block = jax.random.randint(key_full, (), 0, blocks - per_group)
    counts = jnp.where(jnp.arange(blocks)[:, None] == full_block, PAIR, counts)
    counts = jnp.where(sources[None, :] == dest_group[:, None], 0, counts)
    stop_at = jnp.cumsum(counts, axis=1)
    starts = stop_at - counts
    slot_ids = jnp.arange(WB)
    group_of = jnp.sum((stop_at[:, None, :] <= slot_ids[None, :, None]).astype(jnp.int32), axis=2)
    group_of = jnp.minimum(group_of, groups - 1)
    offset = slot_ids[None, :] - jnp.take_along_axis(starts, group_of, axis=1)
    remote = WB + group_of * PAIR + offset
    local_rows = jax.random.randint(key_local, (blocks, WB), 0, WB)
    values = jnp.where(slot_ids[None, :] < stop_at[:, -1:], remote, local_rows)
    block_keys = jax.random.split(key_perm, blocks)
    shuffles = jax.vmap(lambda one_key: jax.random.permutation(one_key, WB))(block_keys)
    return jnp.take_along_axis(values, shuffles, axis=1).reshape(-1).astype(jnp.int32)


def touch_ends(result, rng, smallest, high):
    place = [jax.random.randint(jax.random.fold_in(rng, axis), (), 0, length) for axis, length in enumerate(result.shape)]
    widest = result.shape.index(max(result.shape))
    next_to = place[:widest] + [(place[widest] + 1) % result.shape[widest]] + place[widest + 1:]
    return result.at[tuple(place)].set(smallest).at[tuple(next_to)].set(high)


def shard_levels(key, shape, cuts, least, top_value):
    def one(dim, parts):
        draws = jax.random.uniform(jax.random.fold_in(jax.random.fold_in(key, 6), dim), (parts,), jnp.float32, least / len(cuts), top_value / len(cuts))
        return jnp.repeat(jnp.exp(draws), shape[dim] // parts).reshape((-1,) + (1,) * (len(shape) - dim - 1))

    level = one(*cuts[0])
    for cut in cuts[1:]:
        level = level * one(*cut)
    return level


def noise(own_key, shape, scale, most, cuts=(), held_as=jnp.bfloat16):
    drawn = jax.random.normal(own_key, shape, jnp.float32) * scale
    if len(cuts) > 0:
        drawn = shard_levels(own_key, shape, cuts, -0.22, 0.18) * drawn
    return jnp.clip(drawn, min=-most, max=most).astype(held_as)


def setup_inputs(seed: int = 0) -> dict:
    streams_of = jax.random.split(jax.random.key(seed), 9)
    return {
        "slater": noise(streams_of[0], (WALKERS, NK * NORB * NOCC), 1.0, 6.0, ((0, 256),)),
        "inverse": noise(streams_of[1], (WALKERS, NK * NOCC * NOCC), NOCC ** -0.5, 1.75, ((0, 256),)),
        "send_rows": touch_ends(jax.random.randint(streams_of[2], (BLOCKS * WGROUPS, PAIR), 0, WB), jax.random.fold_in(streams_of[2], 1), 0, WB - 1).astype(jnp.int32),
        "take_rows": draw_take_rows(jax.random.fold_in(streams_of[8], 71), 0),
        "pair_table": jax.vmap(lambda own: jax.random.permutation(own, NK))(jax.random.split(streams_of[4], NQ)).reshape((NQ, NK)).astype(jnp.int32),
        "rotated_chol": noise(streams_of[5], (NQ, NK * NOCC * NORB, NCHOL), (NK * NOCC * NORB) ** -0.5, 0.0625, ((0, 4), (1, 8))),
        "chol_vectors": noise(streams_of[6], (NQ, NCHOL, NK * NORB * NORB), (NQ * NCHOL) ** -0.5, 0.125, ((0, 4), (2, 8))),
        "aux_noise": noise(streams_of[7], (WALKERS, NQ * NCHOL), 1.0, 6.0, ((0, 8), (1, 4))),
    }


tau_coef = 2.0
force_coef = 0.5

def propagate(potential, slater_mats):
    potential = lax.optimization_barrier(potential)
    matrix = potential.astype(jnp.float32)
    taylor_term = slater_mats.astype(jnp.float32)
    summed = taylor_term
    step_size = tau_coef / math.sqrt(NORB)
    for degree in range(1, 7):
        taylor_term = jnp.einsum('rkpq,rkqi->rkpi', matrix, taylor_term, precision=lax.Precision.HIGHEST) * (-step_size / degree)
        summed = summed + taylor_term
    return summed.astype(jnp.bfloat16)

def source_rows(send_rows, take_rows):
    groups = WGROUPS
    per_group = BLOCKS // groups
    walker_ids = jnp.arange(WALKERS, dtype=jnp.int32)
    block_index = walker_ids // WB
    dest_group = block_index // per_group
    column = block_index % per_group
    remote_slot = jnp.maximum(take_rows - WB, 0)
    source_group = jnp.minimum(remote_slot // PAIR, groups - 1)
    slot_index = remote_slot % PAIR
    source_block = source_group * per_group + column
    sent_rows = send_rows[source_block * groups + dest_group, slot_index]
    return jnp.where(take_rows < WB, block_index * WB + take_rows, source_block * WB + sent_rows).astype(jnp.int32)

def reference(slater, inverse, send_rows, take_rows, pair_table, rotated_chol, chol_vectors, aux_noise):
    sources = source_rows(send_rows, take_rows)
    walker_slater = jnp.take(slater, sources, axis=0)
    walker_inverse = jnp.take(inverse, sources, axis=0)
    inverse_mats = walker_inverse.reshape(WALKERS, NK, NOCC, NOCC).astype(jnp.float32)
    slater_mats = walker_slater.reshape(WALKERS, NK, NORB, NOCC).astype(jnp.float32)
    greens = jnp.einsum('wkij,wkrj->wkir', inverse_mats, slater_mats, precision=lax.Precision.HIGHEST)
    greens = greens.astype(jnp.bfloat16).reshape(WALKERS, NK, NOCC * NORB)
    force_parts = []
    for momentum in range(NQ):
        picked = jnp.take(greens, pair_table[momentum], axis=1).reshape(WALKERS, NK * NOCC * NORB)
        force_parts.append(jnp.dot(picked, rotated_chol[momentum], preferred_element_type=jnp.float32))
    force_bias = jnp.concatenate(force_parts, axis=1)
    fields = (aux_noise.astype(jnp.float32) - force_coef * force_bias).astype(jnp.bfloat16)

    def one_block(block_pair):
        block_fields, block_slater = block_pair
        summed = jnp.zeros((WB, NK * NORB * NORB), jnp.float32)
        for momentum in range(NQ):
            term_piece = jnp.dot(block_fields[:, momentum * NCHOL:(momentum + 1) * NCHOL], chol_vectors[momentum], preferred_element_type=jnp.float32).astype(jnp.bfloat16)
            term_piece = lax.optimization_barrier(term_piece)
            summed = summed + term_piece.astype(jnp.float32)
        potential = summed.astype(jnp.bfloat16).reshape(WB, NK, NORB, NORB)
        return propagate(potential, block_slater.reshape(WB, NK, NORB, NOCC)).reshape(WB, NK * NORB * NOCC)
    propagated = lax.map(one_block, (fields.reshape(BLOCKS, WB, NQ * NCHOL), walker_slater.reshape(BLOCKS, WB, NK * NORB * NOCC)))
    return (propagated.reshape(WALKERS, NK * NORB * NOCC), fields)
```

```python
import functools
import math

import jax
import jax.numpy as jnp
import numpy as np
from jax import lax
from jax.experimental import pallas as pl
from jax.experimental.pallas import tpu as pltpu
from jax.sharding import PartitionSpec as P

MESH = pl.DeviceIdType.MESH
BF = jnp.bfloat16
F32 = jnp.float32
PAIR = 3
ROWS = 16
tau_coef = 2.0
force_coef = 0.5


class Sizes:
    def __init__(self, wa, ka, nk, norb, nocc, nchol, wb):
        self.wa, self.pb, self.ka, self.nk = wa, 4, ka, nk
        self.norb, self.nocc, self.nchol, self.wb = norb, nocc, nchol, wb
        self.blk = norb * nocc
        self.sq = nocc * nocc
        self.width = 4 * self.blk
        self.chunks = nk // 4
        self.half = ka // 2
        self.quarter = 2 * self.blk // 4


def dot(a, b):
    return jnp.dot(a, b, preferred_element_type=F32)


def flip(i):
    return i + 1 - 2 * (i % 2)


def remote(src, dst, send, recv, **place):
    return pltpu.make_async_remote_copy(
        src_ref=src, dst_ref=dst, send_sem=send, recv_sem=recv, device_id=place, device_id_type=MESH
    )


def ring_events(half):
    events = [(s, d) for s in range(1, half) for d in (0, 1)]
    return events + [(half, 0)]


class Ring:
    def __init__(self, size, me, core):
        self.n, self.half, self.me, self.core = size, size // 2, me, core
        self.events = ring_events(self.half)

    def index(self, event):
        return self.events.index(event)

    def block(self, event):
        s, d = event
        if s == self.half:
            return (self.me + self.half) % self.n
        return (self.me + (self.n - s if d == 0 else s)) % self.n

    def sent_block(self, event):
        s, d = event
        if s == self.half:
            back = self.half - 1
            return (self.me + self.n - back + 2 * back * self.core) % self.n
        return (self.me + (self.n - s + 1 if d == 0 else s - 1)) % self.n

    def target(self, event):
        s, d = event
        if s == self.half:
            return (self.me + 1 + (self.n - 2) * self.core) % self.n
        return (self.me + (1 if d == 0 else self.n - 1)) % self.n

    def of_step(self, s):
        return [e for e in self.events if e[0] == s]


def first_kernel(
    z, pair_ref, slater_ref, inverse_ref, ssend_ref, sown_ref, srem_ref, perm_ref, expand_ref, tile_ref,
    rc_ref, chol_ref, aux_ref,
    fq_ref, fields_ref, ts_ref, cholk_ref,
    sendbuf, recv, sk, ik, sps, gst, gall, rcf, acc, auxb, fbuf, fqs, relay,
    lsem, a_s, a_r, t_s, t_r, g_s, g_r, ring_s, ring_r, sib_s, sib_r, x_s, x_r, xs_s, xs_r,
    n_s, n_r, p_s, p_r, q_s, q_r, c_s, c_r, fy_s, fy_r, fz_s, fz_r,
):
    wa, pb, ka = lax.axis_index("wa"), lax.axis_index("pb"), lax.axis_index("ka")
    core, x = wa % 2, wa // 2
    xs = z.wa // 2
    sibling = flip(wa)
    x_to = ((x + 1 + (xs - 2) * core) % xs) * 2 + core
    base = pb - pb % 2
    par = pb % 2
    near = flip(pb)
    ring = Ring(z.ka, ka, core)
    wb, blk, norb, nocc, sq = z.wb, z.blk, z.norb, z.nocc, z.sq

    def y_of(e):
        return pb if e == 0 else near

    barrier = pltpu.get_barrier_semaphore()
    greeted = 0
    for d in range(1, z.wa):
        pl.semaphore_signal(barrier, inc=1, device_id={"wa": (wa + d) % z.wa}, device_id_type=MESH)
        greeted += 1
    for d in range(1, z.pb):
        pl.semaphore_signal(barrier, inc=1, device_id={"pb": (pb + d) % z.pb}, device_id_type=MESH)
        greeted += 1
    for d in range(1, z.ka):
        for e in (0, 1):
            pl.semaphore_signal(
                barrier, inc=1, device_id={"pb": y_of(e), "ka": (ka + d) % z.ka}, device_id_type=MESH
            )
            greeted += 1

    def source_chunk(c):
        if c < z.chunks:
            return slater_ref[:, c * z.width : (c + 1) * z.width]
        return inverse_ref[...]

    out = dot(ssend_ref[0], source_chunk(0))
    for c in range(1, z.chunks + 1):
        out = out + dot(ssend_ref[c], source_chunk(c))
    sendbuf[...] = out.astype(BF).reshape(z.wa, ROWS, z.width)
    recv[wa] = jnp.zeros((ROWS, z.width), BF)

    local = []
    for b in range(2):
        local.append(pltpu.make_async_copy(rc_ref.at[0, pl.ds(b * blk, blk)], rcf.at[2 * ka + b], lsem.at[b]))
    local.append(pltpu.make_async_copy(aux_ref.at[:, ka], auxb, lsem.at[2]))
    kcols = norb * norb
    own_cols = pl.ds(pl.multiple_of(par * kcols, kcols), kcols)
    other_cols = pl.ds(pl.multiple_of((1 - par) * kcols, kcols), kcols)
    local.append(
        pltpu.make_async_copy(
            chol_ref.at[0, :, own_cols], cholk_ref.at[pl.ds(pb * z.nchol, z.nchol)], lsem.at[3]
        )
    )
    for copy in local:
        copy.start()

    pl.semaphore_wait(barrier, greeted)

    a_copies = []
    for d in range(1, z.wa):
        to = (wa + d) % z.wa
        a_copies.append(remote(sendbuf.at[to], recv.at[wa], a_s.at[d], a_r.at[d], wa=to))
    for copy in a_copies:
        copy.start()

    quarter = wa % 4
    sib_quarter = flip(quarter)
    x_quarter = (quarter + 2) % 4
    sent = []

    def rcf_part(block, u):
        return rcf.at[2 * block + u // 2, pl.ds((u % 2) * z.quarter, z.quarter)]

    def ring_copy(e, arriving):
        i = ring.index(e)
        if arriving:
            here = rcf_part(ring.block(e), quarter)
            return remote(here, here, ring_s.at[i], ring_r.at[i], ka=ring.target(e))
        block = ring.sent_block(e)
        if e[0] == 1:
            src = rc_ref.at[0, pl.ds(quarter * z.quarter, z.quarter)]
        else:
            src = rcf_part(block, quarter)
        return remote(src, rcf_part(block, quarter), ring_s.at[i], ring_r.at[i], ka=ring.target(e))

    def part_copy(block, u, send, recv_sem, to):
        part = rcf_part(block, u)
        return remote(part, part, send, recv_sem, wa=to)

    def start(copy):
        copy.start()
        sent.append(copy)

    def serve_ring(s):
        for e in ring.of_step(s):
            ring_copy(e, True).wait_recv()
        if s < z.half:
            for e in ring.of_step(s + 1):
                start(ring_copy(e, False))
        for e in ring.of_step(s):
            i, block = ring.index(e), ring.block(e)
            start(part_copy(block, quarter, x_s.at[i], x_r.at[i], x_to))
            start(part_copy(block, quarter, sib_s.at[i], sib_r.at[i], sibling))

    def serve_x(s):
        for e in ring.of_step(s):
            i, block = ring.index(e), ring.block(e)
            part_copy(block, x_quarter, x_s.at[i], x_r.at[i], x_to).wait_recv()
            start(part_copy(block, x_quarter, xs_s.at[i], xs_r.at[i], sibling))

    for e in ring.of_step(1):
        start(ring_copy(e, False))

    hrows, qrows = z.nchol // 2, z.nchol // 4
    right, left = (pb + 1) % z.pb, (pb + 3) % z.pb
    across = (pb + 2) % z.pb
    my_rows = core * hrows

    def chol_rows(q, first, count):
        return cholk_ref.at[pl.ds(q * z.nchol + first, count)]

    near_copies = [
        remote(
            chol_ref.at[0, pl.ds(my_rows, hrows), other_cols],
            chol_rows(pb, my_rows, hrows), n_s.at[i], n_r.at[i], pb=to,
        )
        for i, to in enumerate((right, left))
    ]
    for copy in near_copies:
        start(copy)

    def relay_first():
        for i, to in enumerate((right, left)):
            start(
                remote(
                    chol_ref.at[0, pl.ds(my_rows + i * qrows, qrows), own_cols],
                    relay.at[i], p_s.at[i], p_r.at[i], pb=to,
                )
            )

    def relay_second():
        for i, (q, to) in enumerate(((left, right), (right, left))):
            remote(relay.at[i], relay.at[i], p_s.at[i], p_r.at[i], pb=to).wait_recv()
            start(
                remote(relay.at[i], chol_rows(q, my_rows + i * qrows, qrows), q_s.at[i], q_r.at[i], pb=to)
            )

    def chol_to_sibling(q, first, count, i):
        rows = chol_rows(q, first, count)
        return remote(rows, rows, c_s.at[i], c_r.at[i], wa=sibling)

    def near_to_sibling():
        for i, q in enumerate((left, right)):
            rows = chol_rows(q, my_rows, hrows)
            remote(rows, rows, n_s.at[i], n_r.at[i], pb=right).wait_recv()
            start(chol_to_sibling(q, my_rows, hrows, i))

    def across_to_sibling():
        for i in range(2):
            rows = chol_rows(across, my_rows + i * qrows, qrows)
            remote(rows, rows, q_s.at[i], q_r.at[i], pb=right).wait_recv()
            start(chol_to_sibling(across, my_rows + i * qrows, qrows, 2 + i))

    for d in range(1, z.wa):
        here = recv.at[(wa + z.wa - d) % z.wa]
        remote(here, here, a_s.at[d], a_r.at[d], wa=(wa + d) % z.wa).wait_recv()
    got = recv[...].reshape(z.wa * ROWS, z.width)
    for c in range(z.chunks + 1):
        picked = dot(sown_ref[...], source_chunk(c)) + dot(srem_ref[c], got)
        if c < z.chunks:
            for k in range(4):
                sk[pl.ds((4 * c + k) * wb, wb), :] = picked[:, k * blk : (k + 1) * blk]
        else:
            for k in range(z.nk):
                ik[pl.ds(k * wb, wb), :] = picked[:, k * sq : (k + 1) * sq]

    serve_ring(1)

    g_copies = []
    rows = 4 * wb
    for c in range(z.chunks):
        part = pl.ds(c * rows, rows)
        ordered = dot(sk[part, :].astype(BF), perm_ref[...])
        for k in range(4):
            sps[4 * c + k] = ordered[k * wb : (k + 1) * wb, :].astype(BF)
        ordered = ordered.astype(BF)
        inv = ik[part, :].astype(BF)
        total = None
        for j in range(nocc):
            term = dot(inv, expand_ref[j]) * dot(ordered[:, j * norb : (j + 1) * norb], tile_ref[...])
            total = term if total is None else total + term
        gst[...] = total
        for k in range(4):
            gall[pb, 4 * c + k] = gst[k * wb : (k + 1) * wb, :].astype(BF)
        for d in range(1, z.pb):
            i = c * z.pb + d
            piece = gall.at[pb, pl.ds(4 * c, 4)]
            start(remote(piece, piece, g_s.at[i], g_r.at[i], pb=(pb + d) % z.pb))
        if c == 0 and z.half > 1:
            serve_ring(2)
            serve_x(1)
        if c == 2 and z.half > 2:
            serve_ring(3)
            serve_x(2)

    for d in range(z.ka):
        for e in (0, 1):
            i = 2 * d + e
            to_z, to_y = (ka + d) % z.ka, y_of(e)
            src = sps.at[2 * to_z + to_y % 2]
            dst = ts_ref.at[ka, par]
            if d == 0 and e == 0:
                own_ts = pltpu.make_async_copy(src, dst, lsem.at[4])
                own_ts.start()
            else:
                start(remote(src, dst, t_s.at[i], t_r.at[i], pb=to_y, ka=to_z))
    relay_first()

    done_ring = 1 + (z.half > 1) + (z.half > 2 and z.chunks > 2)
    done_x = done_ring - 1
    for s in range(done_ring + 1, z.half + 1):
        serve_ring(s)
    for s in range(done_x + 1, z.half + 1):
        serve_x(s)
    near_to_sibling()
    for d in range(1, z.pb):
        for c in range(z.chunks):
            i = c * z.pb + d
            piece = gall.at[(pb + z.pb - d) % z.pb, pl.ds(4 * c, 4)]
            remote(piece, piece, g_s.at[i], g_r.at[i], pb=(pb + d) % z.pb).wait_recv()
    for e in ring.events:
        i, block = ring.index(e), ring.block(e)
        part_copy(block, sib_quarter, sib_s.at[i], sib_r.at[i], sibling).wait_recv()
        part_copy(block, (sib_quarter + 2) % 4, xs_s.at[i], xs_r.at[i], sibling).wait_recv()
    for copy in local[:3]:
        copy.wait()

    acc[...] = jnp.zeros_like(acc)

    def one_k(k, carry):
        other = pair_ref[pb, k]
        left_side = jnp.concatenate([gall[y, other].astype(F32) for y in range(z.pb)], axis=0)
        acc[...] += dot(left_side.astype(BF), rcf[k])
        return carry

    lax.fori_loop(0, z.nk, one_k, 0)
    for y in range(z.pb):
        bias = acc[pl.ds(y * wb, wb), :]
        fbuf[y] = (auxb[y].astype(F32) - force_coef * bias).astype(BF)

    for d in range(1, z.pb):
        to = (pb + d) % z.pb
        start(
            remote(fbuf.at[pl.ds(to - to % 2, 2)], fqs.at[pb, ka], fy_s.at[d], fy_r.at[d], pb=to)
        )
    own_f = pltpu.make_async_copy(fbuf.at[pl.ds(base, 2)], fqs.at[pb, ka], lsem.at[5])
    own_f.start()
    out_f = pltpu.make_async_copy(fbuf, fields_ref, lsem.at[6])
    out_f.start()
    relay_second()
    own_f.wait()
    for d in range(1, z.pb):
        here = fqs.at[(pb + z.pb - d) % z.pb, ka]
        remote(here, here, fy_s.at[d], fy_r.at[d], pb=right).wait_recv()

    def fq_copy(e, arriving):
        i = ring.index(e)
        block = ring.block(e) if arriving else ring.sent_block(e)
        here = fqs.at[:, block]
        return remote(here, here, fz_s.at[i], fz_r.at[i], ka=ring.target(e))

    for e in ring.of_step(1):
        start(fq_copy(e, False))
    for s in range(1, z.half + 1):
        for e in ring.of_step(s):
            fq_copy(e, True).wait_recv()
        if s < z.half:
            for e in ring.of_step(s + 1):
                start(fq_copy(e, False))
    out_q = pltpu.make_async_copy(fqs, fq_ref, lsem.at[7])
    out_q.start()
    across_to_sibling()

    for i, (q, first, count) in enumerate(
        ((left, 0, hrows), (right, 0, hrows), (across, 0, qrows), (across, qrows, qrows))
    ):
        chol_to_sibling(q, (1 - core) * hrows + first, count, i).wait_recv()
    for d in range(z.ka):
        for e in (0, 1):
            if d == 0 and e == 0:
                continue
            i = 2 * d + e
            from_y = y_of(e)
            here = ts_ref.at[(ka + z.ka - d) % z.ka, from_y % 2]
            remote(here, here, t_s.at[i], t_r.at[i], pb=near if e else pb, ka=(ka + d) % z.ka).wait_recv()
    own_ts.wait()
    local[3].wait()
    for copy in a_copies + sent:
        copy.wait_send()
    out_f.wait()
    out_q.wait()


def second_kernel(z, steps, fq_ref, ts_ref, chol_ref, perm_ref, back_ref, out_ref, vt, vs, term, total):
    b = pl.program_id(0)
    norb, nocc, blk = z.norb, z.nocc, z.blk
    tiles = vs.shape[0]
    lanes = vs.shape[3]
    ps = norb // steps
    v = dot(fq_ref[0], chol_ref[0 : z.nchol, :])
    for q in range(1, 4):
        v = v + dot(fq_ref[q], chol_ref[q * z.nchol : (q + 1) * z.nchol, :])
    for t in range(tiles):
        vt[t] = v[t * lanes : (t + 1) * lanes, :].T
        for p2 in range(norb):
            vs[t, p2, pl.ds(pl.multiple_of(b * ps, ps), ps), :] = vt[t, pl.ds(p2, ps, stride=norb), :]

    @pl.when(b == steps - 1)
    def _():
        start = ts_ref[...].astype(F32).T
        for t in range(tiles):
            first = start[:, t * lanes : (t + 1) * lanes].reshape(nocc, norb, lanes)
            term[0, t] = first
            total[t] = first
        step_size = tau_coef / math.sqrt(norb)
        group = 4

        def one_tile(t, carry):
            def one_degree(m, carry):
                scale = -step_size / m.astype(F32)
                now, later = (m + 1) % 2, m % 2

                def one_group(g, carry):
                    accs = [jnp.zeros((norb, lanes), F32) for _ in range(group)]
                    for p2 in range(norb):
                        column = vs[t, p2]
                        for a in range(group):
                            accs[a] = accs[a] + column * term[now, t, g * group + a, pl.ds(p2, 1), :]
                    for a in range(group):
                        new = accs[a] * scale
                        term[later, t, g * group + a] = new
                        total[t, g * group + a] += new
                    return carry

                return lax.fori_loop(0, nocc // group, one_group, carry)

            return lax.fori_loop(1, 7, one_degree, carry)

        lax.fori_loop(0, tiles, one_tile, 0)
        for t in range(tiles):
            final = total[t].reshape(blk, lanes).T.astype(BF)
            out_ref[pl.ds(t * lanes, lanes), :] = dot(final, back_ref[...]).astype(BF)


def third_kernel(z, moved_ref, out_ref, land, s_sem, r_sem, l_sem):
    pb, ka = lax.axis_index("pb"), lax.axis_index("ka")
    par = pb % 2
    near = flip(pb)
    barrier = pltpu.get_barrier_semaphore()
    peers = [(d, e) for d in range(z.ka) for e in (0, 1) if d + e > 0]
    for d, e in peers:
        pl.semaphore_signal(
            barrier, inc=1, device_id={"pb": near if e else pb, "ka": (ka + d) % z.ka}, device_id_type=MESH
        )
    k_own = 2 * ka + par
    own = pltpu.make_async_copy(moved_ref.at[ka, par], land.at[k_own], l_sem)
    own.start()
    pl.semaphore_wait(barrier, len(peers))
    copies = []
    for d, e in peers:
        to_y, to_z = (near if e else pb), (ka + d) % z.ka
        i = 2 * d + e
        copies.append(
            remote(moved_ref.at[to_z, to_y % 2], land.at[k_own], s_sem.at[i], r_sem.at[i], pb=to_y, ka=to_z)
        )
    for copy in copies:
        copy.start()
    for d, e in peers:
        i = 2 * d + e
        from_y, from_z = (near if e else pb), (ka + z.ka - d) % z.ka
        here = land.at[2 * from_z + from_y % 2]
        remote(here, here, s_sem.at[i], r_sem.at[i], pb=near if e else pb, ka=(ka + d) % z.ka).wait_recv()
    own.wait()
    for k in range(z.nk):
        out_ref[:, k * z.blk : (k + 1) * z.blk] = land[k]
    for copy in copies:
        copy.wait_send()


def constants(z):
    perm = np.zeros((z.blk, z.blk), np.float32)
    for r in range(z.norb):
        for j in range(z.nocc):
            perm[r * z.nocc + j, j * z.norb + r] = 1
    expand = np.zeros((z.nocc, z.sq, z.blk), np.float32)
    tiled = np.zeros((z.norb, z.blk), np.float32)
    for i in range(z.nocc):
        for r in range(z.norb):
            tiled[r, i * z.norb + r] = 1
            for j in range(z.nocc):
                expand[j, i * z.nocc + j, i * z.norb + r] = 1
    return jnp.asarray(perm, BF), jnp.asarray(perm.T, BF), jnp.asarray(expand, BF), jnp.asarray(tiled, BF)


def body(z, slater, inverse, send_rows, take_rows, pair_table, rotated_chol, chol_vectors, aux_noise):
    wb, nk, nc = z.wb, z.nk, z.chunks + 1
    perm, back, expand, tiled = constants(z)
    which = jnp.arange(nc, dtype=jnp.int32).reshape(nc, 1, 1, 1, 1)
    slot_chunk = jnp.arange(nc, dtype=jnp.int32).reshape(1, 1, 1, nc, 1)
    rows = jnp.arange(wb, dtype=jnp.int32).reshape(1, 1, 1, 1, wb)
    ssend = ((which == slot_chunk) & (send_rows.reshape(1, z.wa, PAIR, 1, 1) == rows)).astype(BF)
    ssend = ssend.reshape(nc, z.wa, PAIR * nc, wb)
    ssend = jnp.pad(ssend, ((0, 0), (0, 0), (0, ROWS - PAIR * nc), (0, 0))).reshape(nc, z.wa * ROWS, wb)
    sown = (take_rows[:, None] == jnp.arange(wb, dtype=jnp.int32)).astype(BF)
    lane = np.arange(z.wa * ROWS)
    src, within = lane // ROWS, lane % ROWS
    code = np.where(within < PAIR * nc, wb + PAIR * src + within // nc, -1).astype(np.int32)
    lane_chunk = (within % nc).astype(np.int32)
    srem = (
        (jnp.arange(nc, dtype=jnp.int32).reshape(nc, 1, 1) == lane_chunk)
        & (take_rows.reshape(1, wb, 1) == code)
    ).astype(BF)

    vmem = pl.BlockSpec(memory_space=pltpu.VMEM)
    smem = pl.BlockSpec(memory_space=pltpu.SMEM)
    hbm = pl.BlockSpec(memory_space=pl.ANY)
    dma = lambda n: pltpu.SemaphoreType.DMA((n,))
    events = z.ka - 1
    kcols = z.norb * z.norb
    fq, fields, ts, cholk = pl.pallas_call(
        functools.partial(first_kernel, z),
        out_shape=(
            jax.ShapeDtypeStruct((4, z.ka, 2, wb, z.nchol), BF),
            jax.ShapeDtypeStruct((4, wb, z.nchol), BF),
            jax.ShapeDtypeStruct((z.ka, 2, wb, z.blk), BF),
            jax.ShapeDtypeStruct((4 * z.nchol, kcols), BF),
        ),
        in_specs=[smem] + [vmem] * 8 + [hbm] * 3,
        out_specs=(hbm,) * 4,
        scratch_shapes=[
            pltpu.VMEM((z.wa, ROWS, z.width), BF),
            pltpu.VMEM((z.wa, ROWS, z.width), BF),
            pltpu.VMEM((nk * wb, z.blk), F32),
            pltpu.VMEM((nk * wb, z.sq), F32),
            pltpu.VMEM((nk, wb, z.blk), BF),
            pltpu.VMEM((4 * wb, z.blk), F32),
            pltpu.VMEM((4, nk, wb, z.blk), BF),
            pltpu.VMEM((nk, z.blk, z.nchol), BF),
            pltpu.VMEM((4 * wb, z.nchol), F32),
            pltpu.VMEM((4, wb, z.nchol), BF),
            pltpu.VMEM((4, wb, z.nchol), BF),
            pltpu.VMEM((4, z.ka, 2, wb, z.nchol), BF),
            pltpu.VMEM((2, z.nchol // 4, kcols), BF),
            dma(8), dma(z.wa), dma(z.wa), dma(2 * z.ka), dma(2 * z.ka),
            dma(4 * z.chunks), dma(4 * z.chunks),
            dma(events), dma(events), dma(events), dma(events), dma(events), dma(events), dma(events), dma(events),
            dma(2), dma(2), dma(2), dma(2), dma(2), dma(2), dma(4), dma(4),
            dma(4), dma(4), dma(events), dma(events),
        ],
        compiler_params=pltpu.CompilerParams(
            collective_id=0, has_side_effects=True, vmem_limit_bytes=50 * 1024 * 1024
        ),
        cost_estimate=pl.CostEstimate(flops=2 * 10**9, bytes_accessed=40 * 10**6, transcendentals=0),
    )(
        pair_table, slater, inverse, ssend, sown, srem, perm, expand, tiled,
        rotated_chol, chol_vectors, aux_noise.reshape(4, z.ka, wb, z.nchol),
    )

    walkers = 2 * z.ka * wb
    lanes = min(128, walkers)
    tiles = walkers // lanes
    steps = max(1, z.norb // 8)
    block = z.norb // steps * z.norb
    moved = pl.pallas_call(
        functools.partial(second_kernel, z, steps),
        grid=(steps,),
        out_shape=jax.ShapeDtypeStruct((walkers, z.blk), BF),
        in_specs=[
            pl.BlockSpec((4, walkers, z.nchol), lambda b: (0, 0, 0)),
            pl.BlockSpec((walkers, z.blk), lambda b: (0, 0)),
            pl.BlockSpec((4 * z.nchol, block), lambda b: (0, b)),
            pl.BlockSpec((z.blk, z.blk), lambda b: (0, 0)),
            pl.BlockSpec((z.blk, z.blk), lambda b: (0, 0)),
        ],
        out_specs=pl.BlockSpec((walkers, z.blk), lambda b: (0, 0)),
        scratch_shapes=[
            pltpu.VMEM((tiles, block, lanes), F32),
            pltpu.VMEM((tiles, z.norb, z.norb, lanes), F32),
            pltpu.VMEM((2, tiles, z.nocc, z.norb, lanes), F32),
            pltpu.VMEM((tiles, z.nocc, z.norb, lanes), F32),
        ],
        compiler_params=pltpu.CompilerParams(vmem_limit_bytes=50 * 1024 * 1024),
        cost_estimate=pl.CostEstimate(flops=4 * 10**9, bytes_accessed=14 * 10**6, transcendentals=0),
    )(fq.reshape(4, walkers, z.nchol), ts.reshape(walkers, z.blk), cholk, perm, back)

    all_fields = lax.all_gather(fields, "ka", axis=1)

    result = pl.pallas_call(
        functools.partial(third_kernel, z),
        out_shape=jax.ShapeDtypeStruct((wb, nk * z.blk), BF),
        in_specs=[hbm],
        out_specs=vmem,
        scratch_shapes=[
            pltpu.VMEM((nk, wb, z.blk), BF),
            dma(2 * z.ka), dma(2 * z.ka), pltpu.SemaphoreType.DMA,
        ],
        compiler_params=pltpu.CompilerParams(
            collective_id=1, has_side_effects=True, vmem_limit_bytes=32 * 1024 * 1024
        ),
    )(moved.reshape(z.ka, 2, wb, z.blk))
    return result, all_fields.reshape(4 * z.ka * wb, z.nchol)


def solution(mesh, z=Sizes(8, 8, 16, 48, 12, 512, 24)):
    placed = (
        P(("wa", "pb", "ka"), None),
        P(("wa", "pb", "ka"), None),
        P(("wa", "pb", "ka"), None),
        P(("wa", "pb", "ka")),
        P(),
        P("pb", "ka", None),
        P("pb", None, "ka"),
        P("wa", "pb"),
    )
    return jax.shard_map(
        functools.partial(body, z),
        mesh=mesh,
        in_specs=placed,
        out_specs=(P(("wa", "pb", "ka"), None), P("wa", "pb")),
        check_vma=False,
    )
```

```python
import functools
import math

import jax
import jax.numpy as jnp
import numpy as np
from jax import lax
from jax.experimental import pallas as pl
from jax.experimental.pallas import tpu as pltpu
from jax.sharding import PartitionSpec as P

MESH = pl.DeviceIdType.MESH
BF = jnp.bfloat16
F32 = jnp.float32
PAIR = 3
ROWS = 16
tau_coef = 2.0
force_coef = 0.5


class Sizes:
    def __init__(self, wa, ka, nk, norb, nocc, nchol, wb):
        self.wa, self.pb, self.ka, self.nk = wa, 4, ka, nk
        self.norb, self.nocc, self.nchol, self.wb = norb, nocc, nchol, wb
        self.blk = norb * nocc
        self.sq = nocc * nocc
        self.width = 4 * self.blk
        self.chunks = nk // 4
        self.half = ka // 2
        self.quarter = 2 * self.blk // 4


def dot(a, b):
    return jnp.dot(a, b, preferred_element_type=F32)


def flip(i):
    return i + 1 - 2 * (i % 2)


def remote(src, dst, send, recv, **place):
    return pltpu.make_async_remote_copy(
        src_ref=src, dst_ref=dst, send_sem=send, recv_sem=recv, device_id=place, device_id_type=MESH
    )


def ring_events(half):
    events = [(s, d) for s in range(1, half) for d in (0, 1)]
    return events + [(half, 0)]


class Ring:
    def __init__(self, size, me, core):
        self.n, self.half, self.me, self.core = size, size // 2, me, core
        self.events = ring_events(self.half)

    def index(self, event):
        return self.events.index(event)

    def block(self, event):
        s, d = event
        if s == self.half:
            return (self.me + self.half) % self.n
        return (self.me + (self.n - s if d == 0 else s)) % self.n

    def sent_block(self, event):
        s, d = event
        if s == self.half:
            back = self.half - 1
            return (self.me + self.n - back + 2 * back * self.core) % self.n
        return (self.me + (self.n - s + 1 if d == 0 else s - 1)) % self.n

    def target(self, event):
        s, d = event
        if s == self.half:
            return (self.me + 1 + (self.n - 2) * self.core) % self.n
        return (self.me + (1 if d == 0 else self.n - 1)) % self.n

    def of_step(self, s):
        return [e for e in self.events if e[0] == s]


def step_kernel(
    z, send_ref, take_ref, pair_ref, slater_hbm, inverse_hbm, perm_hbm, back_hbm, expand_hbm, tile_hbm,
    rc_ref, chol_ref, aux_ref,
    out_ref, fields_ref,
    slater, inverse, perm, back, expand, tiled, sendbuf, recv, sk, ik, sps, gall, rcf, acc, auxb, fbuf,
    fqs, fmat, fall, chols, relay, ts, stage, moved, land, vt, vs, term, total,
    lsem, a_s, a_r, t_s, t_r, g_s, g_r, ring_s, ring_r, sib_s, sib_r, x_s, x_r, xs_s, xs_r,
    n_s, n_r, p_s, p_r, q_s, q_r, cb_s, cb_r, cx_s, cx_r, cs_s, cs_r, fy_s, fy_r, fz_s, fz_r, fo_s, fo_r, m_s, m_r,
):
    wa, pb, ka = lax.axis_index("wa"), lax.axis_index("pb"), lax.axis_index("ka")
    core, x = wa % 2, wa // 2
    xs = z.wa // 2
    sibling = flip(wa)
    x_to = ((x + 1 + (xs - 2) * core) % xs) * 2 + core
    base = pb - pb % 2
    par = pb % 2
    near = flip(pb)
    right, left, across = (pb + 1) % z.pb, (pb + 3) % z.pb, (pb + 2) % z.pb
    ring = Ring(z.ka, ka, core)
    wb, blk, norb, nocc, sq, nchol = z.wb, z.blk, z.norb, z.nocc, z.sq, z.nchol
    nc = z.chunks + 1
    kcols = norb * norb

    def y_of(e):
        return pb if e == 0 else near

    barrier = pltpu.get_barrier_semaphore()
    greeted = 0
    for d in range(1, z.wa):
        pl.semaphore_signal(barrier, inc=1, device_id={"wa": (wa + d) % z.wa}, device_id_type=MESH)
        greeted += 1
    for d in range(1, z.pb):
        pl.semaphore_signal(barrier, inc=1, device_id={"pb": (pb + d) % z.pb}, device_id_type=MESH)
        greeted += 1
    for d in range(1, z.ka):
        for e in (0, 1):
            pl.semaphore_signal(
                barrier, inc=1, device_id={"pb": y_of(e), "ka": (ka + d) % z.ka}, device_id_type=MESH
            )
            greeted += 1

    own_cols = pl.ds(pl.multiple_of(par * kcols, kcols), kcols)
    other_cols = pl.ds(pl.multiple_of((1 - par) * kcols, kcols), kcols)
    pairs = [
        (slater_hbm, slater), (inverse_hbm, inverse), (perm_hbm, perm), (tile_hbm, tiled), (expand_hbm, expand),
        (aux_ref.at[:, ka], auxb),
        (rc_ref.at[0, pl.ds(0, blk)], rcf.at[2 * ka]), (rc_ref.at[0, pl.ds(blk, blk)], rcf.at[2 * ka + 1]),
        (back_hbm, back),
        (chol_ref.at[0, :, own_cols], chols.at[pl.ds(pb * nchol, nchol)]),
    ]
    local = [pltpu.make_async_copy(src, dst, lsem.at[i]) for i, (src, dst) in enumerate(pairs)]
    for copy in local:
        copy.start()

    slot_row = lax.broadcasted_iota(jnp.int32, (z.wa * ROWS, wb), 0)
    slot_walker = lax.broadcasted_iota(jnp.int32, (z.wa * ROWS, wb), 1)
    wanted = jnp.full((z.wa * ROWS, wb), -1, jnp.int32)
    row_chunk = jnp.full((z.wa * ROWS, wb), -1, jnp.int32)
    within = slot_row % ROWS
    for j in range(PAIR):
        inside = (within >= j * nc) & (within < (j + 1) * nc)
        row_chunk = jnp.where(inside, within - j * nc, row_chunk)
        for d in range(z.wa):
            wanted = jnp.where(inside & (slot_row >= d * ROWS) & (slot_row < (d + 1) * ROWS), send_ref[d, j], wanted)
    chosen = (wanted == slot_walker).astype(F32)

    def source_chunk(c):
        if c < z.chunks:
            return slater[:, c * z.width : (c + 1) * z.width]
        return inverse[...]

    local[0].wait()
    local[1].wait()
    out = None
    for c in range(nc):
        select = jnp.where(row_chunk == c, chosen, 0.0).astype(BF)
        part = dot(select, source_chunk(c))
        out = part if out is None else out + part
    sendbuf[...] = out.astype(BF).reshape(z.wa, ROWS, z.width)
    recv[wa] = jnp.zeros((ROWS, z.width), BF)

    pl.semaphore_wait(barrier, greeted)

    a_copies = []
    for d in range(1, z.wa):
        to = (wa + d) % z.wa
        a_copies.append(remote(sendbuf.at[to], recv.at[wa], a_s.at[d], a_r.at[d], wa=to))
    for copy in a_copies:
        copy.start()

    quarter = wa % 4
    sib_quarter = flip(quarter)
    x_quarter = (quarter + 2) % 4
    sent = []

    def start(copy):
        copy.start()
        sent.append(copy)

    def rcf_part(block, u):
        return rcf.at[2 * block + u // 2, pl.ds((u % 2) * z.quarter, z.quarter)]

    def ring_copy(e, arriving):
        i = ring.index(e)
        if arriving:
            here = rcf_part(ring.block(e), quarter)
            return remote(here, here, ring_s.at[i], ring_r.at[i], ka=ring.target(e))
        block = ring.sent_block(e)
        if e[0] == 1:
            src = rc_ref.at[0, pl.ds(quarter * z.quarter, z.quarter)]
        else:
            src = rcf_part(block, quarter)
        return remote(src, rcf_part(block, quarter), ring_s.at[i], ring_r.at[i], ka=ring.target(e))

    def part_copy(block, u, send, recv_sem, to):
        part = rcf_part(block, u)
        return remote(part, part, send, recv_sem, wa=to)

    def serve_ring(s):
        for e in ring.of_step(s):
            ring_copy(e, True).wait_recv()
        if s < z.half:
            for e in ring.of_step(s + 1):
                start(ring_copy(e, False))
        for e in ring.of_step(s):
            i, block = ring.index(e), ring.block(e)
            start(part_copy(block, quarter, x_s.at[i], x_r.at[i], x_to))
            start(part_copy(block, quarter, sib_s.at[i], sib_r.at[i], sibling))

    def serve_x(s):
        for e in ring.of_step(s):
            i, block = ring.index(e), ring.block(e)
            part_copy(block, x_quarter, x_s.at[i], x_r.at[i], x_to).wait_recv()
            start(part_copy(block, x_quarter, xs_s.at[i], xs_r.at[i], sibling))

    qrows = nchol // 4
    hrows = qrows // 2
    sources = (left, right, across)

    def chol_rows(q, u):
        return chols.at[pl.ds(q * nchol + u * qrows, qrows)]

    def chol_half(q, i):
        return chols.at[pl.ds(q * nchol + quarter * qrows + i * hrows, hrows)]

    def chol_first():
        for i, to in enumerate((right, left)):
            start(
                remote(
                    chol_ref.at[0, pl.ds(quarter * qrows, qrows), other_cols],
                    chol_rows(pb, quarter), n_s.at[i], n_r.at[i], pb=to,
                )
            )
        for i, to in enumerate((right, left)):
            start(
                remote(
                    chol_ref.at[0, pl.ds(quarter * qrows + i * hrows, hrows), own_cols],
                    relay.at[i], p_s.at[i], p_r.at[i], pb=to,
                )
            )

    def chol_relay():
        for i, (q, to) in enumerate(((left, right), (right, left))):
            remote(relay.at[i], relay.at[i], p_s.at[i], p_r.at[i], pb=to).wait_recv()
            start(remote(relay.at[i], chol_half(q, i), q_s.at[i], q_r.at[i], pb=to))

    def chol_share(i):
        q = sources[i]
        if i < 2:
            rows = chol_rows(q, quarter)
            remote(rows, rows, n_s.at[i], n_r.at[i], pb=right).wait_recv()
        else:
            for h in range(2):
                rows = chol_half(q, h)
                remote(rows, rows, q_s.at[h], q_r.at[h], pb=right).wait_recv()
        rows = chol_rows(q, quarter)
        start(remote(rows, rows, cx_s.at[i], cx_r.at[i], wa=x_to))
        start(remote(rows, rows, cb_s.at[i], cb_r.at[i], wa=sibling))

    def chol_pass_on(i):
        rows = chol_rows(sources[i], x_quarter)
        remote(rows, rows, cx_s.at[i], cx_r.at[i], wa=x_to).wait_recv()
        start(remote(rows, rows, cs_s.at[i], cs_r.at[i], wa=sibling))

    for e in ring.of_step(1):
        start(ring_copy(e, False))
    chol_first()

    pick_row = lax.broadcasted_iota(jnp.int32, (wb, z.wa * ROWS), 0)
    pick_lane = lax.broadcasted_iota(jnp.int32, (wb, z.wa * ROWS), 1)
    taken = jnp.full((wb, z.wa * ROWS), -1, jnp.int32)
    for w in range(wb):
        taken = jnp.where(pick_row == w, take_ref[w], taken)
    lane_within = pick_lane % ROWS
    code = jnp.full((wb, z.wa * ROWS), -2, jnp.int32)
    lane_chunk = jnp.full((wb, z.wa * ROWS), -1, jnp.int32)
    for j in range(PAIR):
        inside = (lane_within >= j * nc) & (lane_within < (j + 1) * nc)
        code = jnp.where(inside, wb + PAIR * (pick_lane // ROWS) + j, code)
        lane_chunk = jnp.where(inside, lane_within - j * nc, lane_chunk)
    from_others = (taken == code).astype(F32)
    from_own = (taken == pick_lane).astype(F32)[:, :wb].astype(BF)
    for d in range(1, z.wa):
        here = recv.at[(wa + z.wa - d) % z.wa]
        remote(here, here, a_s.at[d], a_r.at[d], wa=(wa + d) % z.wa).wait_recv()
    got = recv[...].reshape(z.wa * ROWS, z.width)
    for c in range(nc):
        select = jnp.where(lane_chunk == c, from_others, 0.0).astype(BF)
        picked = dot(from_own, source_chunk(c)) + dot(select, got)
        if c < z.chunks:
            for k in range(4):
                sk[pl.ds((4 * c + k) * wb, wb), :] = picked[:, k * blk : (k + 1) * blk]
        else:
            for k in range(z.nk):
                ik[pl.ds(k * wb, wb), :] = picked[:, k * sq : (k + 1) * sq]

    serve_ring(1)

    def g_piece(y, c):
        return gall.at[y, pl.ds(2 * c, 2)]

    def g_pass_on(c):
        src, to = (left, right) if c % 2 == 0 else (right, left)
        piece = g_piece(src, c)
        remote(piece, piece, g_s.at[3 * c + c % 2], g_r.at[3 * c + c % 2], pb=to).wait_recv()
        start(remote(piece, piece, g_s.at[3 * c + 2], g_r.at[3 * c + 2], pb=to))

    rows = 4 * wb
    for copy in local[2:5]:
        copy.wait()
    for c in range(z.chunks):
        part = pl.ds(c * rows, rows)
        ordered = dot(sk[part, :].astype(BF), perm[...])
        for k in range(4):
            sps[4 * c + k] = ordered[k * wb : (k + 1) * wb, :].astype(BF)
        ordered = ordered.astype(BF)
        inv = ik[part, :].astype(BF)
        green = None
        for j in range(nocc):
            one = dot(inv, expand[j]) * dot(ordered[:, j * norb : (j + 1) * norb], tiled[...])
            green = one if green is None else green + one
        for k in range(2):
            both = jnp.concatenate(
                [green[2 * k * wb : (2 * k + 1) * wb], green[(2 * k + 1) * wb : (2 * k + 2) * wb]], axis=1
            )
            gall[pb, 2 * c + k] = both.astype(BF)
        for i, to in enumerate((right, left)):
            piece = g_piece(pb, c)
            start(remote(piece, piece, g_s.at[3 * c + i], g_r.at[3 * c + i], pb=to))
        if c == 0 and z.half > 1:
            serve_ring(2)
            serve_x(1)
        if c == 2 and z.half > 2:
            serve_ring(3)
            serve_x(2)
        if c > 0:
            g_pass_on(c - 1)

    def slot(d):
        return (z.ka - d) % z.ka

    for d in range(z.ka):
        for e in (0, 1):
            i = 2 * d + e
            to_z, to_y = (ka + d) % z.ka, y_of(e)
            src = sps.at[2 * to_z + to_y % 2]
            dst = ts.at[slot(d), par]
            if d == 0 and e == 0:
                own_ts = pltpu.make_async_copy(src, dst, lsem.at[10])
                own_ts.start()
            else:
                start(remote(src, dst, t_s.at[i], t_r.at[i], pb=to_y, ka=to_z))
    g_pass_on(z.chunks - 1)
    chol_relay()
    chol_share(0)
    chol_share(1)

    done_ring = 1 + (z.half > 1) + (z.half > 2 and z.chunks > 2)
    for s in range(done_ring + 1, z.half + 1):
        serve_ring(s)
    for s in range(done_ring, z.half + 1):
        serve_x(s)
    for c in range(z.chunks):
        for i, src in ((1, right) if c % 2 == 0 else (0, left), (2, across)):
            piece = g_piece(src, c)
            remote(piece, piece, g_s.at[3 * c + i], g_r.at[3 * c + i], pb=right).wait_recv()
    for e in ring.events:
        i, block = ring.index(e), ring.block(e)
        part_copy(block, sib_quarter, sib_s.at[i], sib_r.at[i], sibling).wait_recv()
        part_copy(block, (sib_quarter + 2) % 4, xs_s.at[i], xs_r.at[i], sibling).wait_recv()
    for copy in local[5:8]:
        copy.wait()

    acc[...] = jnp.zeros_like(acc)

    def one_k(k, carry):
        other = pair_ref[pb, k]
        both = jnp.concatenate([gall[y, other // 2].astype(F32) for y in range(z.pb)], axis=0)
        odd = (other % 2).astype(F32)
        one = both[:, :blk] * (1.0 - odd) + both[:, blk:] * odd
        acc[...] += dot(one.astype(BF), rcf[k])
        return carry

    lax.fori_loop(0, z.nk, one_k, 0)
    for y in range(z.pb):
        bias = acc[pl.ds(y * wb, wb), :]
        fbuf[y] = (auxb[y].astype(F32) - force_coef * bias).astype(BF)

    for d in range(1, z.pb):
        to = (pb + d) % z.pb
        start(remote(fbuf.at[pl.ds(to - to % 2, 2)], fqs.at[pb, 0], fy_s.at[d], fy_r.at[d], pb=to))
    own_f = pltpu.make_async_copy(fbuf.at[pl.ds(base, 2)], fqs.at[pb, 0], lsem.at[11])
    own_f.start()
    own_o = pltpu.make_async_copy(fbuf, fall.at[:, ka], lsem.at[12])
    own_o.start()
    own_f.wait()
    for d in range(1, z.pb):
        here = fqs.at[(pb + z.pb - d) % z.pb, 0]
        remote(here, here, fy_s.at[d], fy_r.at[d], pb=right).wait_recv()

    def arrive_slot(e):
        return (z.ka - e[0]) % z.ka if e[1] == 0 else e[0]

    def fq_copy(e, arriving):
        i = ring.index(e)
        here = fqs.at[:, arrive_slot(e)]
        if arriving or e[0] == 1:
            src = here if arriving else fqs.at[:, 0]
        elif e[0] == z.half:
            back_steps = z.half - 1
            src = fqs.at[:, z.ka - back_steps + core * (2 * back_steps - z.ka)]
        else:
            src = fqs.at[:, arrive_slot((e[0] - 1, e[1]))]
        return remote(src, here, fz_s.at[i], fz_r.at[i], ka=ring.target(e))

    def fo_copy(e, arriving):
        i = ring.index(e)
        block = ring.block(e) if arriving else ring.sent_block(e)
        here = fall.at[:, block]
        src = fbuf if e[0] == 1 and not arriving else here
        return remote(src, here, fo_s.at[i], fo_r.at[i], ka=ring.target(e))

    def serve(copy_of, s):
        for e in ring.of_step(s):
            copy_of(e, True).wait_recv()
        if s < z.half:
            for e in ring.of_step(s + 1):
                start(copy_of(e, False))

    for e in ring.of_step(1):
        start(fq_copy(e, False))
    chol_share(2)
    chol_pass_on(0)
    chol_pass_on(1)

    tiles, lanes = vs.shape[0], vs.shape[3]
    for d in range(z.ka):
        for e in (0, 1):
            if d == 0 and e == 0:
                continue
            i = 2 * d + e
            here = ts.at[slot(d), y_of(e) % 2]
            remote(here, here, t_s.at[i], t_r.at[i], pb=y_of(e), ka=(ka + d) % z.ka).wait_recv()
    own_ts.wait()
    for r in range(z.ka):
        for h in range(2):
            stage[pl.ds((2 * r + h) * wb, wb), :] = ts[r, h].astype(F32)
    for t in range(tiles):
        first = stage[pl.ds(t * lanes, lanes), :].T.reshape(nocc, norb, lanes)
        term[0, t] = first
        total[t] = first

    for s in range(1, z.half + 1):
        serve(fq_copy, s)
    for e in ring.of_step(1):
        start(fo_copy(e, False))
    chol_pass_on(2)
    for q in range(4):
        whole = jnp.concatenate([fqs[q, r, h].astype(F32) for r in range(z.ka) for h in range(2)], axis=0)
        fmat[q] = whole.astype(BF)
    for i, q in enumerate(sources):
        for u, s_sem, r_sem in ((sib_quarter, cb_s, cb_r), ((sib_quarter + 2) % 4, cs_s, cs_r)):
            part = chol_rows(q, u)
            remote(part, part, s_sem.at[i], r_sem.at[i], wa=sibling).wait_recv()
    for copy in local[8:]:
        copy.wait()

    steps = max(1, norb // 8)
    ps = norb // steps
    width = ps * norb

    def potential(b, carry):
        cols = pl.ds(pl.multiple_of(b * width, width), width)
        v = dot(fmat[0], chols[pl.ds(0, nchol), cols])
        for q in range(1, 4):
            v = v + dot(fmat[q], chols[pl.ds(q * nchol, nchol), cols])
        for t in range(tiles):
            vt[t] = v[t * lanes : (t + 1) * lanes, :].T
            for p2 in range(norb):
                vs[t, p2, pl.ds(pl.multiple_of(b * ps, ps), ps), :] = vt[t, pl.ds(p2, ps, stride=norb), :]
        return carry

    lax.fori_loop(0, steps, potential, 0)
    serve(fo_copy, 1)

    step_size = tau_coef / math.sqrt(norb)
    group = 4

    def one_tile(t):
        def one_degree(m, carry):
            scale = -step_size / m.astype(F32)
            now, later = (m + 1) % 2, m % 2

            def one_group(g, carry):
                accs = [jnp.zeros((norb, lanes), F32) for _ in range(group)]
                for p2 in range(norb):
                    column = vs[t, p2]
                    for a in range(group):
                        accs[a] = accs[a] + column * term[now, t, g * group + a, pl.ds(p2, 1), :]
                for a in range(group):
                    new = accs[a] * scale
                    term[later, t, g * group + a] = new
                    total[t, g * group + a] += new
                return carry

            return lax.fori_loop(0, nocc // group, one_group, carry)

        lax.fori_loop(1, 7, one_degree, 0)
        final = total[t].reshape(blk, lanes).T.astype(BF)
        stage[pl.ds(t * lanes, lanes), :] = dot(final, back[...])

    k_own = 2 * ka + par
    own_m = None
    finished = 0
    for t in range(tiles):
        one_tile(t)
        while finished < 2 * z.ka and (finished + 1) * wb <= (t + 1) * lanes:
            r, h = finished // 2, finished % 2
            moved[r, h] = stage[pl.ds(finished * wb, wb), :].astype(BF)
            finished += 1
            if h == 0:
                continue
            to_z = (ka + r) % z.ka
            for e in (0, 1):
                to_y = y_of(e)
                src = moved.at[r, to_y % 2]
                i = 2 * r + e
                if r == 0 and e == 0:
                    own_m = pltpu.make_async_copy(src, land.at[k_own], lsem.at[13])
                    own_m.start()
                else:
                    start(remote(src, land.at[k_own], m_s.at[i], m_r.at[i], pb=to_y, ka=to_z))
        if t == 0 and z.half > 1:
            serve(fo_copy, 2)
        if t == 1 and z.half > 2:
            serve(fo_copy, 3)
    for s in range(1 + (z.half > 1) + (z.half > 2 and tiles > 1) + 1, z.half + 1):
        serve(fo_copy, s)
    own_o.wait()
    out_f = pltpu.make_async_copy(fall, fields_ref, lsem.at[14])
    out_f.start()
    for r in range(z.ka):
        for e in (0, 1):
            if r == 0 and e == 0:
                continue
            i = 2 * r + e
            from_z = (ka + z.ka - r) % z.ka
            here = land.at[2 * from_z + y_of(e) % 2]
            remote(here, here, m_s.at[i], m_r.at[i], pb=y_of(e), ka=(ka + r) % z.ka).wait_recv()
    own_m.wait()
    for k in range(z.nk):
        out_ref[:, k * blk : (k + 1) * blk] = land[k]
    for copy in a_copies + sent:
        copy.wait_send()
    out_f.wait()


def constants(z):
    perm = np.zeros((z.blk, z.blk), np.float32)
    for r in range(z.norb):
        for j in range(z.nocc):
            perm[r * z.nocc + j, j * z.norb + r] = 1
    expand = np.zeros((z.nocc, z.sq, z.blk), np.float32)
    tiled = np.zeros((z.norb, z.blk), np.float32)
    for i in range(z.nocc):
        for r in range(z.norb):
            tiled[r, i * z.norb + r] = 1
            for j in range(z.nocc):
                expand[j, i * z.nocc + j, i * z.norb + r] = 1
    return jnp.asarray(perm, BF), jnp.asarray(perm.T, BF), jnp.asarray(expand, BF), jnp.asarray(tiled, BF)


def body(z, slater, inverse, send_rows, take_rows, pair_table, rotated_chol, chol_vectors, aux_noise):
    wb, nk, blk, nchol, ka = z.wb, z.nk, z.blk, z.nchol, z.ka
    perm, back, expand, tiled = constants(z)
    vmem = pl.BlockSpec(memory_space=pltpu.VMEM)
    smem = pl.BlockSpec(memory_space=pltpu.SMEM)
    hbm = pl.BlockSpec(memory_space=pl.ANY)
    dma = lambda n: pltpu.SemaphoreType.DMA((n,))
    events = ka - 1
    kcols = z.norb * z.norb
    walkers = 2 * ka * wb
    lanes = min(128, walkers)
    tiles = walkers // lanes
    width = z.norb // max(1, z.norb // 8) * z.norb
    moved, fields = pl.pallas_call(
        functools.partial(step_kernel, z),
        out_shape=(
            jax.ShapeDtypeStruct((wb, nk * blk), BF),
            jax.ShapeDtypeStruct((4, ka, wb, nchol), BF),
        ),
        in_specs=[smem] * 3 + [hbm] * 9,
        out_specs=(vmem, hbm),
        scratch_shapes=[
            pltpu.VMEM((wb, nk * blk), BF),
            pltpu.VMEM((wb, nk * z.sq), BF),
            pltpu.VMEM((blk, blk), BF),
            pltpu.VMEM((blk, blk), BF),
            pltpu.VMEM((z.nocc, z.sq, blk), BF),
            pltpu.VMEM((z.norb, blk), BF),
            pltpu.VMEM((z.wa, ROWS, z.width), BF),
            pltpu.VMEM((z.wa, ROWS, z.width), BF),
            pltpu.VMEM((nk * wb, blk), F32),
            pltpu.VMEM((nk * wb, z.sq), F32),
            pltpu.VMEM((nk, wb, blk), BF),
            pltpu.VMEM((4, nk // 2, wb, 2 * blk), BF),
            pltpu.VMEM((nk, blk, nchol), BF),
            pltpu.VMEM((4 * wb, nchol), F32),
            pltpu.VMEM((4, wb, nchol), BF),
            pltpu.VMEM((4, wb, nchol), BF),
            pltpu.VMEM((4, ka, 2, wb, nchol), BF),
            pltpu.VMEM((4, walkers, nchol), BF),
            pltpu.VMEM((4, ka, wb, nchol), BF),
            pltpu.VMEM((4 * nchol, kcols), BF),
            pltpu.VMEM((2, nchol // 8, kcols), BF),
            pltpu.VMEM((ka, 2, wb, blk), BF),
            pltpu.VMEM((walkers, blk), F32),
            pltpu.VMEM((ka, 2, wb, blk), BF),
            pltpu.VMEM((nk, wb, blk), BF),
            pltpu.VMEM((tiles, width, lanes), F32),
            pltpu.VMEM((tiles, z.norb, z.norb, lanes), F32),
            pltpu.VMEM((2, tiles, z.nocc, z.norb, lanes), F32),
            pltpu.VMEM((tiles, z.nocc, z.norb, lanes), F32),
            dma(16), dma(z.wa), dma(z.wa), dma(2 * ka), dma(2 * ka), dma(3 * z.chunks), dma(3 * z.chunks),
            dma(events), dma(events), dma(events), dma(events), dma(events), dma(events), dma(events), dma(events),
            dma(2), dma(2), dma(2), dma(2), dma(2), dma(2), dma(3), dma(3), dma(3), dma(3), dma(3), dma(3),
            dma(4), dma(4), dma(events), dma(events), dma(events), dma(events), dma(2 * ka), dma(2 * ka),
        ],
        compiler_params=pltpu.CompilerParams(
            collective_id=0, has_side_effects=True, vmem_limit_bytes=58 * 1024 * 1024
        ),
        cost_estimate=pl.CostEstimate(flops=6 * 10**9, bytes_accessed=30 * 10**6, transcendentals=0),
    )(
        send_rows, take_rows, pair_table, slater, inverse, perm, back, expand, tiled,
        rotated_chol, chol_vectors, aux_noise.reshape(4, ka, wb, nchol),
    )
    return moved, fields.reshape(4 * ka * wb, nchol)


def solution(mesh, z=Sizes(8, 8, 16, 48, 12, 512, 24)):
    placed = (
        P(("wa", "pb", "ka"), None),
        P(("wa", "pb", "ka"), None),
        P(("wa", "pb", "ka"), None),
        P(("wa", "pb", "ka")),
        P(),
        P("pb", "ka", None),
        P("pb", None, "ka"),
        P("wa", "pb"),
    )
    return jax.shard_map(
        functools.partial(body, z),
        mesh=mesh,
        in_specs=placed,
        out_specs=(P(("wa", "pb", "ka"), None), P("wa", "pb")),
        check_vma=False,
    )
```

```python
import functools
import math

import jax
import jax.numpy as jnp
import numpy as np
from jax import lax
from jax.experimental import pallas as pl
from jax.experimental.pallas import tpu as pltpu
from jax.sharding import PartitionSpec as P

MESH = pl.DeviceIdType.MESH
BF = jnp.bfloat16
F32 = jnp.float32
PAIR = 3
ROWS = 16
tau_coef = 2.0
force_coef = 0.5


class Sizes:
    def __init__(self, wa, ka, nk, norb, nocc, nchol, wb):
        self.wa, self.pb, self.ka, self.nk = wa, 4, ka, nk
        self.norb, self.nocc, self.nchol, self.wb = norb, nocc, nchol, wb
        self.blk = norb * nocc
        self.sq = nocc * nocc
        self.width = 4 * self.blk
        self.chunks = nk // 4
        self.half = ka // 2
        self.quarter = 2 * self.blk // 4


def dot(a, b):
    return jnp.dot(a, b, preferred_element_type=F32)


def flip(i):
    return i + 1 - 2 * (i % 2)


def remote(src, dst, send, recv, **place):
    return pltpu.make_async_remote_copy(
        src_ref=src, dst_ref=dst, send_sem=send, recv_sem=recv, device_id=place, device_id_type=MESH
    )


def ring_events(half):
    events = [(s, d) for s in range(1, half) for d in (0, 1)]
    return events + [(half, 0)]


class Ring:
    def __init__(self, size, me, core):
        self.n, self.half, self.me, self.core = size, size // 2, me, core
        self.events = ring_events(self.half)

    def index(self, event):
        return self.events.index(event)

    def block(self, event):
        s, d = event
        if s == self.half:
            return (self.me + self.half) % self.n
        return (self.me + (self.n - s if d == 0 else s)) % self.n

    def sent_block(self, event):
        s, d = event
        if s == self.half:
            back = self.half - 1
            return (self.me + self.n - back + 2 * back * self.core) % self.n
        return (self.me + (self.n - s + 1 if d == 0 else s - 1)) % self.n

    def target(self, event):
        s, d = event
        if s == self.half:
            return (self.me + 1 + (self.n - 2) * self.core) % self.n
        return (self.me + (1 if d == 0 else self.n - 1)) % self.n

    def of_step(self, s):
        return [e for e in self.events if e[0] == s]


def step_kernel(
    z, send_ref, take_ref, pair_ref, slater_hbm, inverse_hbm, perm_hbm, back_hbm, expand_hbm, tile_hbm,
    rc_ref, chol_ref, aux_ref,
    out_ref, fields_ref,
    slater, inverse, perm, back, expand, tiled, sendbuf, recv, sk, ik, sps, gall, rcf, acc, auxb, fbuf,
    fqs, fmat, chols, relay, ts, stage, moved, land, vt, vs, term, total,
    lsem, a_s, a_r, t_s, t_r, g_s, g_r, ring_s, ring_r, sib_s, sib_r, x_s, x_r, xs_s, xs_r,
    n_s, n_r, p_s, p_r, q_s, q_r, cb_s, cb_r, cx_s, cx_r, cs_s, cs_r, fy_s, fy_r, fz_s, fz_r, o_s, m_s, m_r,
):
    wa, pb, ka = lax.axis_index("wa"), lax.axis_index("pb"), lax.axis_index("ka")
    core, x = wa % 2, wa // 2
    xs = z.wa // 2
    sibling = flip(wa)
    x_to = ((x + 1 + (xs - 2) * core) % xs) * 2 + core
    base = pb - pb % 2
    par = pb % 2
    near = flip(pb)
    right, left, across = (pb + 1) % z.pb, (pb + 3) % z.pb, (pb + 2) % z.pb
    ring = Ring(z.ka, ka, core)
    wb, blk, norb, nocc, sq, nchol = z.wb, z.blk, z.norb, z.nocc, z.sq, z.nchol
    nc = z.chunks + 1
    kcols = norb * norb

    order = [0] + [r for s in range(1, z.half) for r in (s, z.ka - s)] + [z.half]
    place = {r: p for p, r in enumerate(order)}

    def y_of(e):
        return pb if e == 0 else near

    barrier = pltpu.get_barrier_semaphore()
    greeted = 0
    for d in range(1, z.wa):
        pl.semaphore_signal(barrier, inc=1, device_id={"wa": (wa + d) % z.wa}, device_id_type=MESH)
        greeted += 1
    for d in range(1, z.pb):
        pl.semaphore_signal(barrier, inc=1, device_id={"pb": (pb + d) % z.pb}, device_id_type=MESH)
        greeted += 1
    for d in range(1, z.ka):
        for e in (0, 1):
            pl.semaphore_signal(
                barrier, inc=1, device_id={"pb": y_of(e), "ka": (ka + d) % z.ka}, device_id_type=MESH
            )
            greeted += 1

    own_cols = pl.ds(pl.multiple_of(par * kcols, kcols), kcols)
    other_cols = pl.ds(pl.multiple_of((1 - par) * kcols, kcols), kcols)
    pairs = [
        (slater_hbm, slater), (inverse_hbm, inverse), (perm_hbm, perm), (tile_hbm, tiled), (expand_hbm, expand),
        (aux_ref.at[:, ka], auxb),
        (rc_ref.at[0, pl.ds(0, blk)], rcf.at[2 * ka]), (rc_ref.at[0, pl.ds(blk, blk)], rcf.at[2 * ka + 1]),
        (back_hbm, back),
        (chol_ref.at[0, :, own_cols], chols.at[pl.ds(pb * nchol, nchol)]),
    ]
    local = [pltpu.make_async_copy(src, dst, lsem.at[i]) for i, (src, dst) in enumerate(pairs)]
    for copy in local:
        copy.start()

    slot_row = lax.broadcasted_iota(jnp.int32, (z.wa * ROWS, wb), 0)
    slot_walker = lax.broadcasted_iota(jnp.int32, (z.wa * ROWS, wb), 1)
    wanted = jnp.full((z.wa * ROWS, wb), -1, jnp.int32)
    row_chunk = jnp.full((z.wa * ROWS, wb), -1, jnp.int32)
    within = slot_row % ROWS
    for j in range(PAIR):
        inside = (within >= j * nc) & (within < (j + 1) * nc)
        row_chunk = jnp.where(inside, within - j * nc, row_chunk)
        for d in range(z.wa):
            wanted = jnp.where(inside & (slot_row >= d * ROWS) & (slot_row < (d + 1) * ROWS), send_ref[j, d], wanted)
    chosen = (wanted == slot_walker).astype(F32)

    def source_chunk(c):
        if c < z.chunks:
            return slater[:, c * z.width : (c + 1) * z.width]
        return inverse[...]

    local[0].wait()
    local[1].wait()
    out = None
    for c in range(nc):
        select = jnp.where(row_chunk == c, chosen, 0.0).astype(BF)
        part = dot(select, source_chunk(c))
        out = part if out is None else out + part
    sendbuf[...] = out.astype(BF).reshape(z.wa, ROWS, z.width)
    recv[wa] = jnp.zeros((ROWS, z.width), BF)

    pl.semaphore_wait(barrier, greeted)

    a_copies = []
    for d in range(1, z.wa):
        to = (wa + d) % z.wa
        a_copies.append(remote(sendbuf.at[to], recv.at[wa], a_s.at[d], a_r.at[d], wa=to))
    for copy in a_copies:
        copy.start()

    quarter = wa % 4
    sib_quarter = flip(quarter)
    x_quarter = (quarter + 2) % 4
    sent = []

    def start(make):
        make().start()
        sent.append(make)

    def rcf_part(block, u):
        return rcf.at[2 * block + u // 2, pl.ds((u % 2) * z.quarter, z.quarter)]

    def ring_copy(e, arriving):
        i = ring.index(e)
        if arriving:
            here = rcf_part(ring.block(e), quarter)
            return remote(here, here, ring_s.at[i], ring_r.at[i], ka=ring.target(e))
        block = ring.sent_block(e)
        if e[0] == 1:
            src = rc_ref.at[0, pl.ds(quarter * z.quarter, z.quarter)]
        else:
            src = rcf_part(block, quarter)
        return remote(src, rcf_part(block, quarter), ring_s.at[i], ring_r.at[i], ka=ring.target(e))

    def part_copy(block, u, send, recv_sem, to):
        part = rcf_part(block, u)
        return remote(part, part, send, recv_sem, wa=to)

    def serve_ring(s):
        for e in ring.of_step(s):
            ring_copy(e, True).wait_recv()
        if s < z.half:
            for e in ring.of_step(s + 1):
                start(functools.partial(ring_copy, e, False))
        for e in ring.of_step(s):
            i, block = ring.index(e), ring.block(e)
            start(functools.partial(part_copy, block, quarter, x_s.at[i], x_r.at[i], x_to))
            start(functools.partial(part_copy, block, quarter, sib_s.at[i], sib_r.at[i], sibling))

    def serve_x(s):
        for e in ring.of_step(s):
            i, block = ring.index(e), ring.block(e)
            part_copy(block, x_quarter, x_s.at[i], x_r.at[i], x_to).wait_recv()
            start(functools.partial(part_copy, block, x_quarter, xs_s.at[i], xs_r.at[i], sibling))

    qrows = nchol // 4
    hrows = qrows // 2
    sources = (left, right, across)

    def chol_rows(q, u):
        return chols.at[pl.ds(q * nchol + u * qrows, qrows)]

    def chol_half(q, i):
        return chols.at[pl.ds(q * nchol + quarter * qrows + i * hrows, hrows)]

    def chol_first():
        for i, to in enumerate((right, left)):
            start(
                functools.partial(
                    remote,
                    chol_ref.at[0, pl.ds(quarter * qrows, qrows), other_cols],
                    chol_rows(pb, quarter), n_s.at[i], n_r.at[i], pb=to,
                )
            )

    def chol_across():
        for i, to in enumerate((right, left)):
            start(
                functools.partial(
                    remote,
                    chol_ref.at[0, pl.ds(quarter * qrows + i * hrows, hrows), own_cols],
                    relay.at[i], p_s.at[i], p_r.at[i], pb=to,
                )
            )

    def chol_relay():
        for i, (q, to) in enumerate(((left, right), (right, left))):
            remote(relay.at[i], relay.at[i], p_s.at[i], p_r.at[i], pb=to).wait_recv()
            start(functools.partial(remote, relay.at[i], chol_half(q, i), q_s.at[i], q_r.at[i], pb=to))

    def chol_share(i):
        q = sources[i]
        if i < 2:
            rows = chol_rows(q, quarter)
            remote(rows, rows, n_s.at[i], n_r.at[i], pb=right).wait_recv()
        else:
            for h in range(2):
                rows = chol_half(q, h)
                remote(rows, rows, q_s.at[h], q_r.at[h], pb=right).wait_recv()
        rows = chol_rows(q, quarter)
        start(functools.partial(remote, rows, rows, cx_s.at[i], cx_r.at[i], wa=x_to))
        start(functools.partial(remote, rows, rows, cb_s.at[i], cb_r.at[i], wa=sibling))

    def chol_pass_on(i):
        rows = chol_rows(sources[i], x_quarter)
        remote(rows, rows, cx_s.at[i], cx_r.at[i], wa=x_to).wait_recv()
        start(functools.partial(remote, rows, rows, cs_s.at[i], cs_r.at[i], wa=sibling))

    for e in ring.of_step(1):
        start(functools.partial(ring_copy, e, False))
    chol_first()

    pick_row = lax.broadcasted_iota(jnp.int32, (wb, z.wa * ROWS), 0)
    pick_lane = lax.broadcasted_iota(jnp.int32, (wb, z.wa * ROWS), 1)
    taken = jnp.full((wb, z.wa * ROWS), -1, jnp.int32)
    for w in range(wb):
        taken = jnp.where(pick_row == w, take_ref[w], taken)
    lane_within = pick_lane % ROWS
    code = jnp.full((wb, z.wa * ROWS), -2, jnp.int32)
    lane_chunk = jnp.full((wb, z.wa * ROWS), -1, jnp.int32)
    for j in range(PAIR):
        inside = (lane_within >= j * nc) & (lane_within < (j + 1) * nc)
        code = jnp.where(inside, wb + PAIR * (pick_lane // ROWS) + j, code)
        lane_chunk = jnp.where(inside, lane_within - j * nc, lane_chunk)
    from_others = (taken == code).astype(F32)
    from_own = (taken == pick_lane).astype(F32)[:, :wb].astype(BF)
    for d in range(1, z.wa):
        here = recv.at[(wa + z.wa - d) % z.wa]
        remote(here, here, a_s.at[d], a_r.at[d], wa=(wa + d) % z.wa).wait_recv()
    got = recv[...].reshape(z.wa * ROWS, z.width)
    for c in range(nc):
        select = jnp.where(lane_chunk == c, from_others, 0.0).astype(BF)
        picked = dot(from_own, source_chunk(c)) + dot(select, got)
        if c < z.chunks:
            for k in range(4):
                sk[pl.ds((4 * c + k) * wb, wb), :] = picked[:, k * blk : (k + 1) * blk]
        else:
            for k in range(z.nk):
                ik[pl.ds(k * wb, wb), :] = picked[:, k * sq : (k + 1) * sq]

    serve_ring(1)

    def g_piece(y, c):
        return gall.at[y, pl.ds(2 * c, 2)]

    def g_pass_on(c):
        src, to = (left, right) if c % 2 == 0 else (right, left)
        piece = g_piece(src, c)
        remote(piece, piece, g_s.at[3 * c + c % 2], g_r.at[3 * c + c % 2], pb=to).wait_recv()
        start(functools.partial(remote, piece, piece, g_s.at[3 * c + 2], g_r.at[3 * c + 2], pb=to))

    rows = 4 * wb
    for copy in local[2:5]:
        copy.wait()
    for c in range(z.chunks):
        part = pl.ds(c * rows, rows)
        ordered = dot(sk[part, :].astype(BF), perm[...])
        for k in range(4):
            sps[4 * c + k] = ordered[k * wb : (k + 1) * wb, :].astype(BF)
        ordered = ordered.astype(BF)
        inv = ik[part, :].astype(BF)
        green = None
        for j in range(nocc):
            one = dot(inv, expand[j]) * dot(ordered[:, j * norb : (j + 1) * norb], tiled[...])
            green = one if green is None else green + one
        for k in range(2):
            both = jnp.concatenate(
                [green[2 * k * wb : (2 * k + 1) * wb], green[(2 * k + 1) * wb : (2 * k + 2) * wb]], axis=1
            )
            gall[pb, 2 * c + k] = both.astype(BF)
        for i, to in enumerate((right, left)):
            piece = g_piece(pb, c)
            start(functools.partial(remote, piece, piece, g_s.at[3 * c + i], g_r.at[3 * c + i], pb=to))
        if c == 0 and z.half > 1:
            serve_ring(2)
            serve_x(1)
        if c == 2 and z.half > 2:
            serve_ring(3)
            serve_x(2)
        if c > 0:
            g_pass_on(c - 1)

    def slot(d):
        return place[(z.ka - d) % z.ka]

    g_pass_on(z.chunks - 1)
    chol_across()
    done_ring = 1 + (z.half > 1) + (z.half > 2 and z.chunks > 2)
    for s in range(done_ring + 1, z.half + 1):
        serve_ring(s)
    for s in range(done_ring, z.half):
        serve_x(s)
    for d in range(z.ka):
        for e in (0, 1):
            i = 2 * d + e
            to_z, to_y = (ka + d) % z.ka, y_of(e)
            src = sps.at[2 * to_z + to_y % 2]
            dst = ts.at[slot(d), par]
            if d == 0 and e == 0:
                own_ts = pltpu.make_async_copy(src, dst, lsem.at[10])
                own_ts.start()
            else:
                start(functools.partial(remote, src, dst, t_s.at[i], t_r.at[i], pb=to_y, ka=to_z))
    serve_x(z.half)
    chol_share(0)
    chol_share(1)
    for c in range(z.chunks):
        for i, src in ((1, right) if c % 2 == 0 else (0, left), (2, across)):
            piece = g_piece(src, c)
            remote(piece, piece, g_s.at[3 * c + i], g_r.at[3 * c + i], pb=right).wait_recv()
    for e in ring.events:
        i, block = ring.index(e), ring.block(e)
        part_copy(block, sib_quarter, sib_s.at[i], sib_r.at[i], sibling).wait_recv()
        part_copy(block, (sib_quarter + 2) % 4, xs_s.at[i], xs_r.at[i], sibling).wait_recv()
    for copy in local[5:8]:
        copy.wait()

    acc[...] = jnp.zeros_like(acc)

    def one_k(k, carry):
        other = pair_ref[pb, k]
        both = jnp.concatenate([gall[y, other // 2].astype(F32) for y in range(z.pb)], axis=0)
        odd = (other % 2).astype(F32)
        one = both[:, :blk] * (1.0 - odd) + both[:, blk:] * odd
        acc[...] += dot(one.astype(BF), rcf[k])
        return carry

    lax.fori_loop(0, z.nk // 2, one_k, 0)
    chol_relay()
    lax.fori_loop(z.nk // 2, z.nk, one_k, 0)
    for y in range(z.pb):
        bias = acc[pl.ds(y * wb, wb), :]
        fbuf[y] = (auxb[y].astype(F32) - force_coef * bias).astype(BF)

    for d in range(1, z.pb):
        to = (pb + d) % z.pb
        start(functools.partial(
            remote, fbuf.at[pl.ds(to - to % 2, 2)], fqs.at[pb, 0], fy_s.at[d], fy_r.at[d], pb=to
        ))
    own_f = pltpu.make_async_copy(fbuf.at[pl.ds(base, 2)], fqs.at[pb, 0], lsem.at[11])
    own_f.start()
    rest_f = pltpu.make_async_copy(fbuf.at[pl.ds(2 - base, 2)], fqs.at[4, 0], lsem.at[12])
    rest_f.start()
    own_f.wait()
    rest_f.wait()
    for d in range(1, z.pb):
        here = fqs.at[(pb + z.pb - d) % z.pb, 0]
        remote(here, here, fy_s.at[d], fy_r.at[d], pb=right).wait_recv()

    def arrive_slot(e):
        return place[(z.ka - e[0]) % z.ka if e[1] == 0 else e[0]]

    def fq_copy(e, arriving):
        i = ring.index(e)
        here = fqs.at[:, arrive_slot(e)]
        if arriving:
            src = here
        elif e[0] == 1:
            src = fqs.at[:, 0]
        elif e[0] == z.half:
            one, other = place[z.ka - z.half + 1], place[z.half - 1]
            src = fqs.at[:, one + core * (other - one)]
        else:
            src = fqs.at[:, arrive_slot((e[0] - 1, e[1]))]
        return remote(src, here, fz_s.at[i], fz_r.at[i], ka=ring.target(e))

    def serve_fields(s):
        for e in ring.of_step(s):
            fq_copy(e, True).wait_recv()
        if s < z.half:
            for e in ring.of_step(s + 1):
                start(functools.partial(fq_copy, e, False))

    for e in ring.of_step(1):
        start(functools.partial(fq_copy, e, False))

    tiles, lanes = term.shape[1], vs.shape[2]
    for d in range(z.ka):
        for e in (0, 1):
            if d == 0 and e == 0:
                continue
            i = 2 * d + e
            here = ts.at[slot(d), y_of(e) % 2]
            remote(here, here, t_s.at[i], t_r.at[i], pb=y_of(e), ka=(ka + d) % z.ka).wait_recv()
    own_ts.wait()
    for p in range(z.ka):
        for h in range(2):
            stage[pl.ds((2 * p + h) * wb, wb), :] = ts[p, h].astype(F32)
    for t in range(tiles):
        first = stage[pl.ds(t * lanes, lanes), :].T.reshape(nocc, norb, lanes)
        term[0, t] = first
        total[t] = first
    chol_share(2)
    chol_pass_on(0)
    chol_pass_on(1)

    def all_of_chol():
        chol_pass_on(2)
        for i, q in enumerate(sources):
            for u, s_sem, r_sem in ((sib_quarter, cb_s, cb_r), ((sib_quarter + 2) % 4, cs_s, cs_r)):
                part = chol_rows(q, u)
                remote(part, part, s_sem.at[i], r_sem.at[i], wa=sibling).wait_recv()
        for copy in local[8:]:
            copy.wait()

    steps = max(1, norb // 8)
    ps = norb // steps
    width = ps * norb

    def potential(t):
        fields_of = [fmat[q, pl.ds(t * lanes, lanes), :].astype(BF) for q in range(4)]

        def some_rows(b, carry):
            cols = pl.ds(pl.multiple_of(b * width, width), width)
            v = dot(fields_of[0], chols[pl.ds(0, nchol), cols])
            for q in range(1, 4):
                v = v + dot(fields_of[q], chols[pl.ds(q * nchol, nchol), cols])
            vt[...] = v.T
            for p2 in range(norb):
                vs[p2, pl.ds(pl.multiple_of(b * ps, ps), ps), :] = vt[pl.ds(p2, ps, stride=norb), :]
            return carry

        lax.fori_loop(0, steps, some_rows, 0)

    step_size = tau_coef / math.sqrt(norb)
    group = 4

    def propagate(t, between):
        def one_degree(m, carry):
            scale = -step_size / m.astype(F32)
            now, later = (m + 1) % 2, m % 2

            def one_group(g, carry):
                accs = [jnp.zeros((norb, lanes), F32) for _ in range(group)]
                for p2 in range(norb):
                    column = vs[p2]
                    for a in range(group):
                        accs[a] = accs[a] + column * term[now, t, g * group + a, pl.ds(p2, 1), :]
                for a in range(group):
                    new = accs[a] * scale
                    term[later, t, g * group + a] = new
                    total[t, g * group + a] += new
                return carry

            lax.fori_loop(0, nocc // group, one_group, 0)
            return carry

        if between is None:
            lax.fori_loop(1, 7, one_degree, 0)
        else:
            lax.fori_loop(1, 5, one_degree, 0)
            between()
            lax.fori_loop(5, 7, one_degree, 0)
        final = total[t].reshape(blk, lanes).T.astype(BF)
        stage[pl.ds(t * lanes, lanes), :] = dot(final, back[...])

    k_own = 2 * ka + par
    own_m = None
    out_f = []

    def write_fields():
        for p in range(z.ka):
            block = (ka + order[p]) % z.ka
            for n, (q, first) in enumerate(((pb, base), (4, 2 - base))):
                out_f.append(
                    pltpu.make_async_copy(fqs.at[q, p], fields_ref.at[pl.ds(first, 2), block], o_s.at[2 * p + n])
                )
                out_f[-1].start()

    served, arrived, finished = 0, 0, 0

    def serve_to(s):
        nonlocal served
        while served < min(s, z.half):
            served += 1
            serve_fields(served)

    for t in range(tiles):
        last_place = -(-(t + 1) * lanes // (2 * wb)) - 1
        need = min(z.half, (last_place + 1) // 2)
        serve_to(need)
        while arrived <= last_place:
            for q in range(4):
                for h in range(2):
                    fmat[q, pl.ds((2 * arrived + h) * wb, wb), :] = fqs[q, arrived, h].astype(F32)
            arrived += 1
        if t == 0:
            all_of_chol()
        potential(t)
        if served < z.half:
            propagate(t, functools.partial(serve_to, served + 1))
        else:
            if t == tiles - 1:
                write_fields()
            propagate(t, None)
        while finished < 2 * z.ka and (finished + 1) * wb <= (t + 1) * lanes:
            p, h = finished // 2, finished % 2
            moved[p, h] = stage[pl.ds(finished * wb, wb), :].astype(BF)
            finished += 1
            if h == 0:
                continue
            r = order[p]
            to_z = (ka + r) % z.ka
            for e in (0, 1):
                to_y = y_of(e)
                src = moved.at[p, to_y % 2]
                i = 2 * r + e
                if r == 0 and e == 0:
                    own_m = pltpu.make_async_copy(src, land.at[k_own], lsem.at[13])
                    own_m.start()
                else:
                    start(functools.partial(remote, src, land.at[k_own], m_s.at[i], m_r.at[i], pb=to_y, ka=to_z))
    for r in range(z.ka):
        for e in (0, 1):
            if r == 0 and e == 0:
                continue
            i = 2 * r + e
            from_z = (ka + z.ka - r) % z.ka
            here = land.at[2 * from_z + y_of(e) % 2]
            remote(here, here, m_s.at[i], m_r.at[i], pb=y_of(e), ka=(ka + r) % z.ka).wait_recv()
    own_m.wait()
    for k in range(z.nk):
        out_ref[:, k * blk : (k + 1) * blk] = land[k]
    for copy in a_copies:
        copy.wait_send()
    for make in sent:
        make().wait_send()
    for copy in out_f:
        copy.wait()


def constants(z):
    perm = np.zeros((z.blk, z.blk), np.float32)
    for r in range(z.norb):
        for j in range(z.nocc):
            perm[r * z.nocc + j, j * z.norb + r] = 1
    expand = np.zeros((z.nocc, z.sq, z.blk), np.float32)
    tiled = np.zeros((z.norb, z.blk), np.float32)
    for i in range(z.nocc):
        for r in range(z.norb):
            tiled[r, i * z.norb + r] = 1
            for j in range(z.nocc):
                expand[j, i * z.nocc + j, i * z.norb + r] = 1
    return jnp.asarray(perm, BF), jnp.asarray(perm.T, BF), jnp.asarray(expand, BF), jnp.asarray(tiled, BF)


def body(z, slater, inverse, send_rows, take_rows, pair_table, rotated_chol, chol_vectors, aux_noise):
    wb, nk, blk, nchol, ka = z.wb, z.nk, z.blk, z.nchol, z.ka
    perm, back, expand, tiled = constants(z)
    vmem = pl.BlockSpec(memory_space=pltpu.VMEM)
    smem = pl.BlockSpec(memory_space=pltpu.SMEM)
    hbm = pl.BlockSpec(memory_space=pl.ANY)
    dma = lambda n: pltpu.SemaphoreType.DMA((n,))
    events = ka - 1
    kcols = z.norb * z.norb
    walkers = 2 * ka * wb
    lanes = min(128, walkers)
    tiles = walkers // lanes
    width = z.norb // max(1, z.norb // 8) * z.norb
    moved, fields = pl.pallas_call(
        functools.partial(step_kernel, z),
        out_shape=(
            jax.ShapeDtypeStruct((wb, nk * blk), BF),
            jax.ShapeDtypeStruct((4, ka, wb, nchol), BF),
        ),
        in_specs=[smem] * 3 + [hbm] * 9,
        out_specs=(vmem, hbm),
        scratch_shapes=[
            pltpu.VMEM((wb, nk * blk), BF),
            pltpu.VMEM((wb, nk * z.sq), BF),
            pltpu.VMEM((blk, blk), BF),
            pltpu.VMEM((blk, blk), BF),
            pltpu.VMEM((z.nocc, z.sq, blk), BF),
            pltpu.VMEM((z.norb, blk), BF),
            pltpu.VMEM((z.wa, ROWS, z.width), BF),
            pltpu.VMEM((z.wa, ROWS, z.width), BF),
            pltpu.VMEM((nk * wb, blk), F32),
            pltpu.VMEM((nk * wb, z.sq), F32),
            pltpu.VMEM((nk, wb, blk), BF),
            pltpu.VMEM((4, nk // 2, wb, 2 * blk), BF),
            pltpu.VMEM((nk, blk, nchol), BF),
            pltpu.VMEM((4 * wb, nchol), F32),
            pltpu.VMEM((4, wb, nchol), BF),
            pltpu.VMEM((4, wb, nchol), BF),
            pltpu.VMEM((5, ka, 2, wb, nchol), BF),
            pltpu.VMEM((4, walkers, nchol), F32),
            pltpu.VMEM((4 * nchol, kcols), BF),
            pltpu.VMEM((2, nchol // 8, kcols), BF),
            pltpu.VMEM((ka, 2, wb, blk), BF),
            pltpu.VMEM((walkers, blk), F32),
            pltpu.VMEM((ka, 2, wb, blk), BF),
            pltpu.VMEM((nk, wb, blk), BF),
            pltpu.VMEM((width, lanes), F32),
            pltpu.VMEM((z.norb, z.norb, lanes), F32),
            pltpu.VMEM((2, tiles, z.nocc, z.norb, lanes), F32),
            pltpu.VMEM((tiles, z.nocc, z.norb, lanes), F32),
            dma(16), dma(z.wa), dma(z.wa), dma(2 * ka), dma(2 * ka), dma(3 * z.chunks), dma(3 * z.chunks),
            dma(events), dma(events), dma(events), dma(events), dma(events), dma(events), dma(events), dma(events),
            dma(2), dma(2), dma(2), dma(2), dma(2), dma(2), dma(3), dma(3), dma(3), dma(3), dma(3), dma(3),
            dma(4), dma(4), dma(events), dma(events), dma(2 * ka), dma(2 * ka), dma(2 * ka),
        ],
        compiler_params=pltpu.CompilerParams(
            collective_id=0, has_side_effects=True, vmem_limit_bytes=56 * 1024 * 1024
        ),
        cost_estimate=pl.CostEstimate(flops=6 * 10**9, bytes_accessed=30 * 10**6, transcendentals=0),
    )(
        send_rows.T, take_rows, pair_table, slater, inverse, perm, back, expand, tiled,
        rotated_chol, chol_vectors, aux_noise.reshape(4, ka, wb, nchol),
    )
    return moved, fields.reshape(4 * ka * wb, nchol)


def solution(mesh, z=Sizes(8, 8, 16, 48, 12, 512, 24)):
    placed = (
        P(("wa", "pb", "ka"), None),
        P(("wa", "pb", "ka"), None),
        P(("wa", "pb", "ka"), None),
        P(("wa", "pb", "ka")),
        P(),
        P("pb", "ka", None),
        P("pb", None, "ka"),
        P("wa", "pb"),
    )
    return jax.shard_map(
        functools.partial(body, z),
        mesh=mesh,
        in_specs=placed,
        out_specs=(P(("wa", "pb", "ka"), None), P("wa", "pb")),
        check_vma=False,
    )
```

```python
import functools
import math

import jax
import jax.numpy as jnp
import numpy as np
from jax import lax
from jax.experimental import pallas as pl
from jax.experimental.pallas import tpu as pltpu
from jax.sharding import PartitionSpec as P

MESH = pl.DeviceIdType.MESH
BF = jnp.bfloat16
F32 = jnp.float32
PAIR = 3
ROWS = 16
tau_coef = 2.0
force_coef = 0.5


class Sizes:
    def __init__(self, wa, ka, nk, norb, nocc, nchol, wb):
        self.wa, self.pb, self.ka, self.nk = wa, 4, ka, nk
        self.norb, self.nocc, self.nchol, self.wb = norb, nocc, nchol, wb
        self.blk = norb * nocc
        self.sq = nocc * nocc
        self.width = 4 * self.blk
        self.chunks = nk // 4
        self.half = ka // 2
        self.quarter = 2 * self.blk // 4


def dot(a, b):
    return jnp.dot(a, b, preferred_element_type=F32)


def flip(i):
    return i + 1 - 2 * (i % 2)


def remote(src, dst, send, recv, **place):
    return pltpu.make_async_remote_copy(
        src_ref=src, dst_ref=dst, send_sem=send, recv_sem=recv, device_id=place, device_id_type=MESH
    )


def ring_events(half):
    events = [(s, d) for s in range(1, half) for d in (0, 1)]
    return events + [(half, 0)]


class Ring:
    def __init__(self, size, me, core):
        self.n, self.half, self.me, self.core = size, size // 2, me, core
        self.events = ring_events(self.half)

    def index(self, event):
        return self.events.index(event)

    def block(self, event):
        s, d = event
        if s == self.half:
            return (self.me + self.half) % self.n
        return (self.me + (self.n - s if d == 0 else s)) % self.n

    def sent_block(self, event):
        s, d = event
        if s == self.half:
            back = self.half - 1
            return (self.me + self.n - back + 2 * back * self.core) % self.n
        return (self.me + (self.n - s + 1 if d == 0 else s - 1)) % self.n

    def target(self, event):
        s, d = event
        if s == self.half:
            return (self.me + 1 + (self.n - 2) * self.core) % self.n
        return (self.me + (1 if d == 0 else self.n - 1)) % self.n

    def of_step(self, s):
        return [e for e in self.events if e[0] == s]


def step_kernel(
    z, send_ref, take_ref, pair_ref, slater_hbm, inverse_hbm, perm_hbm, back_hbm, expand_hbm, tile_hbm,
    rc_ref, chol_ref, aux_ref,
    out_ref, fields_ref,
    slater, inverse, perm, back, expand, tiled, sendbuf, recv, sk, ik, sps, gall, rcf, acc, auxb, fbuf,
    fqs, fmat, chols, relay, ts, stage, moved, land, vt, vs, term, total,
    lsem, a_s, a_r, t_s, t_r, g_s, g_r, ring_s, ring_r, sib_s, sib_r, x_s, x_r, xs_s, xs_r,
    n_s, n_r, p_s, p_r, q_s, q_r, cb_s, cb_r, cx_s, cx_r, cs_s, cs_r, fy_s, fy_r, fz_s, fz_r, o_s, m_s, m_r,
):
    wa, pb, ka = lax.axis_index("wa"), lax.axis_index("pb"), lax.axis_index("ka")
    core, x = wa % 2, wa // 2
    xs = z.wa // 2
    sibling = flip(wa)
    x_to = ((x + 1 + (xs - 2) * core) % xs) * 2 + core
    base = pb - pb % 2
    par = pb % 2
    near = flip(pb)
    right, left, across = (pb + 1) % z.pb, (pb + 3) % z.pb, (pb + 2) % z.pb
    ring = Ring(z.ka, ka, core)
    wb, blk, norb, nocc, sq, nchol = z.wb, z.blk, z.norb, z.nocc, z.sq, z.nchol
    nc = z.chunks + 1
    kcols = norb * norb

    order = [0] + [r for s in range(1, z.half) for r in (s, z.ka - s)] + [z.half]
    place = {r: p for p, r in enumerate(order)}

    def y_of(e):
        return pb if e == 0 else near

    barrier = pltpu.get_barrier_semaphore()
    greeted = 0
    for d in range(1, z.wa):
        pl.semaphore_signal(barrier, inc=1, device_id={"wa": (wa + d) % z.wa}, device_id_type=MESH)
        greeted += 1
    for d in range(1, z.pb):
        pl.semaphore_signal(barrier, inc=1, device_id={"pb": (pb + d) % z.pb}, device_id_type=MESH)
        greeted += 1
    for d in range(1, z.ka):
        for e in (0, 1):
            pl.semaphore_signal(
                barrier, inc=1, device_id={"pb": y_of(e), "ka": (ka + d) % z.ka}, device_id_type=MESH
            )
            greeted += 1

    own_cols = pl.ds(pl.multiple_of(par * kcols, kcols), kcols)
    other_cols = pl.ds(pl.multiple_of((1 - par) * kcols, kcols), kcols)
    pairs = [
        (slater_hbm, slater), (inverse_hbm, inverse), (perm_hbm, perm), (tile_hbm, tiled), (expand_hbm, expand),
        (aux_ref.at[:, ka], auxb),
        (rc_ref.at[0, pl.ds(0, blk)], rcf.at[2 * ka]), (rc_ref.at[0, pl.ds(blk, blk)], rcf.at[2 * ka + 1]),
        (back_hbm, back),
        (chol_ref.at[0, :, own_cols], chols.at[pl.ds(pb * nchol, nchol)]),
    ]
    local = [pltpu.make_async_copy(src, dst, lsem.at[i]) for i, (src, dst) in enumerate(pairs)]
    for copy in local:
        copy.start()

    slot_row = lax.broadcasted_iota(jnp.int32, (z.wa * ROWS, wb), 0)
    slot_walker = lax.broadcasted_iota(jnp.int32, (z.wa * ROWS, wb), 1)
    wanted = jnp.full((z.wa * ROWS, wb), -1, jnp.int32)
    row_chunk = jnp.full((z.wa * ROWS, wb), -1, jnp.int32)
    within = slot_row % ROWS
    for j in range(PAIR):
        inside = (within >= j * nc) & (within < (j + 1) * nc)
        row_chunk = jnp.where(inside, within - j * nc, row_chunk)
        for d in range(z.wa):
            wanted = jnp.where(inside & (slot_row >= d * ROWS) & (slot_row < (d + 1) * ROWS), send_ref[j, d], wanted)
    chosen = (wanted == slot_walker).astype(F32)

    def source_chunk(c):
        if c < z.chunks:
            return slater[:, c * z.width : (c + 1) * z.width]
        return inverse[...]

    local[0].wait()
    local[1].wait()
    out = None
    for c in range(nc):
        select = jnp.where(row_chunk == c, chosen, 0.0).astype(BF)
        part = dot(select, source_chunk(c))
        out = part if out is None else out + part
    sendbuf[...] = out.astype(BF).reshape(z.wa, ROWS, z.width)
    recv[wa] = jnp.zeros((ROWS, z.width), BF)

    pl.semaphore_wait(barrier, greeted)

    a_copies = []
    for d in range(1, z.wa):
        to = (wa + d) % z.wa
        a_copies.append(remote(sendbuf.at[to], recv.at[wa], a_s.at[d], a_r.at[d], wa=to))
    for copy in a_copies:
        copy.start()

    quarter = wa % 4
    sib_quarter = flip(quarter)
    x_quarter = (quarter + 2) % 4
    sent = []

    def start(make):
        make().start()
        sent.append(make)

    piece_rows = z.quarter // 2

    def rcf_part(block, u, h):
        return rcf.at[2 * block + u // 2, pl.ds((u % 2) * z.quarter + h * piece_rows, piece_rows)]

    def ring_copy(e, h, arriving):
        i = 2 * ring.index(e) + h
        if arriving:
            here = rcf_part(ring.block(e), quarter, h)
            return remote(here, here, ring_s.at[i], ring_r.at[i], ka=ring.target(e))
        block = ring.sent_block(e)
        if e[0] == 1:
            src = rc_ref.at[0, pl.ds(quarter * z.quarter + h * piece_rows, piece_rows)]
        else:
            src = rcf_part(block, quarter, h)
        return remote(src, rcf_part(block, quarter, h), ring_s.at[i], ring_r.at[i], ka=ring.target(e))

    def part_copy(block, u, h, send, recv_sem, to):
        part = rcf_part(block, u, h)
        return remote(part, part, send, recv_sem, wa=to)

    def serve_ring(s):
        for h in range(2):
            for e in ring.of_step(s):
                ring_copy(e, h, True).wait_recv()
            if s < z.half:
                for e in ring.of_step(s + 1):
                    start(functools.partial(ring_copy, e, h, False))
            for e in ring.of_step(s):
                i, block = 2 * ring.index(e) + h, ring.block(e)
                start(functools.partial(part_copy, block, quarter, h, x_s.at[i], x_r.at[i], x_to))
                start(functools.partial(part_copy, block, quarter, h, sib_s.at[i], sib_r.at[i], sibling))

    def serve_x(s):
        for h in range(2):
            for e in ring.of_step(s):
                i, block = 2 * ring.index(e) + h, ring.block(e)
                part_copy(block, x_quarter, h, x_s.at[i], x_r.at[i], x_to).wait_recv()
                start(functools.partial(part_copy, block, x_quarter, h, xs_s.at[i], xs_r.at[i], sibling))

    def from_sibling(s):
        for h in range(2):
            for e in ring.of_step(s):
                i, block = 2 * ring.index(e) + h, ring.block(e)
                part_copy(block, sib_quarter, h, sib_s.at[i], sib_r.at[i], sibling).wait_recv()
                part_copy(block, (sib_quarter + 2) % 4, h, xs_s.at[i], xs_r.at[i], sibling).wait_recv()

    qrows = nchol // 4
    hrows = qrows // 2
    sources = (left, right, across)

    def chol_rows(q, u):
        return chols.at[pl.ds(q * nchol + u * qrows, qrows)]

    def chol_half(q, i):
        return chols.at[pl.ds(q * nchol + quarter * qrows + i * hrows, hrows)]

    def chol_first():
        for i, to in enumerate((right, left)):
            start(
                functools.partial(
                    remote,
                    chol_ref.at[0, pl.ds(quarter * qrows, qrows), other_cols],
                    chol_rows(pb, quarter), n_s.at[i], n_r.at[i], pb=to,
                )
            )

    def chol_across():
        for i, to in enumerate((right, left)):
            start(
                functools.partial(
                    remote,
                    chol_ref.at[0, pl.ds(quarter * qrows + i * hrows, hrows), own_cols],
                    relay.at[i], p_s.at[i], p_r.at[i], pb=to,
                )
            )

    def chol_relay():
        for i, (q, to) in enumerate(((left, right), (right, left))):
            remote(relay.at[i], relay.at[i], p_s.at[i], p_r.at[i], pb=to).wait_recv()
            start(functools.partial(remote, relay.at[i], chol_half(q, i), q_s.at[i], q_r.at[i], pb=to))

    def chol_share(i):
        q = sources[i]
        if i < 2:
            rows = chol_rows(q, quarter)
            remote(rows, rows, n_s.at[i], n_r.at[i], pb=right).wait_recv()
        else:
            for h in range(2):
                rows = chol_half(q, h)
                remote(rows, rows, q_s.at[h], q_r.at[h], pb=right).wait_recv()
        rows = chol_rows(q, quarter)
        start(functools.partial(remote, rows, rows, cx_s.at[i], cx_r.at[i], wa=x_to))
        start(functools.partial(remote, rows, rows, cb_s.at[i], cb_r.at[i], wa=sibling))

    def chol_pass_on(i):
        rows = chol_rows(sources[i], x_quarter)
        remote(rows, rows, cx_s.at[i], cx_r.at[i], wa=x_to).wait_recv()
        start(functools.partial(remote, rows, rows, cs_s.at[i], cs_r.at[i], wa=sibling))

    for h in range(2):
        for e in ring.of_step(1):
            start(functools.partial(ring_copy, e, h, False))
    chol_first()

    pick_row = lax.broadcasted_iota(jnp.int32, (wb, z.wa * ROWS), 0)
    pick_lane = lax.broadcasted_iota(jnp.int32, (wb, z.wa * ROWS), 1)
    taken = jnp.full((wb, z.wa * ROWS), -1, jnp.int32)
    for w in range(wb):
        taken = jnp.where(pick_row == w, take_ref[w], taken)
    lane_within = pick_lane % ROWS
    code = jnp.full((wb, z.wa * ROWS), -2, jnp.int32)
    lane_chunk = jnp.full((wb, z.wa * ROWS), -1, jnp.int32)
    for j in range(PAIR):
        inside = (lane_within >= j * nc) & (lane_within < (j + 1) * nc)
        code = jnp.where(inside, wb + PAIR * (pick_lane // ROWS) + j, code)
        lane_chunk = jnp.where(inside, lane_within - j * nc, lane_chunk)
    from_others = (taken == code).astype(F32)
    from_own = (taken == pick_lane).astype(F32)[:, :wb].astype(BF)
    for d in range(1, z.wa):
        here = recv.at[(wa + z.wa - d) % z.wa]
        remote(here, here, a_s.at[d], a_r.at[d], wa=(wa + d) % z.wa).wait_recv()
    got = recv[...].reshape(z.wa * ROWS, z.width)
    for c in range(nc):
        select = jnp.where(lane_chunk == c, from_others, 0.0).astype(BF)
        picked = dot(from_own, source_chunk(c)) + dot(select, got)
        if c < z.chunks:
            for k in range(4):
                sk[pl.ds((4 * c + k) * wb, wb), :] = picked[:, k * blk : (k + 1) * blk]
        else:
            for k in range(z.nk):
                ik[pl.ds(k * wb, wb), :] = picked[:, k * sq : (k + 1) * sq]

    serve_ring(1)

    def g_piece(y, c):
        return gall.at[y, pl.ds(2 * c, 2)]

    def g_pass_on(c):
        src, to = (left, right) if c % 2 == 0 else (right, left)
        piece = g_piece(src, c)
        remote(piece, piece, g_s.at[3 * c + c % 2], g_r.at[3 * c + c % 2], pb=to).wait_recv()
        start(functools.partial(remote, piece, piece, g_s.at[3 * c + 2], g_r.at[3 * c + 2], pb=to))

    rows = 4 * wb
    for copy in local[2:5]:
        copy.wait()
    for c in range(z.chunks):
        part = pl.ds(c * rows, rows)
        ordered = dot(sk[part, :].astype(BF), perm[...])
        for k in range(4):
            sps[4 * c + k] = ordered[k * wb : (k + 1) * wb, :].astype(BF)
        ordered = ordered.astype(BF)
        inv = ik[part, :].astype(BF)
        green = None
        for j in range(nocc):
            one = dot(inv, expand[j]) * dot(ordered[:, j * norb : (j + 1) * norb], tiled[...])
            green = one if green is None else green + one
        for k in range(2):
            both = jnp.concatenate(
                [green[2 * k * wb : (2 * k + 1) * wb], green[(2 * k + 1) * wb : (2 * k + 2) * wb]], axis=1
            )
            gall[pb, 2 * c + k] = both.astype(BF)
        for i, to in enumerate((right, left)):
            piece = g_piece(pb, c)
            start(functools.partial(remote, piece, piece, g_s.at[3 * c + i], g_r.at[3 * c + i], pb=to))
        if c == 2 and z.half > 1:
            serve_ring(2)
        if c > 0:
            g_pass_on(c - 1)

    def slot(d):
        return place[(z.ka - d) % z.ka]

    def slater_blocks():
        for d in range(z.ka):
            for e in (0, 1):
                i = 2 * d + e
                to_z, to_y = (ka + d) % z.ka, y_of(e)
                src = sps.at[2 * to_z + to_y % 2]
                dst = ts.at[slot(d), par]
                if d == 0 and e == 0:
                    own_ts = pltpu.make_async_copy(src, dst, lsem.at[10])
                    own_ts.start()
                else:
                    start(functools.partial(remote, src, dst, t_s.at[i], t_r.at[i], pb=to_y, ka=to_z))
        return own_ts

    def force_bias(s):
        def one_k(n, carry):
            block = (ka + z.ka - s + (n // 2) * (2 * s)) % z.ka
            k = 2 * block + n % 2
            other = pair_ref[pb, k]
            both = jnp.concatenate([gall[y, other // 2].astype(F32) for y in range(z.pb)], axis=0)
            odd = (other % 2).astype(F32)
            one = both[:, :blk] * (1.0 - odd) + both[:, blk:] * odd
            acc[...] += dot(one.astype(BF), rcf[k])
            return carry

        if s > 0:
            from_sibling(s)
        lax.fori_loop(0, 4 if 0 < s < z.half else 2, one_k, 0)

    g_pass_on(z.chunks - 1)
    chol_across()
    next_ring = 2 + (z.half > 1 and z.chunks > 2)
    if next_ring <= z.half:
        serve_ring(next_ring)
    serve_x(1)
    acc[...] = jnp.zeros_like(acc)
    for c in range(z.chunks):
        for i, src in ((1, right) if c % 2 == 0 else (0, left), (2, across)):
            piece = g_piece(src, c)
            remote(piece, piece, g_s.at[3 * c + i], g_r.at[3 * c + i], pb=right).wait_recv()
    for copy in local[5:8]:
        copy.wait()
    if z.half > 1:
        serve_x(2)
    force_bias(0)
    force_bias(1)
    for s in range(next_ring + 1, z.half + 1):
        serve_ring(s)
    own_ts = slater_blocks()
    for s in range(3, z.half):
        serve_x(s)
    if z.half > 2:
        force_bias(2)
        serve_x(z.half)
    chol_share(0)
    chol_share(1)
    for s in range(3, z.half):
        force_bias(s)
    chol_relay()
    if z.half > 1:
        force_bias(z.half)
    for y in range(z.pb):
        bias = acc[pl.ds(y * wb, wb), :]
        fbuf[y] = (auxb[y].astype(F32) - force_coef * bias).astype(BF)

    for d in range(1, z.pb):
        to = (pb + d) % z.pb
        start(functools.partial(
            remote, fbuf.at[pl.ds(to - to % 2, 2)], fqs.at[pb, 0], fy_s.at[d], fy_r.at[d], pb=to
        ))
    own_f = pltpu.make_async_copy(fbuf.at[pl.ds(base, 2)], fqs.at[pb, 0], lsem.at[11])
    own_f.start()
    rest_f = pltpu.make_async_copy(fbuf.at[pl.ds(2 - base, 2)], fqs.at[4, 0], lsem.at[12])
    rest_f.start()
    own_f.wait()
    rest_f.wait()
    for d in range(1, z.pb):
        here = fqs.at[(pb + z.pb - d) % z.pb, 0]
        remote(here, here, fy_s.at[d], fy_r.at[d], pb=right).wait_recv()

    def arrive_slot(e):
        return place[(z.ka - e[0]) % z.ka if e[1] == 0 else e[0]]

    def fq_copy(e, arriving):
        i = ring.index(e)
        here = fqs.at[:, arrive_slot(e)]
        if arriving:
            src = here
        elif e[0] == 1:
            src = fqs.at[:, 0]
        elif e[0] == z.half:
            one, other = place[z.ka - z.half + 1], place[z.half - 1]
            src = fqs.at[:, one + core * (other - one)]
        else:
            src = fqs.at[:, arrive_slot((e[0] - 1, e[1]))]
        return remote(src, here, fz_s.at[i], fz_r.at[i], ka=ring.target(e))

    def serve_fields(s):
        for e in ring.of_step(s):
            fq_copy(e, True).wait_recv()
        if s < z.half:
            for e in ring.of_step(s + 1):
                start(functools.partial(fq_copy, e, False))

    for e in ring.of_step(1):
        start(functools.partial(fq_copy, e, False))

    tiles, lanes = term.shape[1], vs.shape[2]
    for d in range(z.ka):
        for e in (0, 1):
            if d == 0 and e == 0:
                continue
            i = 2 * d + e
            here = ts.at[slot(d), y_of(e) % 2]
            remote(here, here, t_s.at[i], t_r.at[i], pb=y_of(e), ka=(ka + d) % z.ka).wait_recv()
    own_ts.wait()
    for p in range(z.ka):
        for h in range(2):
            stage[pl.ds((2 * p + h) * wb, wb), :] = ts[p, h].astype(F32)
    for t in range(tiles):
        first = stage[pl.ds(t * lanes, lanes), :].T.reshape(nocc, norb, lanes)
        term[0, t] = first
        total[t] = first
    chol_share(2)
    chol_pass_on(0)
    chol_pass_on(1)

    def all_of_chol():
        chol_pass_on(2)
        for i, q in enumerate(sources):
            for u, s_sem, r_sem in ((sib_quarter, cb_s, cb_r), ((sib_quarter + 2) % 4, cs_s, cs_r)):
                part = chol_rows(q, u)
                remote(part, part, s_sem.at[i], r_sem.at[i], wa=sibling).wait_recv()
        for copy in local[8:]:
            copy.wait()

    steps = max(1, norb // 8)
    ps = norb // steps
    width = ps * norb

    def potential(t):
        fields_of = [fmat[q, pl.ds(t * lanes, lanes), :].astype(BF) for q in range(4)]

        def some_rows(b, carry):
            cols = pl.ds(pl.multiple_of(b * width, width), width)
            v = dot(fields_of[0], chols[pl.ds(0, nchol), cols])
            for q in range(1, 4):
                v = v + dot(fields_of[q], chols[pl.ds(q * nchol, nchol), cols])
            vt[...] = v.T
            for p2 in range(norb):
                vs[p2, pl.ds(pl.multiple_of(b * ps, ps), ps), :] = vt[pl.ds(p2, ps, stride=norb), :]
            return carry

        lax.fori_loop(0, steps, some_rows, 0)

    step_size = tau_coef / math.sqrt(norb)
    group = 4

    def propagate(t, between):
        def one_degree(m, carry):
            scale = -step_size / m.astype(F32)
            now, later = (m + 1) % 2, m % 2

            def one_group(g, carry):
                accs = [jnp.zeros((norb, lanes), F32) for _ in range(group)]
                for p2 in range(norb):
                    column = vs[p2]
                    for a in range(group):
                        accs[a] = accs[a] + column * term[now, t, g * group + a, pl.ds(p2, 1), :]
                for a in range(group):
                    new = accs[a] * scale
                    term[later, t, g * group + a] = new
                    total[t, g * group + a] += new
                return carry

            lax.fori_loop(0, nocc // group, one_group, 0)
            return carry

        if between is None:
            lax.fori_loop(1, 7, one_degree, 0)
        else:
            lax.fori_loop(1, 5, one_degree, 0)
            between()
            lax.fori_loop(5, 7, one_degree, 0)
        final = total[t].reshape(blk, lanes).T.astype(BF)
        stage[pl.ds(t * lanes, lanes), :] = dot(final, back[...])

    k_own = 2 * ka + par
    own_m = None
    out_f = []

    def write_fields():
        for p in range(z.ka):
            block = (ka + order[p]) % z.ka
            for n, (q, first) in enumerate(((pb, base), (4, 2 - base))):
                out_f.append(
                    pltpu.make_async_copy(fqs.at[q, p], fields_ref.at[pl.ds(first, 2), block], o_s.at[2 * p + n])
                )
                out_f[-1].start()

    served, arrived, finished = 0, 0, 0

    def serve_to(s):
        nonlocal served
        while served < min(s, z.half):
            served += 1
            serve_fields(served)

    for t in range(tiles):
        last_place = -(-(t + 1) * lanes // (2 * wb)) - 1
        need = min(z.half, (last_place + 1) // 2)
        serve_to(need)
        while arrived <= last_place:
            for q in range(4):
                for h in range(2):
                    fmat[q, pl.ds((2 * arrived + h) * wb, wb), :] = fqs[q, arrived, h].astype(F32)
            arrived += 1
        if t == 0:
            all_of_chol()
        potential(t)
        if served < z.half:
            propagate(t, functools.partial(serve_to, served + 1))
        else:
            if t == tiles - 1:
                write_fields()
            propagate(t, None)
        while finished < 2 * z.ka and (finished + 1) * wb <= (t + 1) * lanes:
            p, h = finished // 2, finished % 2
            moved[p, h] = stage[pl.ds(finished * wb, wb), :].astype(BF)
            finished += 1
            if h == 0:
                continue
            r = order[p]
            to_z = (ka + r) % z.ka
            for e in (0, 1):
                to_y = y_of(e)
                src = moved.at[p, to_y % 2]
                i = 2 * r + e
                if r == 0 and e == 0:
                    own_m = pltpu.make_async_copy(src, land.at[k_own], lsem.at[13])
                    own_m.start()
                else:
                    start(functools.partial(remote, src, land.at[k_own], m_s.at[i], m_r.at[i], pb=to_y, ka=to_z))
    for r in range(z.ka):
        for e in (0, 1):
            if r == 0 and e == 0:
                continue
            i = 2 * r + e
            from_z = (ka + z.ka - r) % z.ka
            here = land.at[2 * from_z + y_of(e) % 2]
            remote(here, here, m_s.at[i], m_r.at[i], pb=y_of(e), ka=(ka + r) % z.ka).wait_recv()
    own_m.wait()
    for k in range(z.nk):
        out_ref[:, k * blk : (k + 1) * blk] = land[k]
    for copy in a_copies:
        copy.wait_send()
    for make in sent:
        make().wait_send()
    for copy in out_f:
        copy.wait()


def constants(z):
    perm = np.zeros((z.blk, z.blk), np.float32)
    for r in range(z.norb):
        for j in range(z.nocc):
            perm[r * z.nocc + j, j * z.norb + r] = 1
    expand = np.zeros((z.nocc, z.sq, z.blk), np.float32)
    tiled = np.zeros((z.norb, z.blk), np.float32)
    for i in range(z.nocc):
        for r in range(z.norb):
            tiled[r, i * z.norb + r] = 1
            for j in range(z.nocc):
                expand[j, i * z.nocc + j, i * z.norb + r] = 1
    return jnp.asarray(perm, BF), jnp.asarray(perm.T, BF), jnp.asarray(expand, BF), jnp.asarray(tiled, BF)


def body(z, slater, inverse, send_rows, take_rows, pair_table, rotated_chol, chol_vectors, aux_noise):
    wb, nk, blk, nchol, ka = z.wb, z.nk, z.blk, z.nchol, z.ka
    perm, back, expand, tiled = constants(z)
    vmem = pl.BlockSpec(memory_space=pltpu.VMEM)
    smem = pl.BlockSpec(memory_space=pltpu.SMEM)
    hbm = pl.BlockSpec(memory_space=pl.ANY)
    dma = lambda n: pltpu.SemaphoreType.DMA((n,))
    events = ka - 1
    kcols = z.norb * z.norb
    walkers = 2 * ka * wb
    lanes = min(128, walkers)
    tiles = walkers // lanes
    width = z.norb // max(1, z.norb // 8) * z.norb
    moved, fields = pl.pallas_call(
        functools.partial(step_kernel, z),
        out_shape=(
            jax.ShapeDtypeStruct((wb, nk * blk), BF),
            jax.ShapeDtypeStruct((4, ka, wb, nchol), BF),
        ),
        in_specs=[smem] * 3 + [hbm] * 9,
        out_specs=(vmem, hbm),
        scratch_shapes=[
            pltpu.VMEM((wb, nk * blk), BF),
            pltpu.VMEM((wb, nk * z.sq), BF),
            pltpu.VMEM((blk, blk), BF),
            pltpu.VMEM((blk, blk), BF),
            pltpu.VMEM((z.nocc, z.sq, blk), BF),
            pltpu.VMEM((z.norb, blk), BF),
            pltpu.VMEM((z.wa, ROWS, z.width), BF),
            pltpu.VMEM((z.wa, ROWS, z.width), BF),
            pltpu.VMEM((nk * wb, blk), F32),
            pltpu.VMEM((nk * wb, z.sq), F32),
            pltpu.VMEM((nk, wb, blk), BF),
            pltpu.VMEM((4, nk // 2, wb, 2 * blk), BF),
            pltpu.VMEM((nk, blk, nchol), BF),
            pltpu.VMEM((4 * wb, nchol), F32),
            pltpu.VMEM((4, wb, nchol), BF),
            pltpu.VMEM((4, wb, nchol), BF),
            pltpu.VMEM((5, ka, 2, wb, nchol), BF),
            pltpu.VMEM((4, walkers, nchol), F32),
            pltpu.VMEM((4 * nchol, kcols), BF),
            pltpu.VMEM((2, nchol // 8, kcols), BF),
            pltpu.VMEM((ka, 2, wb, blk), BF),
            pltpu.VMEM((walkers, blk), F32),
            pltpu.VMEM((ka, 2, wb, blk), BF),
            pltpu.VMEM((nk, wb, blk), BF),
            pltpu.VMEM((width, lanes), F32),
            pltpu.VMEM((z.norb, z.norb, lanes), F32),
            pltpu.VMEM((2, tiles, z.nocc, z.norb, lanes), F32),
            pltpu.VMEM((tiles, z.nocc, z.norb, lanes), F32),
            dma(16), dma(z.wa), dma(z.wa), dma(2 * ka), dma(2 * ka), dma(3 * z.chunks), dma(3 * z.chunks),
            dma(2 * events), dma(2 * events), dma(2 * events), dma(2 * events),
            dma(2 * events), dma(2 * events), dma(2 * events), dma(2 * events),
            dma(2), dma(2), dma(2), dma(2), dma(2), dma(2), dma(3), dma(3), dma(3), dma(3), dma(3), dma(3),
            dma(4), dma(4), dma(events), dma(events), dma(2 * ka), dma(2 * ka), dma(2 * ka),
        ],
        compiler_params=pltpu.CompilerParams(
            collective_id=0, has_side_effects=True, vmem_limit_bytes=56 * 1024 * 1024
        ),
        cost_estimate=pl.CostEstimate(flops=6 * 10**9, bytes_accessed=30 * 10**6, transcendentals=0),
    )(
        send_rows.T, take_rows, pair_table, slater, inverse, perm, back, expand, tiled,
        rotated_chol, chol_vectors, aux_noise.reshape(4, ka, wb, nchol),
    )
    return moved, fields.reshape(4 * ka * wb, nchol)


def solution(mesh, z=Sizes(8, 8, 16, 48, 12, 512, 24)):
    placed = (
        P(("wa", "pb", "ka"), None),
        P(("wa", "pb", "ka"), None),
        P(("wa", "pb", "ka"), None),
        P(("wa", "pb", "ka")),
        P(),
        P("pb", "ka", None),
        P("pb", None, "ka"),
        P("wa", "pb"),
    )
    return jax.shard_map(
        functools.partial(body, z),
        mesh=mesh,
        in_specs=placed,
        out_specs=(P(("wa", "pb", "ka"), None), P("wa", "pb")),
        check_vma=False,
    )
```

```python
import functools
import math

import jax
import jax.numpy as jnp
import numpy as np
from jax import lax
from jax.experimental import pallas as pl
from jax.experimental.pallas import tpu as pltpu
from jax.sharding import PartitionSpec as P

MESH = pl.DeviceIdType.MESH
BF = jnp.bfloat16
F32 = jnp.float32
PAIR = 3
ROWS = 16
tau_coef = 2.0
force_coef = 0.5


class Sizes:
    def __init__(self, wa, ka, nk, norb, nocc, nchol, wb):
        self.wa, self.pb, self.ka, self.nk = wa, 4, ka, nk
        self.norb, self.nocc, self.nchol, self.wb = norb, nocc, nchol, wb
        self.blk = norb * nocc
        self.sq = nocc * nocc
        self.width = 4 * self.blk
        self.chunks = nk // 4
        self.half = ka // 2
        self.quarter = 2 * self.blk // 4


def dot(a, b):
    return jnp.dot(a, b, preferred_element_type=F32)


def flip(i):
    return i + 1 - 2 * (i % 2)


def remote(src, dst, send, recv, **place):
    return pltpu.make_async_remote_copy(
        src_ref=src, dst_ref=dst, send_sem=send, recv_sem=recv, device_id=place, device_id_type=MESH
    )


def ring_events(half):
    events = [(s, d) for s in range(1, half) for d in (0, 1)]
    return events + [(half, 0)]


class Ring:
    def __init__(self, size, me, core):
        self.n, self.half, self.me, self.core = size, size // 2, me, core
        self.events = ring_events(self.half)

    def index(self, event):
        return self.events.index(event)

    def block(self, event):
        s, d = event
        if s == self.half:
            return (self.me + self.half) % self.n
        return (self.me + (self.n - s if d == 0 else s)) % self.n

    def sent_block(self, event):
        s, d = event
        if s == self.half:
            back = self.half - 1
            return (self.me + self.n - back + 2 * back * self.core) % self.n
        return (self.me + (self.n - s + 1 if d == 0 else s - 1)) % self.n

    def target(self, event):
        s, d = event
        if s == self.half:
            return (self.me + 1 + (self.n - 2) * self.core) % self.n
        return (self.me + (1 if d == 0 else self.n - 1)) % self.n

    def of_step(self, s):
        return [e for e in self.events if e[0] == s]


def step_kernel(
    z, send_ref, take_ref, pair_ref, slater_hbm, inverse_hbm, perm_hbm, back_hbm, expand_hbm, tile_hbm,
    rc_ref, chol_ref, aux_ref,
    out_ref, fields_ref,
    slater, inverse, perm, back, expand, tiled, sendbuf, recv, sk, ik, sps, gall, rcf, acc, auxb, fbuf,
    fqs, fmat, chols, relay, ts, stage, moved, land, vt, vs, term, total,
    lsem, a_s, a_r, t_s, t_r, g_s, g_r, ring_s, ring_r, sib_s, sib_r, x_s, x_r, xs_s, xs_r,
    n_s, n_r, p_s, p_r, q_s, q_r, cb_s, cb_r, cx_s, cx_r, cs_s, cs_r, fy_s, fy_r, fz_s, fz_r, o_s, fo_s, fo_r, m_s, m_r,
):
    wa, pb, ka = lax.axis_index("wa"), lax.axis_index("pb"), lax.axis_index("ka")
    core, x = wa % 2, wa // 2
    xs = z.wa // 2
    sibling = flip(wa)
    x_to = ((x + 1 + (xs - 2) * core) % xs) * 2 + core
    base = pb - pb % 2
    par = pb % 2
    near = flip(pb)
    right, left, across = (pb + 1) % z.pb, (pb + 3) % z.pb, (pb + 2) % z.pb
    ring = Ring(z.ka, ka, core)
    wb, blk, norb, nocc, sq, nchol = z.wb, z.blk, z.norb, z.nocc, z.sq, z.nchol
    nc = z.chunks + 1
    kcols = norb * norb

    order = [0] + [r for s in range(1, z.half) for r in (s, z.ka - s)] + [z.half]
    place = {r: p for p, r in enumerate(order)}

    def y_of(e):
        return pb if e == 0 else near

    barrier = pltpu.get_barrier_semaphore()
    greeted = 0
    for d in range(1, z.wa):
        pl.semaphore_signal(barrier, inc=1, device_id={"wa": (wa + d) % z.wa}, device_id_type=MESH)
        greeted += 1
    for d in range(1, z.pb):
        pl.semaphore_signal(barrier, inc=1, device_id={"pb": (pb + d) % z.pb}, device_id_type=MESH)
        greeted += 1
    for d in range(1, z.ka):
        for e in (0, 1):
            pl.semaphore_signal(
                barrier, inc=1, device_id={"pb": y_of(e), "ka": (ka + d) % z.ka}, device_id_type=MESH
            )
            greeted += 1

    own_cols = pl.ds(pl.multiple_of(par * kcols, kcols), kcols)
    other_cols = pl.ds(pl.multiple_of((1 - par) * kcols, kcols), kcols)
    pairs = [
        (slater_hbm, slater), (inverse_hbm, inverse), (perm_hbm, perm), (tile_hbm, tiled), (expand_hbm, expand),
        (aux_ref.at[:, ka], auxb),
        (rc_ref.at[0, pl.ds(0, blk)], rcf.at[2 * ka]), (rc_ref.at[0, pl.ds(blk, blk)], rcf.at[2 * ka + 1]),
        (back_hbm, back),
        (chol_ref.at[0, :, own_cols], chols.at[pl.ds(pb * nchol, nchol)]),
    ]
    local = [pltpu.make_async_copy(src, dst, lsem.at[i]) for i, (src, dst) in enumerate(pairs)]
    for copy in local:
        copy.start()

    slot_row = lax.broadcasted_iota(jnp.int32, (z.wa * ROWS, wb), 0)
    slot_walker = lax.broadcasted_iota(jnp.int32, (z.wa * ROWS, wb), 1)
    wanted = jnp.full((z.wa * ROWS, wb), -1, jnp.int32)
    row_chunk = jnp.full((z.wa * ROWS, wb), -1, jnp.int32)
    within = slot_row % ROWS
    for j in range(PAIR):
        inside = (within >= j * nc) & (within < (j + 1) * nc)
        row_chunk = jnp.where(inside, within - j * nc, row_chunk)
        for d in range(z.wa):
            wanted = jnp.where(inside & (slot_row >= d * ROWS) & (slot_row < (d + 1) * ROWS), send_ref[j, d], wanted)
    chosen = (wanted == slot_walker).astype(F32)

    def source_chunk(c):
        if c < z.chunks:
            return slater[:, c * z.width : (c + 1) * z.width]
        return inverse[...]

    local[0].wait()
    local[1].wait()
    out = None
    for c in range(nc):
        select = jnp.where(row_chunk == c, chosen, 0.0).astype(BF)
        part = dot(select, source_chunk(c))
        out = part if out is None else out + part
    sendbuf[...] = out.astype(BF).reshape(z.wa, ROWS, z.width)
    recv[wa] = jnp.zeros((ROWS, z.width), BF)

    pl.semaphore_wait(barrier, greeted)

    a_copies = []
    for d in range(1, z.wa):
        to = (wa + d) % z.wa
        a_copies.append(remote(sendbuf.at[to], recv.at[wa], a_s.at[d], a_r.at[d], wa=to))
    for copy in a_copies:
        copy.start()

    quarter = wa % 4
    sib_quarter = flip(quarter)
    x_quarter = (quarter + 2) % 4
    sent = []

    def start(make):
        make().start()
        sent.append(make)

    piece_rows = z.quarter // 2

    def rcf_part(block, u, h):
        return rcf.at[2 * block + u // 2, pl.ds((u % 2) * z.quarter + h * piece_rows, piece_rows)]

    def ring_copy(e, h, arriving):
        i = 2 * ring.index(e) + h
        if arriving:
            here = rcf_part(ring.block(e), quarter, h)
            return remote(here, here, ring_s.at[i], ring_r.at[i], ka=ring.target(e))
        block = ring.sent_block(e)
        if e[0] == 1:
            src = rc_ref.at[0, pl.ds(quarter * z.quarter + h * piece_rows, piece_rows)]
        else:
            src = rcf_part(block, quarter, h)
        return remote(src, rcf_part(block, quarter, h), ring_s.at[i], ring_r.at[i], ka=ring.target(e))

    def part_copy(block, u, h, send, recv_sem, to):
        part = rcf_part(block, u, h)
        return remote(part, part, send, recv_sem, wa=to)

    def serve_ring(s):
        for h in range(2):
            for e in ring.of_step(s):
                ring_copy(e, h, True).wait_recv()
            if s < z.half:
                for e in ring.of_step(s + 1):
                    start(functools.partial(ring_copy, e, h, False))
            for e in ring.of_step(s):
                i, block = 2 * ring.index(e) + h, ring.block(e)
                start(functools.partial(part_copy, block, quarter, h, x_s.at[i], x_r.at[i], x_to))
                start(functools.partial(part_copy, block, quarter, h, sib_s.at[i], sib_r.at[i], sibling))

    def serve_x(s):
        for h in range(2):
            for e in ring.of_step(s):
                i, block = 2 * ring.index(e) + h, ring.block(e)
                part_copy(block, x_quarter, h, x_s.at[i], x_r.at[i], x_to).wait_recv()
                start(functools.partial(part_copy, block, x_quarter, h, xs_s.at[i], xs_r.at[i], sibling))

    def from_sibling(s):
        for h in range(2):
            for e in ring.of_step(s):
                i, block = 2 * ring.index(e) + h, ring.block(e)
                part_copy(block, sib_quarter, h, sib_s.at[i], sib_r.at[i], sibling).wait_recv()
                part_copy(block, (sib_quarter + 2) % 4, h, xs_s.at[i], xs_r.at[i], sibling).wait_recv()

    qrows = nchol // 4
    hrows = qrows // 2
    sources = (left, right, across)

    def chol_rows(q, u):
        return chols.at[pl.ds(q * nchol + u * qrows, qrows)]

    def chol_half(q, i):
        return chols.at[pl.ds(q * nchol + quarter * qrows + i * hrows, hrows)]

    def chol_first():
        for i, to in enumerate((right, left)):
            start(
                functools.partial(
                    remote,
                    chol_ref.at[0, pl.ds(quarter * qrows, qrows), other_cols],
                    chol_rows(pb, quarter), n_s.at[i], n_r.at[i], pb=to,
                )
            )

    def chol_across():
        for i, to in enumerate((right, left)):
            start(
                functools.partial(
                    remote,
                    chol_ref.at[0, pl.ds(quarter * qrows + i * hrows, hrows), own_cols],
                    relay.at[i], p_s.at[i], p_r.at[i], pb=to,
                )
            )

    def chol_relay():
        for i, (q, to) in enumerate(((left, right), (right, left))):
            remote(relay.at[i], relay.at[i], p_s.at[i], p_r.at[i], pb=to).wait_recv()
            start(functools.partial(remote, relay.at[i], chol_half(q, i), q_s.at[i], q_r.at[i], pb=to))

    def chol_share(i):
        q = sources[i]
        if i < 2:
            rows = chol_rows(q, quarter)
            remote(rows, rows, n_s.at[i], n_r.at[i], pb=right).wait_recv()
        else:
            for h in range(2):
                rows = chol_half(q, h)
                remote(rows, rows, q_s.at[h], q_r.at[h], pb=right).wait_recv()
        rows = chol_rows(q, quarter)
        start(functools.partial(remote, rows, rows, cx_s.at[i], cx_r.at[i], wa=x_to))
        start(functools.partial(remote, rows, rows, cb_s.at[i], cb_r.at[i], wa=sibling))

    def chol_pass_on(i):
        rows = chol_rows(sources[i], x_quarter)
        remote(rows, rows, cx_s.at[i], cx_r.at[i], wa=x_to).wait_recv()
        start(functools.partial(remote, rows, rows, cs_s.at[i], cs_r.at[i], wa=sibling))

    for h in range(2):
        for e in ring.of_step(1):
            start(functools.partial(ring_copy, e, h, False))
    chol_first()

    pick_row = lax.broadcasted_iota(jnp.int32, (wb, z.wa * ROWS), 0)
    pick_lane = lax.broadcasted_iota(jnp.int32, (wb, z.wa * ROWS), 1)
    taken = jnp.full((wb, z.wa * ROWS), -1, jnp.int32)
    for w in range(wb):
        taken = jnp.where(pick_row == w, take_ref[w], taken)
    lane_within = pick_lane % ROWS
    code = jnp.full((wb, z.wa * ROWS), -2, jnp.int32)
    lane_chunk = jnp.full((wb, z.wa * ROWS), -1, jnp.int32)
    for j in range(PAIR):
        inside = (lane_within >= j * nc) & (lane_within < (j + 1) * nc)
        code = jnp.where(inside, wb + PAIR * (pick_lane // ROWS) + j, code)
        lane_chunk = jnp.where(inside, lane_within - j * nc, lane_chunk)
    from_others = (taken == code).astype(F32)
    from_own = (taken == pick_lane).astype(F32)[:, :wb].astype(BF)
    for d in range(1, z.wa):
        here = recv.at[(wa + z.wa - d) % z.wa]
        remote(here, here, a_s.at[d], a_r.at[d], wa=(wa + d) % z.wa).wait_recv()
    got = recv[...].reshape(z.wa * ROWS, z.width)
    for c in range(nc):
        select = jnp.where(lane_chunk == c, from_others, 0.0).astype(BF)
        picked = dot(from_own, source_chunk(c)) + dot(select, got)
        if c < z.chunks:
            for k in range(4):
                sk[pl.ds((4 * c + k) * wb, wb), :] = picked[:, k * blk : (k + 1) * blk]
        else:
            for k in range(z.nk):
                ik[pl.ds(k * wb, wb), :] = picked[:, k * sq : (k + 1) * sq]

    serve_ring(1)

    def g_piece(y, c):
        return gall.at[y, pl.ds(2 * c, 2)]

    def g_pass_on(c):
        src, to = (left, right) if c % 2 == 0 else (right, left)
        piece = g_piece(src, c)
        remote(piece, piece, g_s.at[3 * c + c % 2], g_r.at[3 * c + c % 2], pb=to).wait_recv()
        start(functools.partial(remote, piece, piece, g_s.at[3 * c + 2], g_r.at[3 * c + 2], pb=to))

    rows = 4 * wb
    for copy in local[2:5]:
        copy.wait()
    for c in range(z.chunks):
        part = pl.ds(c * rows, rows)
        ordered = dot(sk[part, :].astype(BF), perm[...])
        for k in range(4):
            sps[4 * c + k] = ordered[k * wb : (k + 1) * wb, :].astype(BF)
        ordered = ordered.astype(BF)
        inv = ik[part, :].astype(BF)
        green = None
        for j in range(nocc):
            one = dot(inv, expand[j]) * dot(ordered[:, j * norb : (j + 1) * norb], tiled[...])
            green = one if green is None else green + one
        for k in range(2):
            both = jnp.concatenate(
                [green[2 * k * wb : (2 * k + 1) * wb], green[(2 * k + 1) * wb : (2 * k + 2) * wb]], axis=1
            )
            gall[pb, 2 * c + k] = both.astype(BF)
        for i, to in enumerate((right, left)):
            piece = g_piece(pb, c)
            start(functools.partial(remote, piece, piece, g_s.at[3 * c + i], g_r.at[3 * c + i], pb=to))
        if c == 2 and z.half > 1:
            serve_ring(2)
        if c > 0:
            g_pass_on(c - 1)

    def slot(d):
        return place[(z.ka - d) % z.ka]

    def slater_blocks():
        for d in range(z.ka):
            for e in (0, 1):
                i = 2 * d + e
                to_z, to_y = (ka + d) % z.ka, y_of(e)
                src = sps.at[2 * to_z + to_y % 2]
                dst = ts.at[slot(d), par]
                if d == 0 and e == 0:
                    own_ts = pltpu.make_async_copy(src, dst, lsem.at[10])
                    own_ts.start()
                else:
                    start(functools.partial(remote, src, dst, t_s.at[i], t_r.at[i], pb=to_y, ka=to_z))
        return own_ts

    def force_bias(s):
        def one_k(n, carry):
            block = (ka + z.ka - s + (n // 2) * (2 * s)) % z.ka
            k = 2 * block + n % 2
            other = pair_ref[pb, k]
            both = jnp.concatenate([gall[y, other // 2].astype(F32) for y in range(z.pb)], axis=0)
            odd = (other % 2).astype(F32)
            one = both[:, :blk] * (1.0 - odd) + both[:, blk:] * odd
            acc[...] += dot(one.astype(BF), rcf[k])
            return carry

        if s > 0:
            from_sibling(s)
        lax.fori_loop(0, 4 if 0 < s < z.half else 2, one_k, 0)

    chol_share(0)
    chol_share(1)
    g_pass_on(z.chunks - 1)
    chol_across()
    next_ring = 2 + (z.half > 1 and z.chunks > 2)
    if next_ring <= z.half:
        serve_ring(next_ring)
    serve_x(1)
    acc[...] = jnp.zeros_like(acc)
    for c in range(z.chunks):
        for i, src in ((1, right) if c % 2 == 0 else (0, left), (2, across)):
            piece = g_piece(src, c)
            remote(piece, piece, g_s.at[3 * c + i], g_r.at[3 * c + i], pb=right).wait_recv()
    for copy in local[5:8]:
        copy.wait()
    if z.half > 1:
        serve_x(2)
    force_bias(0)
    force_bias(1)
    chol_relay()
    for s in range(next_ring + 1, z.half + 1):
        serve_ring(s)
    own_ts = slater_blocks()
    for s in range(3, z.half):
        serve_x(s)
    if z.half > 2:
        force_bias(2)
        serve_x(z.half)
    chol_pass_on(0)
    chol_pass_on(1)
    for s in range(3, z.half):
        force_bias(s)
    chol_share(2)
    if z.half > 1:
        force_bias(z.half)
    for y in range(z.pb):
        bias = acc[pl.ds(y * wb, wb), :]
        fbuf[y] = (auxb[y].astype(F32) - force_coef * bias).astype(BF)

    for d in range(1, z.pb):
        to = (pb + d) % z.pb
        start(functools.partial(
            remote, fbuf.at[pl.ds(to - to % 2, 2)], fqs.at[pb, 0], fy_s.at[d], fy_r.at[d], pb=to
        ))
    own_f = pltpu.make_async_copy(fbuf.at[pl.ds(base, 2)], fqs.at[pb, 0], lsem.at[11])
    own_f.start()
    own_f.wait()
    for d in range(1, z.pb):
        here = fqs.at[(pb + z.pb - d) % z.pb, 0]
        remote(here, here, fy_s.at[d], fy_r.at[d], pb=right).wait_recv()

    def arrive_slot(e):
        return place[(z.ka - e[0]) % z.ka if e[1] == 0 else e[0]]

    def fq_copy(e, arriving):
        i = ring.index(e)
        here = fqs.at[pl.ds(0, 4), arrive_slot(e)]
        if arriving:
            src = here
        elif e[0] == 1:
            src = fqs.at[pl.ds(0, 4), 0]
        elif e[0] == z.half:
            one, other = place[z.ka - z.half + 1], place[z.half - 1]
            src = fqs.at[pl.ds(0, 4), one + core * (other - one)]
        else:
            src = fqs.at[pl.ds(0, 4), arrive_slot((e[0] - 1, e[1]))]
        return remote(src, here, fz_s.at[i], fz_r.at[i], ka=ring.target(e))

    def serve_fields(s):
        for e in ring.of_step(s):
            fq_copy(e, True).wait_recv()
        if s < z.half:
            for e in ring.of_step(s + 1):
                start(functools.partial(fq_copy, e, False))

    for e in ring.of_step(1):
        start(functools.partial(fq_copy, e, False))

    tiles, lanes = term.shape[1], vs.shape[2]
    for d in range(z.ka):
        for e in (0, 1):
            if d == 0 and e == 0:
                continue
            i = 2 * d + e
            here = ts.at[slot(d), y_of(e) % 2]
            remote(here, here, t_s.at[i], t_r.at[i], pb=y_of(e), ka=(ka + d) % z.ka).wait_recv()
    own_ts.wait()
    for p in range(z.ka):
        for h in range(2):
            stage[pl.ds((2 * p + h) * wb, wb), :] = ts[p, h].astype(F32)
    for t in range(tiles):
        first = stage[pl.ds(t * lanes, lanes), :].T.reshape(nocc, norb, lanes)
        term[0, t] = first
        total[t] = first

    def all_of_chol():
        chol_pass_on(2)
        for i, q in enumerate(sources):
            for u, s_sem, r_sem in ((sib_quarter, cb_s, cb_r), ((sib_quarter + 2) % 4, cs_s, cs_r)):
                part = chol_rows(q, u)
                remote(part, part, s_sem.at[i], r_sem.at[i], wa=sibling).wait_recv()
        for copy in local[8:]:
            copy.wait()

    steps = max(1, norb // 8)
    ps = norb // steps
    width = ps * norb

    def potential(t):
        fields_of = [fmat[q, pl.ds(t * lanes, lanes), :].astype(BF) for q in range(4)]

        def some_rows(b, carry):
            cols = pl.ds(pl.multiple_of(b * width, width), width)
            v = dot(fields_of[0], chols[pl.ds(0, nchol), cols])
            for q in range(1, 4):
                v = v + dot(fields_of[q], chols[pl.ds(q * nchol, nchol), cols])
            vt[...] = v.T
            for p2 in range(norb):
                vs[p2, pl.ds(pl.multiple_of(b * ps, ps), ps), :] = vt[pl.ds(p2, ps, stride=norb), :]
            return carry

        lax.fori_loop(0, steps, some_rows, 0)

    step_size = tau_coef / math.sqrt(norb)
    group = 4

    def propagate(t, between):
        def one_degree(m, carry):
            scale = -step_size / m.astype(F32)
            now, later = (m + 1) % 2, m % 2

            def one_group(g, carry):
                accs = [jnp.zeros((norb, lanes), F32) for _ in range(group)]
                for p2 in range(norb):
                    column = vs[p2]
                    for a in range(group):
                        accs[a] = accs[a] + column * term[now, t, g * group + a, pl.ds(p2, 1), :]
                for a in range(group):
                    new = accs[a] * scale
                    term[later, t, g * group + a] = new
                    total[t, g * group + a] += new
                return carry

            lax.fori_loop(0, nocc // group, one_group, 0)
            return carry

        if between is None:
            lax.fori_loop(1, 7, one_degree, 0)
        else:
            lax.fori_loop(1, 4, one_degree, 0)
            between()
            lax.fori_loop(4, 7, one_degree, 0)
        final = total[t].reshape(blk, lanes).T.astype(BF)
        stage[pl.ds(t * lanes, lanes), :] = dot(final, back[...])

    k_own = 2 * ka + par
    own_m = None
    out_f = []

    def rest_copy(d):
        src = fbuf.at[pl.ds(2 - base, 2)]
        return remote(src, fqs.at[4, slot(d)], fo_s.at[d], fo_r.at[d], ka=(ka + d) % z.ka)

    def send_rest():
        rest_f = pltpu.make_async_copy(fbuf.at[pl.ds(2 - base, 2)], fqs.at[4, 0], lsem.at[12])
        rest_f.start()
        for d in range(1, z.ka):
            start(functools.partial(rest_copy, d))
        rest_f.wait()

    def write_fields():
        for d in range(1, z.ka):
            rest_copy(d).wait_recv()
        for p in range(z.ka):
            block = (ka + order[p]) % z.ka
            for n, (q, first) in enumerate(((pb, base), (4, 2 - base))):
                out_f.append(
                    pltpu.make_async_copy(fqs.at[q, p], fields_ref.at[pl.ds(first, 2), block], o_s.at[2 * p + n])
                )
                out_f[-1].start()

    served, arrived, finished = 0, 0, 0

    def serve_to(s):
        nonlocal served
        while served < min(s, z.half):
            served += 1
            serve_fields(served)

    for t in range(tiles):
        last_place = -(-(t + 1) * lanes // (2 * wb)) - 1
        need = min(z.half, (last_place + 1) // 2)
        serve_to(need)
        while arrived <= last_place:
            for q in range(4):
                for h in range(2):
                    fmat[q, pl.ds((2 * arrived + h) * wb, wb), :] = fqs[q, arrived, h].astype(F32)
            arrived += 1
        if t == 0:
            all_of_chol()
        potential(t)
        if served < z.half:
            propagate(t, functools.partial(serve_to, served + 1))
        else:
            propagate(t, write_fields if 0 < t == tiles - 1 else None)
        while finished < 2 * z.ka and (finished + 1) * wb <= (t + 1) * lanes:
            p, h = finished // 2, finished % 2
            moved[p, h] = stage[pl.ds(finished * wb, wb), :].astype(BF)
            finished += 1
            if h == 0:
                continue
            r = order[p]
            to_z = (ka + r) % z.ka
            for e in (0, 1):
                to_y = y_of(e)
                src = moved.at[p, to_y % 2]
                i = 2 * r + e
                if r == 0 and e == 0:
                    own_m = pltpu.make_async_copy(src, land.at[k_own], lsem.at[13])
                    own_m.start()
                else:
                    start(functools.partial(remote, src, land.at[k_own], m_s.at[i], m_r.at[i], pb=to_y, ka=to_z))
        if t == max(0, tiles - 2):
            serve_to(z.half)
            send_rest()
    if tiles == 1:
        write_fields()
    for r in range(z.ka):
        for e in (0, 1):
            if r == 0 and e == 0:
                continue
            i = 2 * r + e
            from_z = (ka + z.ka - r) % z.ka
            here = land.at[2 * from_z + y_of(e) % 2]
            remote(here, here, m_s.at[i], m_r.at[i], pb=y_of(e), ka=(ka + r) % z.ka).wait_recv()
    own_m.wait()
    for k in range(z.nk):
        out_ref[:, k * blk : (k + 1) * blk] = land[k]
    for copy in a_copies:
        copy.wait_send()
    for make in sent:
        make().wait_send()
    for copy in out_f:
        copy.wait()


def constants(z):
    perm = np.zeros((z.blk, z.blk), np.float32)
    for r in range(z.norb):
        for j in range(z.nocc):
            perm[r * z.nocc + j, j * z.norb + r] = 1
    expand = np.zeros((z.nocc, z.sq, z.blk), np.float32)
    tiled = np.zeros((z.norb, z.blk), np.float32)
    for i in range(z.nocc):
        for r in range(z.norb):
            tiled[r, i * z.norb + r] = 1
            for j in range(z.nocc):
                expand[j, i * z.nocc + j, i * z.norb + r] = 1
    return jnp.asarray(perm, BF), jnp.asarray(perm.T, BF), jnp.asarray(expand, BF), jnp.asarray(tiled, BF)


def body(z, slater, inverse, send_rows, take_rows, pair_table, rotated_chol, chol_vectors, aux_noise):
    wb, nk, blk, nchol, ka = z.wb, z.nk, z.blk, z.nchol, z.ka
    perm, back, expand, tiled = constants(z)
    vmem = pl.BlockSpec(memory_space=pltpu.VMEM)
    smem = pl.BlockSpec(memory_space=pltpu.SMEM)
    hbm = pl.BlockSpec(memory_space=pl.ANY)
    dma = lambda n: pltpu.SemaphoreType.DMA((n,))
    events = ka - 1
    kcols = z.norb * z.norb
    walkers = 2 * ka * wb
    lanes = min(128, walkers)
    tiles = walkers // lanes
    width = z.norb // max(1, z.norb // 8) * z.norb
    moved, fields = pl.pallas_call(
        functools.partial(step_kernel, z),
        out_shape=(
            jax.ShapeDtypeStruct((wb, nk * blk), BF),
            jax.ShapeDtypeStruct((4, ka, wb, nchol), BF),
        ),
        in_specs=[smem] * 3 + [hbm] * 9,
        out_specs=(vmem, hbm),
        scratch_shapes=[
            pltpu.VMEM((wb, nk * blk), BF),
            pltpu.VMEM((wb, nk * z.sq), BF),
            pltpu.VMEM((blk, blk), BF),
            pltpu.VMEM((blk, blk), BF),
            pltpu.VMEM((z.nocc, z.sq, blk), BF),
            pltpu.VMEM((z.norb, blk), BF),
            pltpu.VMEM((z.wa, ROWS, z.width), BF),
            pltpu.VMEM((z.wa, ROWS, z.width), BF),
            pltpu.VMEM((nk * wb, blk), F32),
            pltpu.VMEM((nk * wb, z.sq), F32),
            pltpu.VMEM((nk, wb, blk), BF),
            pltpu.VMEM((4, nk // 2, wb, 2 * blk), BF),
            pltpu.VMEM((nk, blk, nchol), BF),
            pltpu.VMEM((4 * wb, nchol), F32),
            pltpu.VMEM((4, wb, nchol), BF),
            pltpu.VMEM((4, wb, nchol), BF),
            pltpu.VMEM((5, ka, 2, wb, nchol), BF),
            pltpu.VMEM((4, walkers, nchol), F32),
            pltpu.VMEM((4 * nchol, kcols), BF),
            pltpu.VMEM((2, nchol // 8, kcols), BF),
            pltpu.VMEM((ka, 2, wb, blk), BF),
            pltpu.VMEM((walkers, blk), F32),
            pltpu.VMEM((ka, 2, wb, blk), BF),
            pltpu.VMEM((nk, wb, blk), BF),
            pltpu.VMEM((width, lanes), F32),
            pltpu.VMEM((z.norb, z.norb, lanes), F32),
            pltpu.VMEM((2, tiles, z.nocc, z.norb, lanes), F32),
            pltpu.VMEM((tiles, z.nocc, z.norb, lanes), F32),
            dma(16), dma(z.wa), dma(z.wa), dma(2 * ka), dma(2 * ka), dma(3 * z.chunks), dma(3 * z.chunks),
            dma(2 * events), dma(2 * events), dma(2 * events), dma(2 * events),
            dma(2 * events), dma(2 * events), dma(2 * events), dma(2 * events),
            dma(2), dma(2), dma(2), dma(2), dma(2), dma(2), dma(3), dma(3), dma(3), dma(3), dma(3), dma(3),
            dma(4), dma(4), dma(events), dma(events), dma(2 * ka), dma(ka), dma(ka), dma(2 * ka), dma(2 * ka),
        ],
        compiler_params=pltpu.CompilerParams(
            collective_id=0, has_side_effects=True, vmem_limit_bytes=56 * 1024 * 1024
        ),
        cost_estimate=pl.CostEstimate(flops=6 * 10**9, bytes_accessed=30 * 10**6, transcendentals=0),
    )(
        send_rows.T, take_rows, pair_table, slater, inverse, perm, back, expand, tiled,
        rotated_chol, chol_vectors, aux_noise.reshape(4, ka, wb, nchol),
    )
    return moved, fields.reshape(4 * ka * wb, nchol)


def solution(mesh, z=Sizes(8, 8, 16, 48, 12, 512, 24)):
    placed = (
        P(("wa", "pb", "ka"), None),
        P(("wa", "pb", "ka"), None),
        P(("wa", "pb", "ka"), None),
        P(("wa", "pb", "ka")),
        P(),
        P("pb", "ka", None),
        P("pb", None, "ka"),
        P("wa", "pb"),
    )
    return jax.shard_map(
        functools.partial(body, z),
        mesh=mesh,
        in_specs=placed,
        out_specs=(P(("wa", "pb", "ka"), None), P("wa", "pb")),
        check_vma=False,
    )
```

```python
import functools
import math

import jax
import jax.numpy as jnp
import numpy as np
from jax import lax
from jax.experimental import pallas as pl
from jax.experimental.pallas import tpu as pltpu
from jax.sharding import PartitionSpec as P

MESH = pl.DeviceIdType.MESH
BF = jnp.bfloat16
F32 = jnp.float32
PAIR = 3
ROWS = 16
tau_coef = 2.0
force_coef = 0.5


class Sizes:
    def __init__(self, wa, ka, nk, norb, nocc, nchol, wb):
        self.wa, self.pb, self.ka, self.nk = wa, 4, ka, nk
        self.norb, self.nocc, self.nchol, self.wb = norb, nocc, nchol, wb
        self.blk = norb * nocc
        self.sq = nocc * nocc
        self.width = 4 * self.blk
        self.chunks = nk // 4
        self.half = ka // 2
        self.quarter = 2 * self.blk // 4


def dot(a, b):
    return jnp.dot(a, b, preferred_element_type=F32)


def flip(i):
    return i + 1 - 2 * (i % 2)


def remote(src, dst, send, recv, **place):
    return pltpu.make_async_remote_copy(
        src_ref=src, dst_ref=dst, send_sem=send, recv_sem=recv, device_id=place, device_id_type=MESH
    )


def ring_events(half):
    events = [(s, d) for s in range(1, half) for d in (0, 1)]
    return events + [(half, 0)]


class Ring:
    def __init__(self, size, me, core):
        self.n, self.half, self.me, self.core = size, size // 2, me, core
        self.events = ring_events(self.half)

    def index(self, event):
        return self.events.index(event)

    def block(self, event):
        s, d = event
        if s == self.half:
            return (self.me + self.half) % self.n
        return (self.me + (self.n - s if d == 0 else s)) % self.n

    def sent_block(self, event):
        s, d = event
        if s == self.half:
            back = self.half - 1
            return (self.me + self.n - back + 2 * back * self.core) % self.n
        return (self.me + (self.n - s + 1 if d == 0 else s - 1)) % self.n

    def target(self, event):
        s, d = event
        if s == self.half:
            return (self.me + 1 + (self.n - 2) * self.core) % self.n
        return (self.me + (1 if d == 0 else self.n - 1)) % self.n

    def of_step(self, s):
        return [e for e in self.events if e[0] == s]


def step_kernel(
    z, send_ref, take_ref, pair_ref, slater_hbm, inverse_hbm, perm_hbm, back_hbm, expand_hbm, tile_hbm,
    rc_ref, chol_ref, aux_ref,
    land, fields_ref,
    slater, inverse, perm, back, expand, tiled, sendbuf, recv, sk, ik, sps, gall, rcf, acc, auxb, fbuf,
    fqs, fmat, chols, relay, ts, stage, moved, vt, vs, term, total,
    lsem, a_s, a_r, t_s, t_r, g_s, g_r, ring_s, ring_r, sib_s, sib_r, x_s, x_r, xs_s, xs_r,
    n_s, n_r, p_s, p_r, q_s, q_r, cb_s, cb_r, cx_s, cx_r, cs_s, cs_r, fy_s, fy_r, fz_s, fz_r, o_s, m_s, m_r,
):
    wa, pb, ka = lax.axis_index("wa"), lax.axis_index("pb"), lax.axis_index("ka")
    core, x = wa % 2, wa // 2
    xs = z.wa // 2
    sibling = flip(wa)
    x_to = ((x + 1 + (xs - 2) * core) % xs) * 2 + core
    base = pb - pb % 2
    par = pb % 2
    near = flip(pb)
    right, left, across = (pb + 1) % z.pb, (pb + 3) % z.pb, (pb + 2) % z.pb
    ring = Ring(z.ka, ka, core)
    wb, blk, norb, nocc, sq, nchol = z.wb, z.blk, z.norb, z.nocc, z.sq, z.nchol
    nc = z.chunks + 1
    kcols = norb * norb

    order = [0] + [r for s in range(1, z.half) for r in (s, z.ka - s)] + [z.half]
    place = {r: p for p, r in enumerate(order)}

    def y_of(e):
        return pb if e == 0 else near

    barrier = pltpu.get_barrier_semaphore()
    greeted = 0
    for d in range(1, z.wa):
        pl.semaphore_signal(barrier, inc=1, device_id={"wa": (wa + d) % z.wa}, device_id_type=MESH)
        greeted += 1
    for d in range(1, z.pb):
        pl.semaphore_signal(barrier, inc=1, device_id={"pb": (pb + d) % z.pb}, device_id_type=MESH)
        greeted += 1
    for d in range(1, z.ka):
        for e in (0, 1):
            pl.semaphore_signal(
                barrier, inc=1, device_id={"pb": y_of(e), "ka": (ka + d) % z.ka}, device_id_type=MESH
            )
            greeted += 1

    own_cols = pl.ds(pl.multiple_of(par * kcols, kcols), kcols)
    other_cols = pl.ds(pl.multiple_of((1 - par) * kcols, kcols), kcols)
    pairs = [
        (slater_hbm, slater), (inverse_hbm, inverse), (perm_hbm, perm), (tile_hbm, tiled), (expand_hbm, expand),
        (aux_ref.at[:, ka], auxb),
        (rc_ref.at[0, pl.ds(0, blk)], rcf.at[2 * ka]), (rc_ref.at[0, pl.ds(blk, blk)], rcf.at[2 * ka + 1]),
        (back_hbm, back),
        (chol_ref.at[0, :, own_cols], chols.at[pl.ds(pb * nchol, nchol)]),
    ]
    local = [pltpu.make_async_copy(src, dst, lsem.at[i]) for i, (src, dst) in enumerate(pairs)]
    for copy in local:
        copy.start()

    slot_row = lax.broadcasted_iota(jnp.int32, (z.wa * ROWS, wb), 0)
    slot_walker = lax.broadcasted_iota(jnp.int32, (z.wa * ROWS, wb), 1)
    wanted = jnp.full((z.wa * ROWS, wb), -1, jnp.int32)
    row_chunk = jnp.full((z.wa * ROWS, wb), -1, jnp.int32)
    within = slot_row % ROWS
    for j in range(PAIR):
        inside = (within >= j * nc) & (within < (j + 1) * nc)
        row_chunk = jnp.where(inside, within - j * nc, row_chunk)
        for d in range(z.wa):
            wanted = jnp.where(inside & (slot_row >= d * ROWS) & (slot_row < (d + 1) * ROWS), send_ref[j, d], wanted)
    chosen = (wanted == slot_walker).astype(F32)

    def source_chunk(c):
        if c < z.chunks:
            return slater[:, c * z.width : (c + 1) * z.width]
        return inverse[...]

    local[0].wait()
    local[1].wait()
    out = None
    for c in range(nc):
        select = jnp.where(row_chunk == c, chosen, 0.0).astype(BF)
        part = dot(select, source_chunk(c))
        out = part if out is None else out + part
    sendbuf[...] = out.astype(BF).reshape(z.wa, ROWS, z.width)
    recv[wa] = jnp.zeros((ROWS, z.width), BF)

    pl.semaphore_wait(barrier, greeted)

    a_copies = []
    for d in range(1, z.wa):
        to = (wa + d) % z.wa
        a_copies.append(remote(sendbuf.at[to], recv.at[wa], a_s.at[d], a_r.at[d], wa=to))
    for copy in a_copies:
        copy.start()

    quarter = wa % 4
    sib_quarter = flip(quarter)
    x_quarter = (quarter + 2) % 4
    sent = []

    def start(make):
        make().start()
        sent.append(make)

    piece_rows = z.quarter // 2

    def rcf_part(block, u, h):
        return rcf.at[2 * block + u // 2, pl.ds((u % 2) * z.quarter + h * piece_rows, piece_rows)]

    def ring_copy(e, h, arriving):
        i = 2 * ring.index(e) + h
        if arriving:
            here = rcf_part(ring.block(e), quarter, h)
            return remote(here, here, ring_s.at[i], ring_r.at[i], ka=ring.target(e))
        block = ring.sent_block(e)
        if e[0] == 1:
            src = rc_ref.at[0, pl.ds(quarter * z.quarter + h * piece_rows, piece_rows)]
        else:
            src = rcf_part(block, quarter, h)
        return remote(src, rcf_part(block, quarter, h), ring_s.at[i], ring_r.at[i], ka=ring.target(e))

    def part_copy(block, u, h, send, recv_sem, to):
        part = rcf_part(block, u, h)
        return remote(part, part, send, recv_sem, wa=to)

    def serve_ring(s):
        for h in range(2):
            for e in ring.of_step(s):
                ring_copy(e, h, True).wait_recv()
            if s < z.half:
                for e in ring.of_step(s + 1):
                    start(functools.partial(ring_copy, e, h, False))
            for e in ring.of_step(s):
                i, block = 2 * ring.index(e) + h, ring.block(e)
                start(functools.partial(part_copy, block, quarter, h, x_s.at[i], x_r.at[i], x_to))
                start(functools.partial(part_copy, block, quarter, h, sib_s.at[i], sib_r.at[i], sibling))

    def serve_x(s):
        for h in range(2):
            for e in ring.of_step(s):
                i, block = 2 * ring.index(e) + h, ring.block(e)
                part_copy(block, x_quarter, h, x_s.at[i], x_r.at[i], x_to).wait_recv()
                start(functools.partial(part_copy, block, x_quarter, h, xs_s.at[i], xs_r.at[i], sibling))

    def from_sibling(s):
        for h in range(2):
            for e in ring.of_step(s):
                i, block = 2 * ring.index(e) + h, ring.block(e)
                part_copy(block, sib_quarter, h, sib_s.at[i], sib_r.at[i], sibling).wait_recv()
                part_copy(block, (sib_quarter + 2) % 4, h, xs_s.at[i], xs_r.at[i], sibling).wait_recv()

    qrows = nchol // 4
    hrows = qrows // 2
    sources = (left, right, across)

    def chol_rows(q, u):
        return chols.at[pl.ds(q * nchol + u * qrows, qrows)]

    def chol_half(q, i):
        return chols.at[pl.ds(q * nchol + quarter * qrows + i * hrows, hrows)]

    def chol_first():
        for i, to in enumerate((right, left)):
            start(
                functools.partial(
                    remote,
                    chol_ref.at[0, pl.ds(quarter * qrows, qrows), other_cols],
                    chol_rows(pb, quarter), n_s.at[i], n_r.at[i], pb=to,
                )
            )

    def chol_across():
        for i, to in enumerate((right, left)):
            start(
                functools.partial(
                    remote,
                    chol_ref.at[0, pl.ds(quarter * qrows + i * hrows, hrows), own_cols],
                    relay.at[i], p_s.at[i], p_r.at[i], pb=to,
                )
            )

    def chol_relay():
        for i, (q, to) in enumerate(((left, right), (right, left))):
            remote(relay.at[i], relay.at[i], p_s.at[i], p_r.at[i], pb=to).wait_recv()
            start(functools.partial(remote, relay.at[i], chol_half(q, i), q_s.at[i], q_r.at[i], pb=to))

    def chol_share(i):
        q = sources[i]
        if i < 2:
            rows = chol_rows(q, quarter)
            remote(rows, rows, n_s.at[i], n_r.at[i], pb=right).wait_recv()
        else:
            for h in range(2):
                rows = chol_half(q, h)
                remote(rows, rows, q_s.at[h], q_r.at[h], pb=right).wait_recv()
        rows = chol_rows(q, quarter)
        start(functools.partial(remote, rows, rows, cx_s.at[i], cx_r.at[i], wa=x_to))
        start(functools.partial(remote, rows, rows, cb_s.at[i], cb_r.at[i], wa=sibling))

    def chol_pass_on(i):
        rows = chol_rows(sources[i], x_quarter)
        remote(rows, rows, cx_s.at[i], cx_r.at[i], wa=x_to).wait_recv()
        start(functools.partial(remote, rows, rows, cs_s.at[i], cs_r.at[i], wa=sibling))

    for h in range(2):
        for e in ring.of_step(1):
            start(functools.partial(ring_copy, e, h, False))
    chol_first()

    pick_row = lax.broadcasted_iota(jnp.int32, (wb, z.wa * ROWS), 0)
    pick_lane = lax.broadcasted_iota(jnp.int32, (wb, z.wa * ROWS), 1)
    taken = jnp.full((wb, z.wa * ROWS), -1, jnp.int32)
    for w in range(wb):
        taken = jnp.where(pick_row == w, take_ref[w], taken)
    lane_within = pick_lane % ROWS
    code = jnp.full((wb, z.wa * ROWS), -2, jnp.int32)
    lane_chunk = jnp.full((wb, z.wa * ROWS), -1, jnp.int32)
    for j in range(PAIR):
        inside = (lane_within >= j * nc) & (lane_within < (j + 1) * nc)
        code = jnp.where(inside, wb + PAIR * (pick_lane // ROWS) + j, code)
        lane_chunk = jnp.where(inside, lane_within - j * nc, lane_chunk)
    from_others = (taken == code).astype(F32)
    from_own = (taken == pick_lane).astype(F32)[:, :wb].astype(BF)
    for d in range(1, z.wa):
        here = recv.at[(wa + z.wa - d) % z.wa]
        remote(here, here, a_s.at[d], a_r.at[d], wa=(wa + d) % z.wa).wait_recv()
    got = recv[...].reshape(z.wa * ROWS, z.width)
    for c in range(nc):
        select = jnp.where(lane_chunk == c, from_others, 0.0).astype(BF)
        picked = dot(from_own, source_chunk(c)) + dot(select, got)
        if c < z.chunks:
            for k in range(4):
                sk[pl.ds((4 * c + k) * wb, wb), :] = picked[:, k * blk : (k + 1) * blk]
        else:
            for k in range(z.nk):
                ik[pl.ds(k * wb, wb), :] = picked[:, k * sq : (k + 1) * sq]

    serve_ring(1)

    def g_piece(y, c):
        return gall.at[y, pl.ds(2 * c, 2)]

    def g_pass_on(c):
        src, to = (left, right) if c % 2 == 0 else (right, left)
        piece = g_piece(src, c)
        remote(piece, piece, g_s.at[3 * c + c % 2], g_r.at[3 * c + c % 2], pb=to).wait_recv()
        start(functools.partial(remote, piece, piece, g_s.at[3 * c + 2], g_r.at[3 * c + 2], pb=to))

    rows = 4 * wb
    for copy in local[2:5]:
        copy.wait()
    for c in range(z.chunks):
        part = pl.ds(c * rows, rows)
        ordered = dot(sk[part, :].astype(BF), perm[...])
        for k in range(4):
            sps[4 * c + k] = ordered[k * wb : (k + 1) * wb, :].astype(BF)
        ordered = ordered.astype(BF)
        inv = ik[part, :].astype(BF)
        green = None
        for j in range(nocc):
            one = dot(inv, expand[j]) * dot(ordered[:, j * norb : (j + 1) * norb], tiled[...])
            green = one if green is None else green + one
        for k in range(2):
            both = jnp.concatenate(
                [green[2 * k * wb : (2 * k + 1) * wb], green[(2 * k + 1) * wb : (2 * k + 2) * wb]], axis=1
            )
            gall[pb, 2 * c + k] = both.astype(BF)
        for i, to in enumerate((right, left)):
            piece = g_piece(pb, c)
            start(functools.partial(remote, piece, piece, g_s.at[3 * c + i], g_r.at[3 * c + i], pb=to))
        if c == 2 and z.half > 1:
            serve_ring(2)
        if c > 0:
            g_pass_on(c - 1)

    def slot(d):
        return place[(z.ka - d) % z.ka]

    def slater_blocks():
        for d in range(z.ka):
            for e in (0, 1):
                i = 2 * d + e
                to_z, to_y = (ka + d) % z.ka, y_of(e)
                src = sps.at[2 * to_z + to_y % 2]
                dst = ts.at[slot(d), par]
                if d == 0 and e == 0:
                    own_ts = pltpu.make_async_copy(src, dst, lsem.at[10])
                    own_ts.start()
                else:
                    start(functools.partial(remote, src, dst, t_s.at[i], t_r.at[i], pb=to_y, ka=to_z))
        return own_ts

    def force_bias(s):
        def one_k(n, carry):
            block = (ka + z.ka - s + (n // 2) * (2 * s)) % z.ka
            k = 2 * block + n % 2
            other = pair_ref[pb, k]
            both = jnp.concatenate([gall[y, other // 2].astype(F32) for y in range(z.pb)], axis=0)
            odd = (other % 2).astype(F32)
            one = both[:, :blk] * (1.0 - odd) + both[:, blk:] * odd
            acc[...] += dot(one.astype(BF), rcf[k])
            return carry

        if s > 0:
            from_sibling(s)
        lax.fori_loop(0, 4 if 0 < s < z.half else 2, one_k, 0)

    g_pass_on(z.chunks - 1)
    chol_across()
    next_ring = 2 + (z.half > 1 and z.chunks > 2)
    if next_ring <= z.half:
        serve_ring(next_ring)
    serve_x(1)
    acc[...] = jnp.zeros_like(acc)
    for c in range(z.chunks):
        for i, src in ((1, right) if c % 2 == 0 else (0, left), (2, across)):
            piece = g_piece(src, c)
            remote(piece, piece, g_s.at[3 * c + i], g_r.at[3 * c + i], pb=right).wait_recv()
    for copy in local[5:8]:
        copy.wait()
    if z.half > 1:
        serve_x(2)
    force_bias(0)
    force_bias(1)
    for s in range(next_ring + 1, z.half + 1):
        serve_ring(s)
    own_ts = slater_blocks()
    for s in range(3, z.half):
        serve_x(s)
    if z.half > 2:
        force_bias(2)
        serve_x(z.half)
    chol_share(0)
    chol_share(1)
    for s in range(3, z.half):
        force_bias(s)
    chol_relay()
    if z.half > 1:
        force_bias(z.half)
    for y in range(z.pb):
        bias = acc[pl.ds(y * wb, wb), :]
        fbuf[y] = (auxb[y].astype(F32) - force_coef * bias).astype(BF)

    for d in range(1, z.pb):
        to = (pb + d) % z.pb
        start(functools.partial(
            remote, fbuf.at[pl.ds(to - to % 2, 2)], fqs.at[pb, 0], fy_s.at[d], fy_r.at[d], pb=to
        ))
    own_f = pltpu.make_async_copy(fbuf.at[pl.ds(base, 2)], fqs.at[pb, 0], lsem.at[11])
    own_f.start()
    rest_f = pltpu.make_async_copy(fbuf.at[pl.ds(2 - base, 2)], fqs.at[4, 0], lsem.at[12])
    rest_f.start()
    own_f.wait()
    rest_f.wait()
    for d in range(1, z.pb):
        here = fqs.at[(pb + z.pb - d) % z.pb, 0]
        remote(here, here, fy_s.at[d], fy_r.at[d], pb=right).wait_recv()

    def arrive_slot(e):
        return place[(z.ka - e[0]) % z.ka if e[1] == 0 else e[0]]

    def fq_copy(e, arriving):
        i = ring.index(e)
        here = fqs.at[:, arrive_slot(e)]
        if arriving:
            src = here
        elif e[0] == 1:
            src = fqs.at[:, 0]
        elif e[0] == z.half:
            one, other = place[z.ka - z.half + 1], place[z.half - 1]
            src = fqs.at[:, one + core * (other - one)]
        else:
            src = fqs.at[:, arrive_slot((e[0] - 1, e[1]))]
        return remote(src, here, fz_s.at[i], fz_r.at[i], ka=ring.target(e))

    def serve_fields(s):
        for e in ring.of_step(s):
            fq_copy(e, True).wait_recv()
        if s < z.half:
            for e in ring.of_step(s + 1):
                start(functools.partial(fq_copy, e, False))

    for e in ring.of_step(1):
        start(functools.partial(fq_copy, e, False))

    tiles, lanes = term.shape[1], vs.shape[2]
    for d in range(z.ka):
        for e in (0, 1):
            if d == 0 and e == 0:
                continue
            i = 2 * d + e
            here = ts.at[slot(d), y_of(e) % 2]
            remote(here, here, t_s.at[i], t_r.at[i], pb=y_of(e), ka=(ka + d) % z.ka).wait_recv()
    own_ts.wait()
    for p in range(z.ka):
        for h in range(2):
            stage[pl.ds((2 * p + h) * wb, wb), :] = ts[p, h].astype(F32)
    for t in range(tiles):
        first = stage[pl.ds(t * lanes, lanes), :].T.reshape(nocc, norb, lanes)
        term[0, t] = first
        total[t] = first
    chol_share(2)
    chol_pass_on(0)
    chol_pass_on(1)

    def all_of_chol():
        chol_pass_on(2)
        for i, q in enumerate(sources):
            for u, s_sem, r_sem in ((sib_quarter, cb_s, cb_r), ((sib_quarter + 2) % 4, cs_s, cs_r)):
                part = chol_rows(q, u)
                remote(part, part, s_sem.at[i], r_sem.at[i], wa=sibling).wait_recv()
        for copy in local[8:]:
            copy.wait()

    steps = max(1, norb // 8)
    ps = norb // steps
    width = ps * norb

    def potential(t):
        fields_of = [fmat[q, pl.ds(t * lanes, lanes), :].astype(BF) for q in range(4)]

        def some_rows(b, carry):
            cols = pl.ds(pl.multiple_of(b * width, width), width)
            v = dot(fields_of[0], chols[pl.ds(0, nchol), cols])
            for q in range(1, 4):
                v = v + dot(fields_of[q], chols[pl.ds(q * nchol, nchol), cols])
            vt[...] = v.T
            for p2 in range(norb):
                vs[p2, pl.ds(pl.multiple_of(b * ps, ps), ps), :] = vt[pl.ds(p2, ps, stride=norb), :]
            return carry

        lax.fori_loop(0, steps, some_rows, 0)

    step_size = tau_coef / math.sqrt(norb)
    group = 4

    def propagate(t, between):
        def one_degree(m, carry):
            scale = -step_size / m.astype(F32)
            now, later = (m + 1) % 2, m % 2

            def one_group(g, carry):
                accs = [jnp.zeros((norb, lanes), F32) for _ in range(group)]
                for p2 in range(norb):
                    column = vs[p2]
                    for a in range(group):
                        accs[a] = accs[a] + column * term[now, t, g * group + a, pl.ds(p2, 1), :]
                for a in range(group):
                    new = accs[a] * scale
                    term[later, t, g * group + a] = new
                    total[t, g * group + a] += new
                return carry

            lax.fori_loop(0, nocc // group, one_group, 0)
            return carry

        if between is None:
            lax.fori_loop(1, 7, one_degree, 0)
        else:
            lax.fori_loop(1, 5, one_degree, 0)
            between()
            lax.fori_loop(5, 7, one_degree, 0)
        final = total[t].reshape(blk, lanes).T.astype(BF)
        stage[pl.ds(t * lanes, lanes), :] = dot(final, back[...])

    k_own = 2 * ka + par
    own_m = None
    out_f = []

    def write_fields():
        for p in range(z.ka):
            block = (ka + order[p]) % z.ka
            for n, (q, first) in enumerate(((pb, base), (4, 2 - base))):
                out_f.append(
                    pltpu.make_async_copy(fqs.at[q, p], fields_ref.at[pl.ds(first, 2), block], o_s.at[2 * p + n])
                )
                out_f[-1].start()

    served, arrived, finished = 0, 0, 0

    def serve_to(s):
        nonlocal served
        while served < min(s, z.half):
            served += 1
            serve_fields(served)

    for t in range(tiles):
        last_place = -(-(t + 1) * lanes // (2 * wb)) - 1
        need = min(z.half, (last_place + 1) // 2)
        serve_to(need)
        while arrived <= last_place:
            for q in range(4):
                for h in range(2):
                    fmat[q, pl.ds((2 * arrived + h) * wb, wb), :] = fqs[q, arrived, h].astype(F32)
            arrived += 1
        if t == 0:
            all_of_chol()
        potential(t)
        if served < z.half:
            propagate(t, functools.partial(serve_to, served + 1))
        else:
            if t == tiles - 1:
                write_fields()
            propagate(t, None)
        while finished < 2 * z.ka and (finished + 1) * wb <= (t + 1) * lanes:
            p, h = finished // 2, finished % 2
            moved[p, h] = stage[pl.ds(finished * wb, wb), :].astype(BF)
            finished += 1
            if h == 0:
                continue
            r = order[p]
            to_z = (ka + r) % z.ka
            for e in (0, 1):
                to_y = y_of(e)
                src = moved.at[p, to_y % 2]
                i = 2 * r + e
                if r == 0 and e == 0:
                    own_m = pltpu.make_async_copy(src, land.at[k_own], lsem.at[13])
                    own_m.start()
                else:
                    start(functools.partial(remote, src, land.at[k_own], m_s.at[i], m_r.at[i], pb=to_y, ka=to_z))
    for r in range(z.ka):
        for e in (0, 1):
            if r == 0 and e == 0:
                continue
            i = 2 * r + e
            from_z = (ka + z.ka - r) % z.ka
            here = land.at[2 * from_z + y_of(e) % 2]
            remote(here, here, m_s.at[i], m_r.at[i], pb=y_of(e), ka=(ka + r) % z.ka).wait_recv()
    own_m.wait()
    for copy in a_copies:
        copy.wait_send()
    for make in sent:
        make().wait_send()
    for copy in out_f:
        copy.wait()


def outputs_kernel(z, blocks_hbm, fields_hbm, out_hbm, fields_out_hbm, blocks, fields, out, sems):
    in_b = pltpu.make_async_copy(blocks_hbm, blocks, sems.at[0])
    in_f = pltpu.make_async_copy(fields_hbm, fields, sems.at[1])
    out_b = pltpu.make_async_copy(out, out_hbm, sems.at[2])
    out_f = pltpu.make_async_copy(fields, fields_out_hbm, sems.at[3])
    in_b.start()
    in_f.start()
    in_b.wait()
    for k in range(z.nk):
        out[:, k * z.blk : (k + 1) * z.blk] = blocks[k]
    out_b.start()
    in_f.wait()
    out_f.start()
    out_b.wait()
    out_f.wait()


def constants(z):
    perm = np.zeros((z.blk, z.blk), np.float32)
    for r in range(z.norb):
        for j in range(z.nocc):
            perm[r * z.nocc + j, j * z.norb + r] = 1
    expand = np.zeros((z.nocc, z.sq, z.blk), np.float32)
    tiled = np.zeros((z.norb, z.blk), np.float32)
    for i in range(z.nocc):
        for r in range(z.norb):
            tiled[r, i * z.norb + r] = 1
            for j in range(z.nocc):
                expand[j, i * z.nocc + j, i * z.norb + r] = 1
    return jnp.asarray(perm, BF), jnp.asarray(perm.T, BF), jnp.asarray(expand, BF), jnp.asarray(tiled, BF)


def body(z, slater, inverse, send_rows, take_rows, pair_table, rotated_chol, chol_vectors, aux_noise):
    wb, nk, blk, nchol, ka = z.wb, z.nk, z.blk, z.nchol, z.ka
    perm, back, expand, tiled = constants(z)
    smem = pl.BlockSpec(memory_space=pltpu.SMEM)
    hbm = pl.BlockSpec(memory_space=pl.ANY)
    dma = lambda n: pltpu.SemaphoreType.DMA((n,))
    events = ka - 1
    kcols = z.norb * z.norb
    walkers = 2 * ka * wb
    lanes = min(128, walkers)
    tiles = walkers // lanes
    width = z.norb // max(1, z.norb // 8) * z.norb
    blocks, fields = pl.pallas_call(
        functools.partial(step_kernel, z),
        out_shape=(
            jax.ShapeDtypeStruct((nk, wb, blk), BF),
            jax.ShapeDtypeStruct((4, ka, wb, nchol), BF),
        ),
        in_specs=[smem] * 3 + [hbm] * 9,
        out_specs=(hbm, hbm),
        scratch_shapes=[
            pltpu.VMEM((wb, nk * blk), BF),
            pltpu.VMEM((wb, nk * z.sq), BF),
            pltpu.VMEM((blk, blk), BF),
            pltpu.VMEM((blk, blk), BF),
            pltpu.VMEM((z.nocc, z.sq, blk), BF),
            pltpu.VMEM((z.norb, blk), BF),
            pltpu.VMEM((z.wa, ROWS, z.width), BF),
            pltpu.VMEM((z.wa, ROWS, z.width), BF),
            pltpu.VMEM((nk * wb, blk), F32),
            pltpu.VMEM((nk * wb, z.sq), F32),
            pltpu.VMEM((nk, wb, blk), BF),
            pltpu.VMEM((4, nk // 2, wb, 2 * blk), BF),
            pltpu.VMEM((nk, blk, nchol), BF),
            pltpu.VMEM((4 * wb, nchol), F32),
            pltpu.VMEM((4, wb, nchol), BF),
            pltpu.VMEM((4, wb, nchol), BF),
            pltpu.VMEM((5, ka, 2, wb, nchol), BF),
            pltpu.VMEM((4, walkers, nchol), F32),
            pltpu.VMEM((4 * nchol, kcols), BF),
            pltpu.VMEM((2, nchol // 8, kcols), BF),
            pltpu.VMEM((ka, 2, wb, blk), BF),
            pltpu.VMEM((walkers, blk), F32),
            pltpu.VMEM((ka, 2, wb, blk), BF),
            pltpu.VMEM((width, lanes), F32),
            pltpu.VMEM((z.norb, z.norb, lanes), F32),
            pltpu.VMEM((2, tiles, z.nocc, z.norb, lanes), F32),
            pltpu.VMEM((tiles, z.nocc, z.norb, lanes), F32),
            dma(16), dma(z.wa), dma(z.wa), dma(2 * ka), dma(2 * ka), dma(3 * z.chunks), dma(3 * z.chunks),
            dma(2 * events), dma(2 * events), dma(2 * events), dma(2 * events),
            dma(2 * events), dma(2 * events), dma(2 * events), dma(2 * events),
            dma(2), dma(2), dma(2), dma(2), dma(2), dma(2), dma(3), dma(3), dma(3), dma(3), dma(3), dma(3),
            dma(4), dma(4), dma(events), dma(events), dma(2 * ka), dma(2 * ka), dma(2 * ka),
        ],
        compiler_params=pltpu.CompilerParams(
            collective_id=0, has_side_effects=True, vmem_limit_bytes=56 * 1024 * 1024
        ),
        cost_estimate=pl.CostEstimate(flops=6 * 10**9, bytes_accessed=30 * 10**6, transcendentals=0),
    )(
        send_rows.T, take_rows, pair_table, slater, inverse, perm, back, expand, tiled,
        rotated_chol, chol_vectors, aux_noise.reshape(4, ka, wb, nchol),
    )
    moved, fields = pl.pallas_call(
        functools.partial(outputs_kernel, z),
        out_shape=(
            jax.ShapeDtypeStruct((wb, nk * blk), BF),
            jax.ShapeDtypeStruct((4, ka, wb, nchol), BF),
        ),
        in_specs=[hbm] * 2,
        out_specs=(hbm, hbm),
        scratch_shapes=[
            pltpu.VMEM((nk, wb, blk), BF),
            pltpu.VMEM((4, ka, wb, nchol), BF),
            pltpu.VMEM((wb, nk * blk), BF),
            dma(4),
        ],
        compiler_params=pltpu.CompilerParams(vmem_limit_bytes=56 * 1024 * 1024),
    )(blocks, fields)
    return moved, fields.reshape(4 * ka * wb, nchol)


def solution(mesh, z=Sizes(8, 8, 16, 48, 12, 512, 24)):
    placed = (
        P(("wa", "pb", "ka"), None),
        P(("wa", "pb", "ka"), None),
        P(("wa", "pb", "ka"), None),
        P(("wa", "pb", "ka")),
        P(),
        P("pb", "ka", None),
        P("pb", None, "ka"),
        P("wa", "pb"),
    )
    return jax.shard_map(
        functools.partial(body, z),
        mesh=mesh,
        in_specs=placed,
        out_specs=(P(("wa", "pb", "ka"), None), P("wa", "pb")),
        check_vma=False,
    )
```

```python
import functools
import math

import jax
import jax.numpy as jnp
import numpy as np
from jax import lax
from jax.experimental import pallas as pl
from jax.experimental.pallas import tpu as pltpu
from jax.sharding import PartitionSpec as P

MESH = pl.DeviceIdType.MESH
BF = jnp.bfloat16
F32 = jnp.float32
PAIR = 3
ROWS = 16
tau_coef = 2.0
force_coef = 0.5


class Sizes:
    def __init__(self, wa, ka, nk, norb, nocc, nchol, wb):
        self.wa, self.pb, self.ka, self.nk = wa, 4, ka, nk
        self.norb, self.nocc, self.nchol, self.wb = norb, nocc, nchol, wb
        self.blk = norb * nocc
        self.sq = nocc * nocc
        self.width = 4 * self.blk
        self.chunks = nk // 4
        self.half = ka // 2
        self.quarter = 2 * self.blk // 4


def dot(a, b):
    return jnp.dot(a, b, preferred_element_type=F32)


def flip(i):
    return i + 1 - 2 * (i % 2)


def remote(src, dst, send, recv, **place):
    return pltpu.make_async_remote_copy(
        src_ref=src, dst_ref=dst, send_sem=send, recv_sem=recv, device_id=place, device_id_type=MESH
    )


def ring_events(half):
    events = [(s, d) for s in range(1, half) for d in (0, 1)]
    return events + [(half, 0)]


class Ring:
    def __init__(self, size, me, core):
        self.n, self.half, self.me, self.core = size, size // 2, me, core
        self.events = ring_events(self.half)

    def index(self, event):
        return self.events.index(event)

    def block(self, event):
        s, d = event
        if s == self.half:
            return (self.me + self.half) % self.n
        return (self.me + (self.n - s if d == 0 else s)) % self.n

    def sent_block(self, event):
        s, d = event
        if s == self.half:
            back = self.half - 1
            return (self.me + self.n - back + 2 * back * self.core) % self.n
        return (self.me + (self.n - s + 1 if d == 0 else s - 1)) % self.n

    def target(self, event):
        s, d = event
        if s == self.half:
            return (self.me + 1 + (self.n - 2) * self.core) % self.n
        return (self.me + (1 if d == 0 else self.n - 1)) % self.n

    def of_step(self, s):
        return [e for e in self.events if e[0] == s]


def step_kernel(
    z, send_ref, take_ref, pair_ref, slater_hbm, inverse_hbm, perm_hbm, back_hbm, expand_hbm, tile_hbm,
    rc_ref, chol_ref, aux_ref,
    land, fields_ref,
    slater, inverse, perm, back, expand, tiled, sendbuf, recv, sk, ik, sps, gall, rcf, acc, auxb, fbuf,
    fqs, fmat, chols, relay, ts, stage, moved, vt, vs, term, total,
    lsem, a_s, a_r, t_s, t_r, g_s, g_r, ring_s, ring_r, sib_s, sib_r, x_s, x_r, xs_s, xs_r,
    n_s, n_r, p_s, p_r, q_s, q_r, cb_s, cb_r, cx_s, cx_r, cs_s, cs_r, fy_s, fy_r, fz_s, fz_r, o_s, m_s, m_r,
):
    wa, pb, ka = lax.axis_index("wa"), lax.axis_index("pb"), lax.axis_index("ka")
    core, x = wa % 2, wa // 2
    xs = z.wa // 2
    sibling = flip(wa)
    x_to = ((x + 1 + (xs - 2) * core) % xs) * 2 + core
    base = pb - pb % 2
    par = pb % 2
    near = flip(pb)
    right, left, across = (pb + 1) % z.pb, (pb + 3) % z.pb, (pb + 2) % z.pb
    ring = Ring(z.ka, ka, core)
    wb, blk, norb, nocc, sq, nchol = z.wb, z.blk, z.norb, z.nocc, z.sq, z.nchol
    nc = z.chunks + 1
    kcols = norb * norb

    order = [0] + [r for s in range(1, z.half) for r in (s, z.ka - s)] + [z.half]
    place = {r: p for p, r in enumerate(order)}

    def y_of(e):
        return pb if e == 0 else near

    barrier = pltpu.get_barrier_semaphore()
    greeted = 0
    for d in range(1, z.wa):
        pl.semaphore_signal(barrier, inc=1, device_id={"wa": (wa + d) % z.wa}, device_id_type=MESH)
        greeted += 1
    for d in range(1, z.pb):
        pl.semaphore_signal(barrier, inc=1, device_id={"pb": (pb + d) % z.pb}, device_id_type=MESH)
        greeted += 1
    for d in range(1, z.ka):
        for e in (0, 1):
            pl.semaphore_signal(
                barrier, inc=1, device_id={"pb": y_of(e), "ka": (ka + d) % z.ka}, device_id_type=MESH
            )
            greeted += 1

    own_cols = pl.ds(pl.multiple_of(par * kcols, kcols), kcols)
    other_cols = pl.ds(pl.multiple_of((1 - par) * kcols, kcols), kcols)
    pairs = [
        (slater_hbm, slater), (inverse_hbm, inverse), (perm_hbm, perm), (tile_hbm, tiled), (expand_hbm, expand),
        (aux_ref.at[:, ka], auxb),
        (rc_ref.at[0, pl.ds(0, blk)], rcf.at[2 * ka]), (rc_ref.at[0, pl.ds(blk, blk)], rcf.at[2 * ka + 1]),
        (back_hbm, back),
        (chol_ref.at[0, :, own_cols], chols.at[pl.ds(pb * nchol, nchol)]),
    ]
    local = [pltpu.make_async_copy(src, dst, lsem.at[i]) for i, (src, dst) in enumerate(pairs)]
    for copy in local:
        copy.start()

    slot_row = lax.broadcasted_iota(jnp.int32, (z.wa * ROWS, wb), 0)
    slot_walker = lax.broadcasted_iota(jnp.int32, (z.wa * ROWS, wb), 1)
    wanted = jnp.full((z.wa * ROWS, wb), -1, jnp.int32)
    row_chunk = jnp.full((z.wa * ROWS, wb), -1, jnp.int32)
    within = slot_row % ROWS
    for j in range(PAIR):
        inside = (within >= j * nc) & (within < (j + 1) * nc)
        row_chunk = jnp.where(inside, within - j * nc, row_chunk)
        for d in range(z.wa):
            wanted = jnp.where(inside & (slot_row >= d * ROWS) & (slot_row < (d + 1) * ROWS), send_ref[j, d], wanted)
    chosen = (wanted == slot_walker).astype(F32)

    def source_chunk(c):
        if c < z.chunks:
            return slater[:, c * z.width : (c + 1) * z.width]
        return inverse[...]

    local[0].wait()
    local[1].wait()
    out = None
    for c in range(nc):
        select = jnp.where(row_chunk == c, chosen, 0.0).astype(BF)
        part = dot(select, source_chunk(c))
        out = part if out is None else out + part
    sendbuf[...] = out.astype(BF).reshape(z.wa, ROWS, z.width)
    recv[wa] = jnp.zeros((ROWS, z.width), BF)

    pl.semaphore_wait(barrier, greeted)

    a_copies = []
    for d in range(1, z.wa):
        to = (wa + d) % z.wa
        a_copies.append(remote(sendbuf.at[to], recv.at[wa], a_s.at[d], a_r.at[d], wa=to))
    for copy in a_copies:
        copy.start()

    quarter = wa % 4
    sib_quarter = flip(quarter)
    x_quarter = (quarter + 2) % 4
    sent = []

    def start(make):
        make().start()
        sent.append(make)

    piece_rows = z.quarter // 2

    def rcf_part(block, u, h):
        return rcf.at[2 * block + u // 2, pl.ds((u % 2) * z.quarter + h * piece_rows, piece_rows)]

    def ring_copy(e, h, arriving):
        i = 2 * ring.index(e) + h
        if arriving:
            here = rcf_part(ring.block(e), quarter, h)
            return remote(here, here, ring_s.at[i], ring_r.at[i], ka=ring.target(e))
        block = ring.sent_block(e)
        if e[0] == 1:
            src = rc_ref.at[0, pl.ds(quarter * z.quarter + h * piece_rows, piece_rows)]
        else:
            src = rcf_part(block, quarter, h)
        return remote(src, rcf_part(block, quarter, h), ring_s.at[i], ring_r.at[i], ka=ring.target(e))

    def part_copy(block, u, h, send, recv_sem, to):
        part = rcf_part(block, u, h)
        return remote(part, part, send, recv_sem, wa=to)

    def serve_ring(s):
        for h in range(2):
            for e in ring.of_step(s):
                ring_copy(e, h, True).wait_recv()
            if s < z.half:
                for e in ring.of_step(s + 1):
                    start(functools.partial(ring_copy, e, h, False))
            for e in ring.of_step(s):
                i, block = 2 * ring.index(e) + h, ring.block(e)
                start(functools.partial(part_copy, block, quarter, h, x_s.at[i], x_r.at[i], x_to))
                start(functools.partial(part_copy, block, quarter, h, sib_s.at[i], sib_r.at[i], sibling))

    def serve_x(s):
        for h in range(2):
            for e in ring.of_step(s):
                i, block = 2 * ring.index(e) + h, ring.block(e)
                part_copy(block, x_quarter, h, x_s.at[i], x_r.at[i], x_to).wait_recv()
                start(functools.partial(part_copy, block, x_quarter, h, xs_s.at[i], xs_r.at[i], sibling))

    def from_sibling(s):
        for h in range(2):
            for e in ring.of_step(s):
                i, block = 2 * ring.index(e) + h, ring.block(e)
                part_copy(block, sib_quarter, h, sib_s.at[i], sib_r.at[i], sibling).wait_recv()
                part_copy(block, (sib_quarter + 2) % 4, h, xs_s.at[i], xs_r.at[i], sibling).wait_recv()

    qrows = nchol // 4
    hrows = qrows // 2
    sources = (left, right, across)

    def chol_rows(q, u):
        return chols.at[pl.ds(q * nchol + u * qrows, qrows)]

    def chol_half(q, i):
        return chols.at[pl.ds(q * nchol + quarter * qrows + i * hrows, hrows)]

    def chol_first():
        for i, to in enumerate((right, left)):
            start(
                functools.partial(
                    remote,
                    chol_ref.at[0, pl.ds(quarter * qrows, qrows), other_cols],
                    chol_rows(pb, quarter), n_s.at[i], n_r.at[i], pb=to,
                )
            )

    def chol_across():
        for i, to in enumerate((right, left)):
            start(
                functools.partial(
                    remote,
                    chol_ref.at[0, pl.ds(quarter * qrows + i * hrows, hrows), own_cols],
                    relay.at[i], p_s.at[i], p_r.at[i], pb=to,
                )
            )

    def chol_relay():
        for i, (q, to) in enumerate(((left, right), (right, left))):
            remote(relay.at[i], relay.at[i], p_s.at[i], p_r.at[i], pb=to).wait_recv()
            start(functools.partial(remote, relay.at[i], chol_half(q, i), q_s.at[i], q_r.at[i], pb=to))

    def chol_share(i):
        q = sources[i]
        if i < 2:
            rows = chol_rows(q, quarter)
            remote(rows, rows, n_s.at[i], n_r.at[i], pb=right).wait_recv()
        else:
            for h in range(2):
                rows = chol_half(q, h)
                remote(rows, rows, q_s.at[h], q_r.at[h], pb=right).wait_recv()
        rows = chol_rows(q, quarter)
        start(functools.partial(remote, rows, rows, cx_s.at[i], cx_r.at[i], wa=x_to))
        start(functools.partial(remote, rows, rows, cb_s.at[i], cb_r.at[i], wa=sibling))

    def chol_pass_on(i):
        rows = chol_rows(sources[i], x_quarter)
        remote(rows, rows, cx_s.at[i], cx_r.at[i], wa=x_to).wait_recv()
        start(functools.partial(remote, rows, rows, cs_s.at[i], cs_r.at[i], wa=sibling))

    for h in range(2):
        for e in ring.of_step(1):
            start(functools.partial(ring_copy, e, h, False))
    chol_first()

    pick_row = lax.broadcasted_iota(jnp.int32, (wb, z.wa * ROWS), 0)
    pick_lane = lax.broadcasted_iota(jnp.int32, (wb, z.wa * ROWS), 1)
    taken = jnp.full((wb, z.wa * ROWS), -1, jnp.int32)
    for w in range(wb):
        taken = jnp.where(pick_row == w, take_ref[w], taken)
    lane_within = pick_lane % ROWS
    code = jnp.full((wb, z.wa * ROWS), -2, jnp.int32)
    lane_chunk = jnp.full((wb, z.wa * ROWS), -1, jnp.int32)
    for j in range(PAIR):
        inside = (lane_within >= j * nc) & (lane_within < (j + 1) * nc)
        code = jnp.where(inside, wb + PAIR * (pick_lane // ROWS) + j, code)
        lane_chunk = jnp.where(inside, lane_within - j * nc, lane_chunk)
    from_others = (taken == code).astype(F32)
    from_own = (taken == pick_lane).astype(F32)[:, :wb].astype(BF)
    for d in range(1, z.wa):
        here = recv.at[(wa + z.wa - d) % z.wa]
        remote(here, here, a_s.at[d], a_r.at[d], wa=(wa + d) % z.wa).wait_recv()
    got = recv[...].reshape(z.wa * ROWS, z.width)
    for c in range(nc):
        select = jnp.where(lane_chunk == c, from_others, 0.0).astype(BF)
        picked = dot(from_own, source_chunk(c)) + dot(select, got)
        if c < z.chunks:
            for k in range(4):
                sk[pl.ds((4 * c + k) * wb, wb), :] = picked[:, k * blk : (k + 1) * blk]
        else:
            for k in range(z.nk):
                ik[pl.ds(k * wb, wb), :] = picked[:, k * sq : (k + 1) * sq]

    serve_ring(1)

    def g_piece(y, c):
        return gall.at[y, pl.ds(2 * c, 2)]

    def g_pass_on(c):
        src, to = (left, right) if c % 2 == 0 else (right, left)
        piece = g_piece(src, c)
        remote(piece, piece, g_s.at[3 * c + c % 2], g_r.at[3 * c + c % 2], pb=to).wait_recv()
        start(functools.partial(remote, piece, piece, g_s.at[3 * c + 2], g_r.at[3 * c + 2], pb=to))

    rows = 4 * wb
    for copy in local[2:5]:
        copy.wait()
    for c in range(z.chunks):
        part = pl.ds(c * rows, rows)
        ordered = dot(sk[part, :].astype(BF), perm[...])
        for k in range(4):
            sps[4 * c + k] = ordered[k * wb : (k + 1) * wb, :].astype(BF)
        ordered = ordered.astype(BF)
        inv = ik[part, :].astype(BF)
        green = None
        for j in range(nocc):
            one = dot(inv, expand[j]) * dot(ordered[:, j * norb : (j + 1) * norb], tiled[...])
            green = one if green is None else green + one
        for k in range(2):
            both = jnp.concatenate(
                [green[2 * k * wb : (2 * k + 1) * wb], green[(2 * k + 1) * wb : (2 * k + 2) * wb]], axis=1
            )
            gall[pb, 2 * c + k] = both.astype(BF)
        for i, to in enumerate((right, left)):
            piece = g_piece(pb, c)
            start(functools.partial(remote, piece, piece, g_s.at[3 * c + i], g_r.at[3 * c + i], pb=to))
        if c == 2 and z.half > 1:
            serve_ring(2)
        if c > 0:
            g_pass_on(c - 1)

    def slot(d):
        return place[(z.ka - d) % z.ka]

    def slater_blocks():
        for d in range(z.ka):
            for e in (0, 1):
                i = 2 * d + e
                to_z, to_y = (ka + d) % z.ka, y_of(e)
                src = sps.at[2 * to_z + to_y % 2]
                dst = ts.at[slot(d), par]
                if d == 0 and e == 0:
                    own_ts = pltpu.make_async_copy(src, dst, lsem.at[10])
                    own_ts.start()
                else:
                    start(functools.partial(remote, src, dst, t_s.at[i], t_r.at[i], pb=to_y, ka=to_z))
        return own_ts

    def force_bias(s):
        def one_k(n, carry):
            block = (ka + z.ka - s + (n // 2) * (2 * s)) % z.ka
            k = 2 * block + n % 2
            other = pair_ref[pb, k]
            both = jnp.concatenate([gall[y, other // 2].astype(F32) for y in range(z.pb)], axis=0)
            odd = (other % 2).astype(F32)
            one = both[:, :blk] * (1.0 - odd) + both[:, blk:] * odd
            acc[...] += dot(one.astype(BF), rcf[k])
            return carry

        if s > 0:
            from_sibling(s)
        lax.fori_loop(0, 4 if 0 < s < z.half else 2, one_k, 0)

    g_pass_on(z.chunks - 1)
    chol_across()
    next_ring = 2 + (z.half > 1 and z.chunks > 2)
    if next_ring <= z.half:
        serve_ring(next_ring)
    serve_x(1)
    acc[...] = jnp.zeros_like(acc)
    for c in range(z.chunks):
        for i, src in ((1, right) if c % 2 == 0 else (0, left), (2, across)):
            piece = g_piece(src, c)
            remote(piece, piece, g_s.at[3 * c + i], g_r.at[3 * c + i], pb=right).wait_recv()
    for copy in local[5:8]:
        copy.wait()
    if z.half > 1:
        serve_x(2)
    force_bias(0)
    force_bias(1)
    for s in range(next_ring + 1, z.half + 1):
        serve_ring(s)
    own_ts = slater_blocks()
    for s in range(3, z.half):
        serve_x(s)
    if z.half > 2:
        force_bias(2)
        serve_x(z.half)
    chol_share(0)
    chol_share(1)
    for s in range(3, z.half):
        force_bias(s)
    chol_relay()
    if z.half > 1:
        force_bias(z.half)
    for y in range(z.pb):
        bias = acc[pl.ds(y * wb, wb), :]
        fbuf[y] = (auxb[y].astype(F32) - force_coef * bias).astype(BF)

    for d in range(1, z.pb):
        to = (pb + d) % z.pb
        start(functools.partial(
            remote, fbuf.at[pl.ds(to - to % 2, 2)], fqs.at[pb, 0], fy_s.at[d], fy_r.at[d], pb=to
        ))
    own_f = pltpu.make_async_copy(fbuf.at[pl.ds(base, 2)], fqs.at[pb, 0], lsem.at[11])
    own_f.start()
    rest_f = pltpu.make_async_copy(fbuf.at[pl.ds(2 - base, 2)], fqs.at[4, 0], lsem.at[12])
    rest_f.start()
    own_f.wait()
    rest_f.wait()
    for d in range(1, z.pb):
        here = fqs.at[(pb + z.pb - d) % z.pb, 0]
        remote(here, here, fy_s.at[d], fy_r.at[d], pb=right).wait_recv()

    def arrive_slot(e):
        return place[(z.ka - e[0]) % z.ka if e[1] == 0 else e[0]]

    def fq_copy(e, arriving):
        i = ring.index(e)
        here = fqs.at[:, arrive_slot(e)]
        if arriving:
            src = here
        elif e[0] == 1:
            src = fqs.at[:, 0]
        elif e[0] == z.half:
            one, other = place[z.ka - z.half + 1], place[z.half - 1]
            src = fqs.at[:, one + core * (other - one)]
        else:
            src = fqs.at[:, arrive_slot((e[0] - 1, e[1]))]
        return remote(src, here, fz_s.at[i], fz_r.at[i], ka=ring.target(e))

    def serve_fields(s):
        for e in ring.of_step(s):
            fq_copy(e, True).wait_recv()
        if s < z.half:
            for e in ring.of_step(s + 1):
                start(functools.partial(fq_copy, e, False))

    for e in ring.of_step(1):
        start(functools.partial(fq_copy, e, False))

    tiles, lanes = term.shape[1], vs.shape[2]
    for d in range(z.ka):
        for e in (0, 1):
            if d == 0 and e == 0:
                continue
            i = 2 * d + e
            here = ts.at[slot(d), y_of(e) % 2]
            remote(here, here, t_s.at[i], t_r.at[i], pb=y_of(e), ka=(ka + d) % z.ka).wait_recv()
    own_ts.wait()
    for p in range(z.ka):
        for h in range(2):
            stage[pl.ds((2 * p + h) * wb, wb), :] = ts[p, h].astype(F32)
    for t in range(tiles):
        first = stage[pl.ds(t * lanes, lanes), :].T.reshape(nocc, norb, lanes)
        term[0, t] = first
        total[t] = first
    chol_share(2)
    chol_pass_on(0)
    chol_pass_on(1)

    def all_of_chol():
        chol_pass_on(2)
        for i, q in enumerate(sources):
            for u, s_sem, r_sem in ((sib_quarter, cb_s, cb_r), ((sib_quarter + 2) % 4, cs_s, cs_r)):
                part = chol_rows(q, u)
                remote(part, part, s_sem.at[i], r_sem.at[i], wa=sibling).wait_recv()
        for copy in local[8:]:
            copy.wait()

    steps = max(1, norb // 8)
    ps = norb // steps
    width = ps * norb

    def potential(t):
        fields_of = [fmat[q, pl.ds(t * lanes, lanes), :].astype(BF) for q in range(4)]

        def some_rows(b, carry):
            cols = pl.ds(pl.multiple_of(b * width, width), width)
            v = dot(fields_of[0], chols[pl.ds(0, nchol), cols])
            for q in range(1, 4):
                v = v + dot(fields_of[q], chols[pl.ds(q * nchol, nchol), cols])
            vt[...] = v.T
            for p2 in range(norb):
                vs[p2, pl.ds(pl.multiple_of(b * ps, ps), ps), :] = vt[pl.ds(p2, ps, stride=norb), :]
            return carry

        lax.fori_loop(0, steps, some_rows, 0)

    step_size = tau_coef / math.sqrt(norb)
    group = 3

    def propagate(t, between):
        def one_degree(m, carry):
            scale = -step_size / m.astype(F32)
            now, later = (m + 1) % 2, m % 2

            def one_group(g, carry):
                accs = [jnp.zeros((norb, lanes), F32) for _ in range(group)]
                for p2 in range(norb):
                    column = vs[p2]
                    for a in range(group):
                        accs[a] = accs[a] + column * term[now, t, g * group + a, pl.ds(p2, 1), :]
                for a in range(group):
                    new = accs[a] * scale
                    term[later, t, g * group + a] = new
                    total[t, g * group + a] += new
                return carry

            lax.fori_loop(0, nocc // group, one_group, 0)
            return carry

        if between is None:
            lax.fori_loop(1, 7, one_degree, 0)
        else:
            lax.fori_loop(1, 5, one_degree, 0)
            between()
            lax.fori_loop(5, 7, one_degree, 0)
        final = total[t].reshape(blk, lanes).T.astype(BF)
        stage[pl.ds(t * lanes, lanes), :] = dot(final, back[...])

    k_own = 2 * ka + par
    own_m = None
    out_f = []

    def write_fields():
        for p in range(z.ka):
            block = (ka + order[p]) % z.ka
            for n, (q, first) in enumerate(((pb, base), (4, 2 - base))):
                out_f.append(
                    pltpu.make_async_copy(fqs.at[q, p], fields_ref.at[pl.ds(first, 2), block], o_s.at[2 * p + n])
                )
                out_f[-1].start()

    served, arrived, finished = 0, 0, 0

    def serve_to(s):
        nonlocal served
        while served < min(s, z.half):
            served += 1
            serve_fields(served)

    for t in range(tiles):
        last_place = -(-(t + 1) * lanes // (2 * wb)) - 1
        need = min(z.half, (last_place + 1) // 2)
        serve_to(need)
        while arrived <= last_place:
            for q in range(4):
                for h in range(2):
                    fmat[q, pl.ds((2 * arrived + h) * wb, wb), :] = fqs[q, arrived, h].astype(F32)
            arrived += 1
        if t == 0:
            all_of_chol()
        potential(t)
        if served < z.half:
            propagate(t, functools.partial(serve_to, served + 1))
        else:
            if t == tiles - 1:
                write_fields()
            propagate(t, None)
        while finished < 2 * z.ka and (finished + 1) * wb <= (t + 1) * lanes:
            p, h = finished // 2, finished % 2
            moved[p, h] = stage[pl.ds(finished * wb, wb), :].astype(BF)
            finished += 1
            if h == 0:
                continue
            r = order[p]
            to_z = (ka + r) % z.ka
            for e in (0, 1):
                to_y = y_of(e)
                src = moved.at[p, to_y % 2]
                i = 2 * r + e
                if r == 0 and e == 0:
                    own_m = pltpu.make_async_copy(src, land.at[k_own], lsem.at[13])
                    own_m.start()
                else:
                    start(functools.partial(remote, src, land.at[k_own], m_s.at[i], m_r.at[i], pb=to_y, ka=to_z))
    for r in range(z.ka):
        for e in (0, 1):
            if r == 0 and e == 0:
                continue
            i = 2 * r + e
            from_z = (ka + z.ka - r) % z.ka
            here = land.at[2 * from_z + y_of(e) % 2]
            remote(here, here, m_s.at[i], m_r.at[i], pb=y_of(e), ka=(ka + r) % z.ka).wait_recv()
    own_m.wait()
    for copy in a_copies:
        copy.wait_send()
    for make in sent:
        make().wait_send()
    for copy in out_f:
        copy.wait()


def outputs_kernel(z, blocks_hbm, fields_hbm, out_hbm, fields_out_hbm, blocks, fields, out, sems):
    in_b = pltpu.make_async_copy(blocks_hbm, blocks, sems.at[0])
    in_f = pltpu.make_async_copy(fields_hbm, fields, sems.at[1])
    out_b = pltpu.make_async_copy(out, out_hbm, sems.at[2])
    out_f = pltpu.make_async_copy(fields, fields_out_hbm, sems.at[3])
    in_b.start()
    in_f.start()
    in_b.wait()
    for k in range(z.nk):
        out[:, k * z.blk : (k + 1) * z.blk] = blocks[k]
    out_b.start()
    in_f.wait()
    out_f.start()
    out_b.wait()
    out_f.wait()


def constants(z):
    perm = np.zeros((z.blk, z.blk), np.float32)
    for r in range(z.norb):
        for j in range(z.nocc):
            perm[r * z.nocc + j, j * z.norb + r] = 1
    expand = np.zeros((z.nocc, z.sq, z.blk), np.float32)
    tiled = np.zeros((z.norb, z.blk), np.float32)
    for i in range(z.nocc):
        for r in range(z.norb):
            tiled[r, i * z.norb + r] = 1
            for j in range(z.nocc):
                expand[j, i * z.nocc + j, i * z.norb + r] = 1
    return jnp.asarray(perm, BF), jnp.asarray(perm.T, BF), jnp.asarray(expand, BF), jnp.asarray(tiled, BF)


def body(z, slater, inverse, send_rows, take_rows, pair_table, rotated_chol, chol_vectors, aux_noise):
    wb, nk, blk, nchol, ka = z.wb, z.nk, z.blk, z.nchol, z.ka
    perm, back, expand, tiled = constants(z)
    smem = pl.BlockSpec(memory_space=pltpu.SMEM)
    hbm = pl.BlockSpec(memory_space=pl.ANY)
    dma = lambda n: pltpu.SemaphoreType.DMA((n,))
    events = ka - 1
    kcols = z.norb * z.norb
    walkers = 2 * ka * wb
    lanes = min(128, walkers)
    tiles = walkers // lanes
    width = z.norb // max(1, z.norb // 8) * z.norb
    blocks, fields = pl.pallas_call(
        functools.partial(step_kernel, z),
        out_shape=(
            jax.ShapeDtypeStruct((nk, wb, blk), BF),
            jax.ShapeDtypeStruct((4, ka, wb, nchol), BF),
        ),
        in_specs=[smem] * 3 + [hbm] * 9,
        out_specs=(hbm, hbm),
        scratch_shapes=[
            pltpu.VMEM((wb, nk * blk), BF),
            pltpu.VMEM((wb, nk * z.sq), BF),
            pltpu.VMEM((blk, blk), BF),
            pltpu.VMEM((blk, blk), BF),
            pltpu.VMEM((z.nocc, z.sq, blk), BF),
            pltpu.VMEM((z.norb, blk), BF),
            pltpu.VMEM((z.wa, ROWS, z.width), BF),
            pltpu.VMEM((z.wa, ROWS, z.width), BF),
            pltpu.VMEM((nk * wb, blk), F32),
            pltpu.VMEM((nk * wb, z.sq), F32),
            pltpu.VMEM((nk, wb, blk), BF),
            pltpu.VMEM((4, nk // 2, wb, 2 * blk), BF),
            pltpu.VMEM((nk, blk, nchol), BF),
            pltpu.VMEM((4 * wb, nchol), F32),
            pltpu.VMEM((4, wb, nchol), BF),
            pltpu.VMEM((4, wb, nchol), BF),
            pltpu.VMEM((5, ka, 2, wb, nchol), BF),
            pltpu.VMEM((4, walkers, nchol), F32),
            pltpu.VMEM((4 * nchol, kcols), BF),
            pltpu.VMEM((2, nchol // 8, kcols), BF),
            pltpu.VMEM((ka, 2, wb, blk), BF),
            pltpu.VMEM((walkers, blk), F32),
            pltpu.VMEM((ka, 2, wb, blk), BF),
            pltpu.VMEM((width, lanes), F32),
            pltpu.VMEM((z.norb, z.norb, lanes), F32),
            pltpu.VMEM((2, tiles, z.nocc, z.norb, lanes), F32),
            pltpu.VMEM((tiles, z.nocc, z.norb, lanes), F32),
            dma(16), dma(z.wa), dma(z.wa), dma(2 * ka), dma(2 * ka), dma(3 * z.chunks), dma(3 * z.chunks),
            dma(2 * events), dma(2 * events), dma(2 * events), dma(2 * events),
            dma(2 * events), dma(2 * events), dma(2 * events), dma(2 * events),
            dma(2), dma(2), dma(2), dma(2), dma(2), dma(2), dma(3), dma(3), dma(3), dma(3), dma(3), dma(3),
            dma(4), dma(4), dma(events), dma(events), dma(2 * ka), dma(2 * ka), dma(2 * ka),
        ],
        compiler_params=pltpu.CompilerParams(
            collective_id=0, has_side_effects=True, vmem_limit_bytes=56 * 1024 * 1024
        ),
        cost_estimate=pl.CostEstimate(flops=6 * 10**9, bytes_accessed=30 * 10**6, transcendentals=0),
    )(
        send_rows.T, take_rows, pair_table, slater, inverse, perm, back, expand, tiled,
        rotated_chol, chol_vectors, aux_noise.reshape(4, ka, wb, nchol),
    )
    moved, fields = pl.pallas_call(
        functools.partial(outputs_kernel, z),
        out_shape=(
            jax.ShapeDtypeStruct((wb, nk * blk), BF),
            jax.ShapeDtypeStruct((4, ka, wb, nchol), BF),
        ),
        in_specs=[hbm] * 2,
        out_specs=(hbm, hbm),
        scratch_shapes=[
            pltpu.VMEM((nk, wb, blk), BF),
            pltpu.VMEM((4, ka, wb, nchol), BF),
            pltpu.VMEM((wb, nk * blk), BF),
            dma(4),
        ],
        compiler_params=pltpu.CompilerParams(vmem_limit_bytes=56 * 1024 * 1024),
    )(blocks, fields)
    return moved, fields.reshape(4 * ka * wb, nchol)


def solution(mesh, z=Sizes(8, 8, 16, 48, 12, 512, 24)):
    placed = (
        P(("wa", "pb", "ka"), None),
        P(("wa", "pb", "ka"), None),
        P(("wa", "pb", "ka"), None),
        P(("wa", "pb", "ka")),
        P(),
        P("pb", "ka", None),
        P("pb", None, "ka"),
        P("wa", "pb"),
    )
    return jax.shard_map(
        functools.partial(body, z),
        mesh=mesh,
        in_specs=placed,
        out_specs=(P(("wa", "pb", "ka"), None), P("wa", "pb")),
        check_vma=False,
    )
```
